32 devices in a mesh: rep: 2 (over y), seq: 4 (over z), mp: 2 (over x), sub: 2 (over core).
Axes of the slice: x: 2, y: 2, z: 4, core: 2. Of those that a mesh axis runs over, the one named last changes fastest.
Arguments:
- normed_inputs: bfloat16 [4096, 5120], P(('rep', 'seq', 'sub'), 'mp'), parts along dimension 0, may hold values from -6 to 6
- base_queries: bfloat16 [4096, 8192], P(('rep', 'seq', 'sub'), 'mp'), parts along dimension 0, may hold values from -8 to 8
- base_keys: bfloat16 [4096, 1024], P(('rep', 'seq', 'sub'), 'mp'), parts along dimension 0, may hold values from -8 to 8
- base_values: bfloat16 [4096, 1024], P(('rep', 'seq', 'sub'), 'mp'), parts along dimension 0, may hold values from -6 to 6
- adapter_down: bfloat16 [8, 5120, 16], P(None, 'mp'), may hold values from -0.078125 to 0.078125
- adapter_up: bfloat16 [8, 16, 8192], P(None, None, 'mp'), may hold values from -0.75 to 0.75
- position_document: int32 [4096], P(('rep', 'seq', 'sub')), parts along dimension 0, may hold values from 0 to 15, never falling along the last dimension, each value on 1 to 768 neighbouring positions
- document_tenant: int32 [32], P('rep'), parts along dimension 0, may hold values from 0 to 7, as said below
- output_gradient: bfloat16 [4096, 8192], P(('rep', 'seq', 'sub'), 'mp'), parts along dimension 0, may hold values from -6 to 6
Outputs:
- attn_out: bfloat16 [4096, 8192], P(('rep', 'seq', 'sub'), 'mp'), parts along dimension 0
- grad_a: float32 [16, 5120, 16], P('rep', 'mp'), parts along dimension 0
- grad_b: float32 [16, 16, 8192], P('rep', None, 'mp'), parts along dimension 0
The draws below stay inside these ranges and needn't reach their ends.
There are 2 independent parts, one for each index of `rep`. The reference program is written for one: setup_inputs(seed, part) draws one part's arguments, and reference() takes and returns one part's arrays. A program takes and returns all parts, laid end to end along the dimension named above; an argument that names none is the same for every part. Nothing has to cross between parts.
Inputs may be any that keep to these rules, and one draw needn't show every extreme that they name: `position_document`: Non-decreasing along the row; each document spans 1 to 768 positions, and one spans exactly that many. `document_tenant`: every tenant owns exactly 2 documents.
All inputs are finite; a program needn't handle non-finite values.
Results may differ from the reference program's by a relative error of at most 0.035.
Values may be sent and summed in bfloat16 or wider, within the bound.
No kernel may reach another device: no remote copies, remote signals or barrier semaphores. Data moves between devices by JAX's collectives and lax.ppermute only.
A program may use at most 192 MiB of HBM per device.

```python
import math
import jax
import jax.numpy as jnp
import numpy as np
from jax import lax

MODEL_WIDTH = 5120
QUERY_HEADS = 64
KEY_VALUE_HEADS = 8
HEAD_SIZE = 128
ADAPTER_RANK = 16
TENANT_COUNT = 8
REACH = 3
DEVICE_POSITIONS = 256
PACKED_LENGTH = 2048
SEGS = 16


def draw_base_queries(key, part):
    key = jax.random.fold_in(key, 1)
    value_rows = jnp.clip(jax.random.normal(key, (PACKED_LENGTH, QUERY_HEADS * HEAD_SIZE), jnp.float32), -8.0, 8.0)
    return value_rows.astype(jnp.bfloat16)


def draw_base_keys(key, part):
    key = jax.random.fold_in(key, 2)
    value_rows = jnp.clip(jax.random.normal(key, (PACKED_LENGTH, KEY_VALUE_HEADS * HEAD_SIZE), jnp.float32), -8.0, 8.0)
    return value_rows.astype(jnp.bfloat16)


def draw_document_tenant(key, part):
    key = jax.random.fold_in(key, 3)
    return (jax.random.permutation(key, SEGS) % TENANT_COUNT).astype(jnp.int32)


def steps_of(key, extent, pieces, smallest, largest):
    factor_of, own = 1.0, jax.random.fold_in(key, 6)
    for position, parts in pieces:
        steps = jnp.exp(jax.random.uniform(jax.random.fold_in(own, position), (parts,), jnp.float32, smallest / len(pieces), largest / len(pieces)))
        factor_of = factor_of * jnp.repeat(steps, extent[position] // parts).reshape([-1 if axis == position else 1 for axis in range(len(extent))])
    return factor_of


def length_profile(count, total, reach, slope):
    portions = [(1 << 20) // math.isqrt(rank ** slope) + 1 for rank in range(2, count + 1)]
    surplus, counts = total - reach - (count - 1), [1] * (count - 1)
    while surplus > 0:
        movable = [i for i in range(count - 1) if counts[i] < reach]
        mass, budget = sum([portions[i] for i in movable]), surplus
        for i in movable:
            addition = min(reach - counts[i], max(1, budget * portions[i] // mass), surplus)
            counts[i] = counts[i] + addition
            surplus = surplus - addition
    return np.array([reach] + counts)


def uneven_parts(own_key, number_of, total, most, lean):
    if number_of == 2:
        one = jax.random.randint(own_key, (), max(1, total - most), min(most, total - 1) + 1)
        return jnp.stack([one, total - one])
    lengths = jnp.asarray(length_profile(number_of, total, most, lean), jnp.int32)
    couples = (number_of - 1) // 2
    donor, receiver = lengths[1:1 + 2 * couples:2], lengths[2:2 + 2 * couples:2]
    room = jnp.minimum(donor - 1, most - receiver)
    passed = jax.random.randint(jax.random.fold_in(own_key, 1), (couples,), 0, 1 << 20) % (room + 1)
    lengths = lengths.at[1:1 + 2 * couples:2].set(donor - passed).at[2:2 + 2 * couples:2].set(receiver + passed)
    return lengths[jax.random.permutation(jax.random.fold_in(own_key, 2), number_of)]


def gaussian(stream_key, dims, width, limit, shards=(), kind=jnp.bfloat16):
    loudness = steps_of(stream_key, dims, shards, -0.22, 0.18) if shards else 1.0
    entries = jax.random.normal(stream_key, dims, jnp.float32) * width * loudness
    return jnp.minimum(jnp.maximum(entries, -limit), limit).astype(kind)


def setup_inputs(seed: int = 0, part: int = 0) -> dict:
    key_list = jax.random.split(jax.random.key(seed), 10)
    part_splits = jax.random.split(jax.random.fold_in(key_list[9], part), 10)
    return {
        "normed_inputs": gaussian(part_splits[0], (PACKED_LENGTH, MODEL_WIDTH), 1.0, 6.0, ((0, 8), (1, 2))),
        "base_queries": draw_base_queries(jax.random.fold_in(jax.random.fold_in(key_list[9], part), 71), part),
        "base_keys": draw_base_keys(jax.random.fold_in(jax.random.fold_in(key_list[9], part), 71), part),
        "base_values": gaussian(part_splits[3], (PACKED_LENGTH, KEY_VALUE_HEADS * HEAD_SIZE), 1.0, 6.0, ((0, 8), (1, 2))),
        "adapter_down": gaussian(key_list[4], (TENANT_COUNT, MODEL_WIDTH, ADAPTER_RANK), MODEL_WIDTH ** -0.5, 0.078125, ((1, 2),)),
        "adapter_up": gaussian(key_list[5], (TENANT_COUNT, ADAPTER_RANK, QUERY_HEADS * HEAD_SIZE), (4 * ADAPTER_RANK) ** -0.5, 0.75, ((2, 2),)),
        "position_document": jnp.searchsorted(jnp.cumsum(uneven_parts(part_splits[6], SEGS, PACKED_LENGTH, REACH * DEVICE_POSITIONS, 0)), jnp.arange(PACKED_LENGTH), side="right").astype(jnp.int32),
        "document_tenant": draw_document_tenant(jax.random.fold_in(jax.random.fold_in(key_list[9], part), 71), part),
        "output_gradient": gaussian(part_splits[8], (PACKED_LENGTH, QUERY_HEADS * HEAD_SIZE), 1.0, 6.0, ((0, 8), (1, 2))),
    }


NEG = -1.0e30
SCALE = 2.0


def reference(normed_inputs, base_queries, base_keys, base_values, adapter_down, adapter_up, position_document, document_tenant, output_gradient):
    highest = lax.Precision.HIGHEST
    owner = document_tenant[position_document]
    columns = jnp.arange(TENANT_COUNT * ADAPTER_RANK, dtype=jnp.int32) // ADAPTER_RANK
    selector = owner[:, None] == columns[None, :]
    flattened_down = jnp.transpose(adapter_down, (1, 0, 2)).reshape(MODEL_WIDTH, TENANT_COUNT * ADAPTER_RANK)
    flattened_up = adapter_up.reshape(TENANT_COUNT * ADAPTER_RANK, QUERY_HEADS * HEAD_SIZE)
    down = jnp.dot(normed_inputs, flattened_down, preferred_element_type=jnp.float32)
    bottle = jnp.where(selector, down, 0.0).astype(jnp.bfloat16)
    lifted = jnp.dot(bottle, flattened_up, preferred_element_type=jnp.float32)
    query_rows = (base_queries.astype(jnp.float32) + SCALE * lifted).astype(jnp.bfloat16)
    query_groups = QUERY_HEADS // KEY_VALUE_HEADS
    inv = HEAD_SIZE ** -0.5
    margin = REACH * DEVICE_POSITIONS
    window_length = (REACH + 1) * DEVICE_POSITIONS
    padded_keys = jnp.pad(base_keys, ((margin, 0), (0, 0)))
    padded_values = jnp.pad(base_values, ((margin, 0), (0, 0)))
    seg_pad = jnp.pad(position_document, (margin, 0), constant_values=-1)

    def one_block(index):
        start_index = (index * DEVICE_POSITIONS).astype(jnp.int32)
        query_block = lax.dynamic_slice_in_dim(query_rows, start_index, DEVICE_POSITIONS, 0).reshape(DEVICE_POSITIONS, KEY_VALUE_HEADS, query_groups, HEAD_SIZE).astype(jnp.float32)
        gradient_block = lax.dynamic_slice_in_dim(output_gradient, start_index, DEVICE_POSITIONS, 0).reshape(DEVICE_POSITIONS, KEY_VALUE_HEADS, query_groups, HEAD_SIZE).astype(jnp.float32)
        key_block = lax.dynamic_slice_in_dim(padded_keys, start_index, window_length, 0).reshape(window_length, KEY_VALUE_HEADS, HEAD_SIZE).astype(jnp.float32)
        value_block = lax.dynamic_slice_in_dim(padded_values, start_index, window_length, 0).reshape(window_length, KEY_VALUE_HEADS, HEAD_SIZE).astype(jnp.float32)
        kseg = lax.dynamic_slice_in_dim(seg_pad, start_index, window_length, 0)
        qseg = lax.dynamic_slice_in_dim(position_document, start_index, DEVICE_POSITIONS, 0)
        qpos = start_index + jnp.arange(DEVICE_POSITIONS, dtype=jnp.int32)
        kpos = start_index - margin + jnp.arange(window_length, dtype=jnp.int32)
        allowed = (kpos[None, :] <= qpos[:, None]) & (kseg[None, :] == qseg[:, None])
        scores = jnp.einsum("ihgd,jhd->hgij", query_block, key_block, precision=highest) * inv
        peak = jnp.max(jnp.where(allowed, scores, NEG), axis=-1)
        weights = jnp.where(allowed, jnp.exp(scores - peak[..., None]), 0.0)
        total = jnp.sum(weights, axis=-1)
        rounded = lax.optimization_barrier(weights.astype(jnp.bfloat16)).astype(jnp.float32)
        accum = jnp.einsum("hgij,jhd->hgid", rounded, value_block, precision=highest)
        out4 = jnp.transpose(accum / total[..., None], (2, 0, 1, 3)).astype(jnp.bfloat16)
        logsum = peak + jnp.log(total)
        rowdot = jnp.einsum("ihgd,ihgd->hgi", gradient_block, out4.astype(jnp.float32), precision=highest)
        prob = jnp.where(allowed, jnp.exp(scores - logsum[..., None]), 0.0)
        dprob = jnp.einsum("ihgd,jhd->hgij", gradient_block, value_block, precision=highest)
        dscore = lax.optimization_barrier((prob * (dprob - rowdot[..., None])).astype(jnp.bfloat16)).astype(jnp.float32)
        dquery = jnp.einsum("hgij,jhd->ihgd", dscore, key_block, precision=highest) * inv
        gquery = (SCALE * dquery).reshape(DEVICE_POSITIONS, QUERY_HEADS * HEAD_SIZE).astype(jnp.bfloat16)
        return out4.reshape(DEVICE_POSITIONS, QUERY_HEADS * HEAD_SIZE), gquery

    outs, grads = lax.map(one_block, jnp.arange(PACKED_LENGTH // DEVICE_POSITIONS, dtype=jnp.int32))
    attn_out = outs.reshape(PACKED_LENGTH, QUERY_HEADS * HEAD_SIZE)
    gquery = grads.reshape(PACKED_LENGTH, QUERY_HEADS * HEAD_SIZE)
    gdown = jnp.dot(gquery, flattened_up.T, preferred_element_type=jnp.float32)
    gbottle = jnp.where(selector, gdown, 0.0).astype(jnp.bfloat16)
    grad_a = jnp.dot(normed_inputs.T, gbottle, preferred_element_type=jnp.float32)
    grad_a = jnp.transpose(grad_a.reshape(MODEL_WIDTH, TENANT_COUNT, ADAPTER_RANK), (1, 0, 2))
    grad_b = jnp.dot(bottle.T, gquery, preferred_element_type=jnp.float32).reshape(TENANT_COUNT, ADAPTER_RANK, QUERY_HEADS * HEAD_SIZE)
    return (attn_out, grad_a, grad_b)
```

```python
import functools

import jax
import jax.numpy as jnp
from jax import lax
from jax.experimental import pallas as pl
from jax.experimental.pallas import tpu as pltpu
from jax.sharding import PartitionSpec as P

HEAD = 128
REACH = 3
NEG = -1e30
LIFT = 2.0
LOG2E = 1.4426950408889634
TAIL = 16
VMEM_BYTES = 48 * 1024 * 1024

VM = pl.BlockSpec(memory_space=pltpu.VMEM)
SM = pl.BlockSpec(memory_space=pltpu.SMEM)
ANY = pl.BlockSpec(memory_space=pl.ANY)


def nt(a, b):
    return lax.dot_general(a, b, (((1,), (1,)), ((), ())), preferred_element_type=jnp.float32)


def nn(a, b):
    return jnp.dot(a, b, preferred_element_type=jnp.float32)


def params():
    return pltpu.CompilerParams(vmem_limit_bytes=VMEM_BYTES)


def pack_kernel(keys, values, doc, *outs):
    rows = keys.shape[0]
    half = outs[0].shape[1] // 2
    ids = jnp.broadcast_to((doc[...] + 1).astype(jnp.float32), (TAIL, rows)).astype(jnp.bfloat16)
    for c, out in enumerate(outs):
        out[0:rows, 0:half] = keys[:, c * half : (c + 1) * half]
        out[0:rows, half:] = values[:, c * half : (c + 1) * half]
        out[rows:, :] = jnp.zeros((TAIL, 2 * half), jnp.bfloat16)
        out[rows:, 0:rows] = ids


def pack(keys, values, doc, chunks):
    rows, width = keys.shape
    shape = jax.ShapeDtypeStruct((rows + TAIL, 2 * width // chunks), jnp.bfloat16)
    return pl.pallas_call(
        pack_kernel,
        out_shape=[shape] * chunks,
        in_specs=[VM] * 3,
        out_specs=[VM] * chunks,
        compiler_params=params(),
        cost_estimate=pl.CostEstimate(flops=0, bytes_accessed=8 * rows * width, transcendentals=0),
        name="pack_keys_values",
    )(keys, values, doc)


def relay_kernel(own, got, out, sem):
    sub = lax.axis_index("sub")

    @pl.when(sub == 0)
    def _():
        copy = pltpu.make_async_copy(own, out, sem)
        copy.start()
        copy.wait()

    @pl.when(sub != 0)
    def _():
        copy = pltpu.make_async_copy(got, out, sem)
        copy.start()
        copy.wait()


def relay(own, got):
    return pl.pallas_call(
        relay_kernel,
        out_shape=jax.ShapeDtypeStruct(own.shape, own.dtype),
        in_specs=[ANY, ANY],
        out_specs=ANY,
        scratch_shapes=[pltpu.SemaphoreType.DMA(())],
        compiler_params=params(),
        cost_estimate=pl.CostEstimate(flops=0, bytes_accessed=4 * own.size, transcendentals=0),
        name="relay_block",
    )(own, got)


def selector_of(owner, tenants, rank):
    rows = owner.shape[1]
    tenant = lax.broadcasted_iota(jnp.int32, (tenants * rank, rows), 0) // rank
    return tenant == owner


def fold(full, owner, tenants, rank):
    kept = jnp.where(selector_of(owner, tenants, rank), full, 0.0)
    total = kept[0:rank]
    for t in range(1, tenants):
        total = total + kept[t * rank : (t + 1) * rank]
    return total


def unfold(compact, owner, tenants, rank):
    spread = jnp.concatenate([compact] * tenants, axis=0)
    return jnp.where(selector_of(owner, tenants, rank), spread, 0.0)


def down_kernel(tenants, rank, x, adapter, doc, tenant_of, compact, owner):
    ids = doc[...]
    found = jnp.zeros(ids.shape, jnp.int32)
    for s in range(tenant_of.shape[0]):
        found = jnp.where(ids == s, tenant_of[s], found)
    owner[...] = found
    compact[...] = fold(nt(x[...], adapter[...]).T, found, tenants, rank)


def down_project(x, adapter, doc, tenant_of, tenants, rank):
    rows, width = x.shape
    return pl.pallas_call(
        functools.partial(down_kernel, tenants, rank),
        out_shape=[
            jax.ShapeDtypeStruct((rank, rows), jnp.float32),
            jax.ShapeDtypeStruct((1, rows), jnp.int32),
        ],
        in_specs=[VM, VM, VM, SM],
        out_specs=[VM, VM],
        compiler_params=params(),
        cost_estimate=pl.CostEstimate(
            flops=2 * rows * width * tenants * rank,
            bytes_accessed=2 * width * (rows + tenants * rank),
            transcendentals=0,
        ),
        name="down_project",
    )(x, adapter, doc, tenant_of)


def attention_kernel(
    tenants, rank, group, first,
    base, grad, up, own_k, own_v, two_k, two_v, swap_k, swap_v, pass_k, pass_v,
    own_c, other_c, owner, own_tail, two_tail, swap_tail, pass_tail, *rest,
):
    if first:
        out, part_b, gdown, *scratch = rest
        gdown_before = None
    else:
        gdown_before, _, out, part_b, gdown, *scratch = rest
    bottle, bottle_t, bias, query, gquery, kt, kw, vt, vw, s_ref, gsum, blocks = scratch
    rows = base.shape[0]
    sub = lax.axis_index("sub")
    step = pl.program_id(0)
    last = pl.num_programs(0) - 1
    scale = HEAD**-0.5

    @pl.when(step == 0)
    def _():
        lifted = unfold(own_c[...] + other_c[...], owner[...], tenants, rank)
        bottle_t[...] = lifted.astype(jnp.bfloat16)
        bottle[...] = lifted.T.astype(jnp.bfloat16)
        gsum[...] = jnp.zeros_like(gsum)
        mine = own_tail[0:1, 0:rows].astype(jnp.float32)
        column = jnp.broadcast_to(mine, (rows, rows)).T
        swapped = swap_tail[0:1, 0:rows].astype(jnp.float32)
        passed = pass_tail[0:1, 0:rows].astype(jnp.float32)
        near = jnp.where(sub == 0, swapped, passed)
        far = jnp.where(sub == 0, passed, swapped)
        two = two_tail[0:1, 0:rows].astype(jnp.float32)
        for d, ids in ((3, far), (2, two), (1, near)):
            at = (REACH - d) * rows
            bias[:, at : at + rows] = jnp.where(column == ids, 0.0, NEG)
        causal = lax.broadcasted_iota(jnp.int32, (rows, rows), 0) >= lax.broadcasted_iota(
            jnp.int32, (rows, rows), 1
        )
        bias[:, REACH * rows :] = jnp.where(causal & (column == mine), 0.0, NEG)
        head = jnp.min(mine)
        reach = jnp.where(jnp.max(near) == head, 1, 0)
        reach = jnp.where(jnp.max(two) == head, 2, reach)
        blocks[0] = jnp.where(jnp.max(far) == head, 3, reach)

    ones = jnp.ones((rows, HEAD), jnp.bfloat16)

    def place(slot, k_block, v_block):
        at = pl.ds(slot * rows, rows)
        k = k_block[0:rows, :]
        v = v_block[0:rows, :]
        kw[at, :] = k
        vw[at, 0:HEAD] = v
        vw[at, HEAD:] = ones
        kt[:, at] = k.T
        vt[:, at] = v.T

    place(REACH, own_k, own_v)
    place(REACH - 2, two_k, two_v)

    @pl.when(sub == 0)
    def _():
        place(REACH - 1, swap_k, swap_v)
        place(REACH - 3, pass_k, pass_v)

    @pl.when(sub != 0)
    def _():
        place(REACH - 1, pass_k, pass_v)
        place(REACH - 3, swap_k, swap_v)

    query[...] = (base[...].astype(jnp.float32) + LIFT * nn(bottle[...], up[...])).astype(
        jnp.bfloat16
    )

    def run(count, heads):
        chunks = range(REACH - count, REACH + 1)
        cols = [pl.ds(h * HEAD, HEAD) for h in heads]
        slots = range(len(heads))

        def keys(c):
            return slice(c * rows, (c + 1) * rows)

        def lanes_max(s):
            m = s[:, 0:HEAD]
            for at in range(HEAD, rows, HEAD):
                m = jnp.maximum(m, s[:, at : at + HEAD])
            return m

        peaks = [None] * len(heads)
        for c in chunks:
            for i in slots:
                s = nn(query[:, cols[i]], kt[:, keys(c)]) + bias[:, keys(c)]
                s_ref[i, :, keys(c)] = s
                m = lanes_max(s)
                peaks[i] = m if peaks[i] is None else jnp.maximum(peaks[i], m)
        peaks = [jnp.max(m, axis=1, keepdims=True) for m in peaks]
        sums = [None] * len(heads)
        for c in chunks:
            for i in slots:
                w = jnp.exp2((s_ref[i, :, keys(c)] - peaks[i]) * (scale * LOG2E))
                s_ref[i, :, keys(c)] = w
                o = nn(w.astype(jnp.bfloat16), vw[keys(c), :])
                sums[i] = o if sums[i] is None else sums[i] + o
        inverses, rowdots = [], []
        for i in slots:
            inverse = 1.0 / sums[i][:, HEAD:]
            attn = (sums[i][:, 0:HEAD] * inverse).astype(jnp.bfloat16)
            out[:, cols[i]] = attn
            product = grad[:, cols[i]].astype(jnp.float32) * attn.astype(jnp.float32)
            rowdots.append(jnp.sum(product, axis=1, keepdims=True))
            inverses.append(inverse)
        moved = [None] * len(heads)
        for c in chunks:
            for i in slots:
                dprob = nn(grad[:, cols[i]], vt[:, keys(c)])
                ds = (s_ref[i, :, keys(c)] * (dprob - rowdots[i])).astype(jnp.bfloat16)
                dq = nn(ds, kw[keys(c), :])
                moved[i] = dq if moved[i] is None else moved[i] + dq
        for i in slots:
            gquery[:, cols[i]] = (moved[i] * (inverses[i] * (LIFT * scale))).astype(jnp.bfloat16)

    pair = s_ref.shape[0]
    for count in range(REACH + 1):

        @pl.when(blocks[0] == count)
        def _():
            @pl.loop(0, group // pair)
            def _(i):
                run(count, [i * pair + k for k in range(pair)])

    part_b[...] = nn(bottle_t[...], gquery[...]).astype(jnp.bfloat16)
    gsum[...] += nt(up[...], gquery[...])

    @pl.when(step == last)
    def _():
        total = fold(gsum[...], owner[...], tenants, rank)
        gdown[...] = total if gdown_before is None else total + gdown_before[...]


def attention(
    chunk, chunks, base, grad, up, own, two, swap, passed, own_c, other_c, owner, before, tenants, rank
):
    rows, width = base.shape
    payload_rows, payload_width = own.shape
    heads = payload_width // (2 * HEAD)
    group = width // HEAD // (heads * chunks)
    span = group * HEAD
    first = before is None
    offset = chunk * heads
    wide = lambda r: pl.BlockSpec((r, span), lambda i: (0, i + offset))
    key_block = pl.BlockSpec((payload_rows, HEAD), lambda i: (0, i))
    value_block = pl.BlockSpec((payload_rows, HEAD), lambda i: (0, i + heads))
    tail = pl.BlockSpec((TAIL, payload_width), lambda i: (rows // TAIL, 0))
    same = lambda a: pl.BlockSpec(a.shape, lambda i: (0, 0))
    operands = [base, grad, up]
    specs = [wide(rows), wide(rows), wide(up.shape[0])]
    for block in (own, two, swap, passed):
        operands += [block, block]
        specs += [key_block, value_block]
    operands += [own_c, other_c, owner, own, two, swap, passed]
    specs += [same(own_c), same(other_c), same(owner), tail, tail, tail, tail]
    aliases = {}
    if not first:
        operands += [before[2], before[0]]
        specs += [same(before[2]), ANY]
        aliases = {len(operands) - 1: 0}
    window = (REACH + 1) * rows
    pair = 2
    return pl.pallas_call(
        functools.partial(attention_kernel, tenants, rank, group, first),
        grid=(heads,),
        out_shape=[
            jax.ShapeDtypeStruct((rows, width), jnp.bfloat16),
            jax.ShapeDtypeStruct((tenants * rank, heads * span), jnp.bfloat16),
            jax.ShapeDtypeStruct((rank, rows), jnp.float32),
        ],
        in_specs=specs,
        out_specs=[
            wide(rows),
            pl.BlockSpec((tenants * rank, span), lambda i: (0, i)),
            pl.BlockSpec((rank, rows), lambda i: (0, 0)),
        ],
        scratch_shapes=[
            pltpu.VMEM((rows, tenants * rank), jnp.bfloat16),
            pltpu.VMEM((tenants * rank, rows), jnp.bfloat16),
            pltpu.VMEM((rows, window), jnp.float32),
            pltpu.VMEM((rows, span), jnp.bfloat16),
            pltpu.VMEM((rows, span), jnp.bfloat16),
            pltpu.VMEM((HEAD, window), jnp.bfloat16),
            pltpu.VMEM((window, HEAD), jnp.bfloat16),
            pltpu.VMEM((HEAD, window), jnp.bfloat16),
            pltpu.VMEM((window, 2 * HEAD), jnp.bfloat16),
            pltpu.VMEM((pair, rows, window), jnp.float32),
            pltpu.VMEM((tenants * rank, rows), jnp.float32),
            pltpu.SMEM((1,), jnp.int32),
        ],
        input_output_aliases=aliases,
        compiler_params=params(),
        cost_estimate=pl.CostEstimate(
            flops=8 * rows * window * span * heads,
            bytes_accessed=6 * rows * span * heads,
            transcendentals=rows * window * group * heads,
        ),
        name="attention",
    )(*operands)


def part_a_kernel(tenants, rank, own, other, owner, x, out):
    g = unfold(own[...] + other[...], owner[...], tenants, rank).astype(jnp.bfloat16)
    out[...] = nn(g, x[...]).astype(jnp.bfloat16)


def grad_a_part(own, other, owner, x, tenants, rank):
    rows, width = x.shape
    return pl.pallas_call(
        functools.partial(part_a_kernel, tenants, rank),
        out_shape=jax.ShapeDtypeStruct((tenants * rank, width), jnp.bfloat16),
        in_specs=[VM] * 4,
        out_specs=VM,
        compiler_params=params(),
        cost_estimate=pl.CostEstimate(
            flops=2 * rows * width * tenants * rank,
            bytes_accessed=2 * width * (rows + tenants * rank),
            transcendentals=0,
        ),
        name="grad_a_part",
    )(own, other, owner, x)


def swap_over(block, axis):
    return lax.ppermute(block, axis, [(0, 1), (1, 0)])


def terms_over(block, axis):
    if lax.axis_size(axis) == 2:
        return block, swap_over(block, axis)
    return lax.psum(block, axis), jnp.zeros_like(block)


def shift_over(block, axis):
    size = lax.axis_size(axis)
    return lax.ppermute(block, axis, [(i, i + 1) for i in range(size - 1)])


def body(
    normed_inputs, base_queries, base_keys, base_values, adapter_down, adapter_up,
    position_document, document_tenant, output_gradient,
):
    rows, width = normed_inputs.shape
    tenants, _, rank = adapter_down.shape
    up_width = adapter_up.shape[2]
    doc = position_document.reshape(1, rows)
    adapter = jnp.transpose(adapter_down, (0, 2, 1)).reshape(tenants * rank, width)
    up = adapter_up.reshape(tenants * rank, up_width)

    chunks = 2 if base_keys.shape[1] % (2 * HEAD) == 0 else 1

    own = pack(base_keys, base_values, doc, chunks)
    two = [shift_over(block, "seq") for block in own]
    compact, owner = down_project(normed_inputs, adapter, doc, document_tenant, tenants, rank)
    compact, other = terms_over(compact, "mp")
    swapped = [swap_over(block, "sub") for block in two]
    passed = [shift_over(relay(o, t), ("seq", "sub")) for o, t in zip(own, two)]

    before, parts = None, []
    for c in range(chunks):
        before = attention(
            c, chunks, base_queries, output_gradient, up, own[c], two[c], swapped[c], passed[c],
            compact, other, owner, before, tenants, rank,
        )
        parts.append(lax.psum(before[1], ("seq", "sub")))
    attn_out, _, gdown = before
    gdown, other = terms_over(gdown, "mp")
    part_a = grad_a_part(gdown, other, owner, normed_inputs, tenants, rank)
    sum_a = lax.psum(part_a, ("seq", "sub")).astype(jnp.float32)
    grad_a = jnp.transpose(sum_a.reshape(tenants, rank, width), (0, 2, 1))
    sum_b = jnp.concatenate(parts, axis=1).astype(jnp.float32)
    return attn_out, grad_a, sum_b.reshape(tenants, rank, up_width)


def solution(mesh):
    split = P(("rep", "seq", "sub"), "mp")
    in_specs = (
        split, split, split, split, P(None, "mp", None), P(None, None, "mp"),
        P(("rep", "seq", "sub")), P("rep"), split,
    )
    out_specs = (split, P("rep", "mp", None), P("rep", None, "mp"))
    return jax.shard_map(body, mesh=mesh, in_specs=in_specs, out_specs=out_specs, check_vma=False)
```

```python
import functools

import jax
import jax.numpy as jnp
from jax import lax
from jax.experimental import pallas as pl
from jax.experimental.pallas import tpu as pltpu
from jax.sharding import PartitionSpec as P

HEAD = 128
REACH = 3
NEG = -1e30
LIFT = 2.0
LOG2E = 1.4426950408889634
TAIL = 16
VMEM_BYTES = 48 * 1024 * 1024
VMEM_MOST = 60 * 1024 * 1024

VM = pl.BlockSpec(memory_space=pltpu.VMEM)
SM = pl.BlockSpec(memory_space=pltpu.SMEM)
ANY = pl.BlockSpec(memory_space=pl.ANY)


def nt(a, b):
    return lax.dot_general(a, b, (((1,), (1,)), ((), ())), preferred_element_type=jnp.float32)


def nn(a, b):
    return jnp.dot(a, b, preferred_element_type=jnp.float32)


def params(limit=VMEM_BYTES):
    return pltpu.CompilerParams(vmem_limit_bytes=limit)


def fetch(pairs, sems):
    copies = [pltpu.make_async_copy(src, dst, sems.at[i]) for i, (src, dst) in enumerate(pairs)]
    for copy in copies:
        copy.start()
    return copies


def pack_kernel(keys, values, doc, *rest):
    outs, ids, tail, sems = rest[:-3], rest[-3], rest[-2], rest[-1]
    rows = keys.shape[0]
    half = outs[0].shape[1] // 2
    pairs = [(doc, ids)]
    for c, out in enumerate(outs):
        cols = pl.ds(c * half, half)
        pairs.append((keys.at[:, cols], out.at[pl.ds(0, rows), pl.ds(0, half)]))
        pairs.append((values.at[:, cols], out.at[pl.ds(0, rows), pl.ds(half, half)]))
    copies = fetch(pairs, sems)
    copies[0].wait()
    tail[...] = jnp.zeros_like(tail)
    tail[:, 0:rows] = jnp.broadcast_to((ids[...] + 1).astype(jnp.float32), (TAIL, rows)).astype(
        jnp.bfloat16
    )
    copies += fetch(
        [(tail, out.at[pl.ds(rows, TAIL), :]) for out in outs], sems.at[pl.ds(len(pairs), len(outs))]
    )
    for copy in copies[1:]:
        copy.wait()


def pack(keys, values, doc, chunks):
    rows, width = keys.shape
    shape = jax.ShapeDtypeStruct((rows + TAIL, 2 * width // chunks), jnp.bfloat16)
    return pl.pallas_call(
        pack_kernel,
        out_shape=[shape] * chunks,
        in_specs=[ANY] * 3,
        out_specs=[ANY] * chunks,
        scratch_shapes=[
            pltpu.VMEM((1, rows), jnp.int32),
            pltpu.VMEM((TAIL, 2 * width // chunks), jnp.bfloat16),
            pltpu.SemaphoreType.DMA((1 + 3 * chunks,)),
        ],
        compiler_params=params(VMEM_MOST),
        cost_estimate=pl.CostEstimate(flops=0, bytes_accessed=8 * rows * width, transcendentals=0),
        name="pack_keys_values",
    )(keys, values, doc)


def relay_kernel(own, got, after, out, sem):
    sub = lax.axis_index("sub")

    @pl.when(sub == 0)
    def _():
        copy = pltpu.make_async_copy(own, out, sem)
        copy.start()
        copy.wait()

    @pl.when(sub != 0)
    def _():
        copy = pltpu.make_async_copy(got, out, sem)
        copy.start()
        copy.wait()


def relay(own, got, after):
    return pl.pallas_call(
        relay_kernel,
        out_shape=jax.ShapeDtypeStruct(own.shape, own.dtype),
        in_specs=[ANY, ANY, ANY],
        out_specs=ANY,
        scratch_shapes=[pltpu.SemaphoreType.DMA(())],
        compiler_params=params(),
        cost_estimate=pl.CostEstimate(flops=0, bytes_accessed=4 * own.size, transcendentals=0),
        name="relay_block",
    )(own, got, after)


def selector_of(owner, tenants, rank):
    rows = owner.shape[1]
    tenant = lax.broadcasted_iota(jnp.int32, (tenants * rank, rows), 0) // rank
    return tenant == owner


def fold(full, owner, tenants, rank):
    kept = jnp.where(selector_of(owner, tenants, rank), full, 0.0)
    total = kept[0:rank]
    for t in range(1, tenants):
        total = total + kept[t * rank : (t + 1) * rank]
    return total


def unfold(compact, owner, tenants, rank):
    spread = jnp.concatenate([compact] * tenants, axis=0)
    return jnp.where(selector_of(owner, tenants, rank), spread, 0.0)


def down_kernel(
    tenants, rank, x_hbm, adapter_hbm, doc_hbm, tenant_of, compact, owner, x, adapter, doc, sems
):
    copies = fetch([(doc_hbm, doc), (x_hbm, x), (adapter_hbm, adapter)], sems)
    copies[0].wait()
    ids = doc[...]
    found = jnp.zeros(ids.shape, jnp.int32)
    for s in range(tenant_of.shape[0]):
        found = jnp.where(ids == s, tenant_of[s], found)
    owner[...] = found
    copies[1].wait()
    copies[2].wait()
    compact[...] = fold(nt(x[...], adapter[...]).T, found, tenants, rank)


def down_project(x, adapter, doc, tenant_of, tenants, rank):
    rows, width = x.shape
    return pl.pallas_call(
        functools.partial(down_kernel, tenants, rank),
        out_shape=[
            jax.ShapeDtypeStruct((rank, rows), jnp.float32),
            jax.ShapeDtypeStruct((1, rows), jnp.int32),
        ],
        in_specs=[ANY, ANY, ANY, SM],
        out_specs=[VM, VM],
        scratch_shapes=[
            pltpu.VMEM(x.shape, x.dtype),
            pltpu.VMEM(adapter.shape, adapter.dtype),
            pltpu.VMEM(doc.shape, doc.dtype),
            pltpu.SemaphoreType.DMA((3,)),
        ],
        compiler_params=params(VMEM_MOST),
        cost_estimate=pl.CostEstimate(
            flops=2 * rows * width * tenants * rank,
            bytes_accessed=2 * width * (rows + tenants * rank),
            transcendentals=0,
        ),
        name="down_project",
    )(x, adapter, doc, tenant_of)


def attention_kernel(
    tenants, rank, group, first,
    base, grad, up, own_k, own_v, two_k, two_v, swap_k, swap_v, pass_k, pass_v,
    own_c, other_c, owner, own_tail, two_tail, swap_tail, pass_tail, *rest,
):
    if first:
        out, part_b, gdown, *scratch = rest
        gdown_before = None
    else:
        gdown_before, _, out, part_b, gdown, *scratch = rest
    bottle, bottle_t, bias, query, gquery, kt, kw, vt, vw, s_ref, gsum, blocks = scratch
    rows = base.shape[0]
    sub = lax.axis_index("sub")
    step = pl.program_id(0)
    last = pl.num_programs(0) - 1
    scale = HEAD**-0.5

    @pl.when(step == 0)
    def _():
        lifted = unfold(own_c[...] + other_c[...], owner[...], tenants, rank)
        bottle_t[...] = lifted.astype(jnp.bfloat16)
        bottle[...] = lifted.T.astype(jnp.bfloat16)
        gsum[...] = jnp.zeros_like(gsum)
        mine = own_tail[0:1, 0:rows].astype(jnp.float32)
        column = jnp.broadcast_to(mine, (rows, rows)).T
        swapped = swap_tail[0:1, 0:rows].astype(jnp.float32)
        passed = pass_tail[0:1, 0:rows].astype(jnp.float32)
        near = jnp.where(sub == 0, swapped, passed)
        far = jnp.where(sub == 0, passed, swapped)
        two = two_tail[0:1, 0:rows].astype(jnp.float32)
        for d, ids in ((3, far), (2, two), (1, near)):
            at = (REACH - d) * rows
            bias[:, at : at + rows] = jnp.where(column == ids, 0.0, NEG)
        causal = lax.broadcasted_iota(jnp.int32, (rows, rows), 0) >= lax.broadcasted_iota(
            jnp.int32, (rows, rows), 1
        )
        bias[:, REACH * rows :] = jnp.where(causal & (column == mine), 0.0, NEG)
        head = jnp.min(mine)
        reach = jnp.where(jnp.max(near) == head, 1, 0)
        reach = jnp.where(jnp.max(two) == head, 2, reach)
        blocks[0] = jnp.where(jnp.max(far) == head, 3, reach)

    ones = jnp.ones((rows, HEAD), jnp.bfloat16)
    ones_two = jnp.ones((2 * HEAD, HEAD), jnp.bfloat16)

    def place(slot, k_block, v_block):
        at = pl.ds(slot * rows, rows)
        k = k_block[0:rows, :]
        v = v_block[0:rows, :]
        kw[at, :] = k
        vw[at, 0:HEAD] = v
        vw[at, HEAD:] = ones
        kt[:, at] = k.T
        vt[:, at] = v.T

    place(REACH, own_k, own_v)
    place(REACH - 2, two_k, two_v)

    @pl.when(sub == 0)
    def _():
        place(REACH - 1, swap_k, swap_v)
        place(REACH - 3, pass_k, pass_v)

    @pl.when(sub != 0)
    def _():
        place(REACH - 1, pass_k, pass_v)
        place(REACH - 3, swap_k, swap_v)

    query[...] = (base[...].astype(jnp.float32) + LIFT * nn(bottle[...], up[...])).astype(
        jnp.bfloat16
    )

    def run(count, heads):
        chunks = range(REACH - count, REACH + 1)
        cols = [pl.ds(h * HEAD, HEAD) for h in heads]
        slots = range(len(heads))

        def keys(c):
            return slice(c * rows, (c + 1) * rows)

        def lanes_max(s):
            m = s[:, 0:HEAD]
            for at in range(HEAD, rows, HEAD):
                m = jnp.maximum(m, s[:, at : at + HEAD])
            return m

        peaks = [None] * len(heads)
        for c in chunks:
            for i in slots:
                s = nn(query[:, cols[i]], kt[:, keys(c)]) + bias[:, keys(c)]
                s_ref[i, :, keys(c)] = s
                m = lanes_max(s)
                peaks[i] = m if peaks[i] is None else jnp.maximum(peaks[i], m)
        peaks = [jnp.max(m, axis=1, keepdims=True) for m in peaks]
        sums = [None] * len(heads)
        for c in chunks:
            for i in slots:
                w = jnp.exp2((s_ref[i, :, keys(c)] - peaks[i]) * (scale * LOG2E))
                s_ref[i, :, keys(c)] = w
                o = nn(w.astype(jnp.bfloat16), vw[keys(c), :])
                sums[i] = o if sums[i] is None else sums[i] + o
        inverses, rowdots = [], []
        for i in slots:
            inverse = 1.0 / sums[i][:, HEAD:]
            attn = (sums[i][:, 0:HEAD] * inverse).astype(jnp.bfloat16)
            out[:, cols[i]] = attn
            product = grad[:, cols[i]].astype(jnp.float32) * attn.astype(jnp.float32)
            high = product.astype(jnp.bfloat16)
            low = (product - high.astype(jnp.float32)).astype(jnp.bfloat16)
            dot = nn(jnp.concatenate([high, low], axis=1), ones_two)
            rowdots.append(jnp.concatenate([dot] * (rows // HEAD), axis=1))
            inverses.append(inverse)
        moved = [None] * len(heads)
        for c in chunks:
            for i in slots:
                dprob = nn(grad[:, cols[i]], vt[:, keys(c)])
                ds = (s_ref[i, :, keys(c)] * (dprob - rowdots[i])).astype(jnp.bfloat16)
                dq = nn(ds, kw[keys(c), :])
                moved[i] = dq if moved[i] is None else moved[i] + dq
        for i in slots:
            gquery[:, cols[i]] = (moved[i] * (inverses[i] * (LIFT * scale))).astype(jnp.bfloat16)

    pair = s_ref.shape[0]
    for count in range(REACH + 1):

        @pl.when(blocks[0] == count)
        def _():
            @pl.loop(0, group // pair)
            def _(i):
                run(count, [i * pair + k for k in range(pair)])

    part_b[...] = nn(bottle_t[...], gquery[...]).astype(jnp.bfloat16)
    gsum[...] += nt(up[...], gquery[...])

    @pl.when(step == last)
    def _():
        total = fold(gsum[...], owner[...], tenants, rank)
        gdown[...] = total if gdown_before is None else total + gdown_before[...]


def attention(
    chunk, chunks, base, grad, up, own, two, swap, passed, own_c, other_c, owner, before, tenants, rank
):
    rows, width = base.shape
    payload_rows, payload_width = own.shape
    heads = payload_width // (2 * HEAD)
    group = width // HEAD // (heads * chunks)
    span = group * HEAD
    first = before is None
    offset = chunk * heads
    wide = lambda r: pl.BlockSpec((r, span), lambda i: (0, i + offset))
    key_block = pl.BlockSpec((payload_rows, HEAD), lambda i: (0, i))
    value_block = pl.BlockSpec((payload_rows, HEAD), lambda i: (0, i + heads))
    tail = pl.BlockSpec((TAIL, payload_width), lambda i: (rows // TAIL, 0))
    same = lambda a: pl.BlockSpec(a.shape, lambda i: (0, 0))
    operands = [base, grad, up]
    specs = [wide(rows), wide(rows), wide(up.shape[0])]
    for block in (own, two, swap, passed):
        operands += [block, block]
        specs += [key_block, value_block]
    operands += [own_c, other_c, owner, own, two, swap, passed]
    specs += [same(own_c), same(other_c), same(owner), tail, tail, tail, tail]
    aliases = {}
    if not first:
        operands += [before[2], before[0]]
        specs += [same(before[2]), ANY]
        aliases = {len(operands) - 1: 0}
    window = (REACH + 1) * rows
    pair = min(4, group)
    return pl.pallas_call(
        functools.partial(attention_kernel, tenants, rank, group, first),
        grid=(heads,),
        out_shape=[
            jax.ShapeDtypeStruct((rows, width), jnp.bfloat16),
            jax.ShapeDtypeStruct((tenants * rank, heads * span), jnp.bfloat16),
            jax.ShapeDtypeStruct((rank, rows), jnp.float32),
        ],
        in_specs=specs,
        out_specs=[
            wide(rows),
            pl.BlockSpec((tenants * rank, span), lambda i: (0, i)),
            pl.BlockSpec((rank, rows), lambda i: (0, 0)),
        ],
        scratch_shapes=[
            pltpu.VMEM((rows, tenants * rank), jnp.bfloat16),
            pltpu.VMEM((tenants * rank, rows), jnp.bfloat16),
            pltpu.VMEM((rows, window), jnp.float32),
            pltpu.VMEM((rows, span), jnp.bfloat16),
            pltpu.VMEM((rows, span), jnp.bfloat16),
            pltpu.VMEM((HEAD, window), jnp.bfloat16),
            pltpu.VMEM((window, HEAD), jnp.bfloat16),
            pltpu.VMEM((HEAD, window), jnp.bfloat16),
            pltpu.VMEM((window, 2 * HEAD), jnp.bfloat16),
            pltpu.VMEM((pair, rows, window), jnp.float32),
            pltpu.VMEM((tenants * rank, rows), jnp.float32),
            pltpu.SMEM((1,), jnp.int32),
        ],
        input_output_aliases=aliases,
        compiler_params=params(),
        cost_estimate=pl.CostEstimate(
            flops=8 * rows * window * span * heads,
            bytes_accessed=6 * rows * span * heads,
            transcendentals=rows * window * group * heads,
        ),
        name="attention",
    )(*operands)


def part_a_kernel(tenants, rank, own, other, owner, x, out):
    g = unfold(own[...] + other[...], owner[...], tenants, rank).astype(jnp.bfloat16)
    out[...] = nn(g, x[...]).astype(jnp.bfloat16)


def grad_a_part(own, other, owner, x, tenants, rank):
    rows, width = x.shape
    return pl.pallas_call(
        functools.partial(part_a_kernel, tenants, rank),
        out_shape=jax.ShapeDtypeStruct((tenants * rank, width), jnp.bfloat16),
        in_specs=[VM] * 4,
        out_specs=VM,
        compiler_params=params(),
        cost_estimate=pl.CostEstimate(
            flops=2 * rows * width * tenants * rank,
            bytes_accessed=2 * width * (rows + tenants * rank),
            transcendentals=0,
        ),
        name="grad_a_part",
    )(own, other, owner, x)


def small_call(kernel, name, shapes, *operands, scratch=()):
    size = sum(2 * a.size for a in operands)
    return pl.pallas_call(
        kernel,
        out_shape=shapes,
        in_specs=[VM] * len(operands),
        out_specs=jax.tree.map(lambda _: VM, shapes),
        scratch_shapes=list(scratch),
        compiler_params=params(),
        cost_estimate=pl.CostEstimate(flops=size, bytes_accessed=2 * size, transcendentals=0),
        name=name,
    )(*operands)


def split_kernel(tenants, rank, own, other, owner, x, *rest):
    parts, keep, send = rest[:-2], rest[-2], rest[-1]
    g = unfold(own[...] + other[...], owner[...], tenants, rank).astype(jnp.bfloat16)
    a = nn(g, x[...]).astype(jnp.bfloat16)
    half = keep.shape[0]
    sub = lax.axis_index("sub")

    def put(mine, theirs):
        for out, at in ((keep, mine * half), (send, theirs * half)):
            col = 0
            for part in parts:
                out[:, col : col + part.shape[1]] = part[at : at + half, :]
                col += part.shape[1]
            out[:, col:] = a[at : at + half, :]

    @pl.when(sub == 0)
    def _():
        put(0, 1)

    @pl.when(sub != 0)
    def _():
        put(1, 0)


def add_kernel(keep, got, out):
    out[...] = (keep[...].astype(jnp.float32) + got[...].astype(jnp.float32)).astype(jnp.bfloat16)


def sum_kernel(size, blocks, out):
    rows = out.shape[0] // size
    total = blocks[0:rows, :].astype(jnp.float32)
    for i in range(1, size):
        total = total + blocks[i * rows : (i + 1) * rows, :].astype(jnp.float32)
    total = total.astype(jnp.bfloat16)
    for i in range(size):
        out[i * rows : (i + 1) * rows, :] = total


def finish_kernel(half_ref, other_ref, grad_b, grad_a):
    sub = lax.axis_index("sub")
    half = half_ref.shape[0]
    wide = grad_b.shape[1]

    def put(ref, at):
        grad_b[at : at + half, :] = ref[:, 0:wide].astype(jnp.float32)
        grad_a[at : at + half, :] = ref[:, wide:].astype(jnp.float32)

    @pl.when(sub == 0)
    def _():
        put(half_ref, 0)
        put(other_ref, half)

    @pl.when(sub != 0)
    def _():
        put(half_ref, half)
        put(other_ref, 0)


def grads_by_halves(parts, own, other, owner, x, tenants, rank):
    rows, width = tenants * rank, x.shape[1]
    size = lax.axis_size("seq")
    wide = sum(part.shape[1] for part in parts)
    half = jax.ShapeDtypeStruct((rows // 2, wide + width), jnp.bfloat16)
    keep, send = small_call(
        functools.partial(split_kernel, tenants, rank), "split_grads", [half, half],
        own, other, owner, x, *parts,
    )
    mine = small_call(add_kernel, "add_cores", half, keep, swap_over(send, "sub"))
    blocks = lax.all_to_all(mine, "seq", 0, 0, tiled=True)
    summed = small_call(functools.partial(sum_kernel, size), "sum_grads", half, blocks)
    gathered = lax.all_to_all(summed, "seq", 0, 0, tiled=True)
    return small_call(
        finish_kernel, "finish_grads",
        [
            jax.ShapeDtypeStruct((rows, wide), jnp.float32),
            jax.ShapeDtypeStruct((rows, width), jnp.float32),
        ],
        gathered, swap_over(gathered, "sub"),
    )


def swap_over(block, axis):
    return lax.ppermute(block, axis, [(0, 1), (1, 0)])


def terms_over(block, axis):
    if lax.axis_size(axis) == 2:
        return block, swap_over(block, axis)
    return lax.psum(block, axis), jnp.zeros_like(block)


def shift_over(block, axis):
    size = lax.axis_size(axis)
    return lax.ppermute(block, axis, [(i, i + 1) for i in range(size - 1)])


def body(
    normed_inputs, base_queries, base_keys, base_values, adapter_down, adapter_up,
    position_document, document_tenant, output_gradient,
):
    rows, width = normed_inputs.shape
    tenants, _, rank = adapter_down.shape
    up_width = adapter_up.shape[2]
    doc = position_document.reshape(1, rows)
    adapter = jnp.transpose(adapter_down, (0, 2, 1)).reshape(tenants * rank, width)
    up = adapter_up.reshape(tenants * rank, up_width)

    chunks = 2 if base_keys.shape[1] % (2 * HEAD) == 0 else 1

    own = pack(base_keys, base_values, doc, chunks)
    two = [shift_over(block, "seq") for block in own]
    compact, owner = down_project(normed_inputs, adapter, doc, document_tenant, tenants, rank)
    swapped = [swap_over(block, "sub") for block in two]
    passed = [shift_over(relay(o, t, compact), ("seq", "sub")) for o, t in zip(own, two)]

    compact, other = terms_over(compact, "mp")
    by_hand = tenants * rank % (2 * TAIL * lax.axis_size("seq")) == 0
    before, parts = None, []
    for c in range(chunks):
        before = attention(
            c, chunks, base_queries, output_gradient, up, own[c], two[c], swapped[c], passed[c],
            compact, other, owner, before, tenants, rank,
        )
        parts.append(before[1])
    attn_out, _, gdown = before
    gdown, other = terms_over(gdown, "mp")
    if by_hand:
        grad_b, grad_a = grads_by_halves(
            parts, gdown, other, owner, normed_inputs, tenants, rank
        )
    else:
        part_a = grad_a_part(gdown, other, owner, normed_inputs, tenants, rank)
        grad_a = lax.psum(part_a, ("seq", "sub")).astype(jnp.float32)
        grad_b = lax.psum(jnp.concatenate(parts, axis=1), ("seq", "sub")).astype(jnp.float32)
    grad_a = jnp.transpose(grad_a.reshape(tenants, rank, width), (0, 2, 1))
    return attn_out, grad_a, grad_b.reshape(tenants, rank, up_width)


def solution(mesh):
    split = P(("rep", "seq", "sub"), "mp")
    in_specs = (
        split, split, split, split, P(None, "mp", None), P(None, None, "mp"),
        P(("rep", "seq", "sub")), P("rep"), split,
    )
    out_specs = (split, P("rep", "mp", None), P("rep", None, "mp"))
    return jax.shard_map(body, mesh=mesh, in_specs=in_specs, out_specs=out_specs, check_vma=False)
```

```python
import functools

import jax
import jax.numpy as jnp
from jax import lax
from jax.experimental import pallas as pl
from jax.experimental.pallas import tpu as pltpu
from jax.sharding import PartitionSpec as P

HEAD = 128
REACH = 3
NEG = -1e30
LIFT = 2.0
LOG2E = 1.4426950408889634
TAIL = 16
VMEM_BYTES = 48 * 1024 * 1024
VMEM_MOST = 60 * 1024 * 1024

VM = pl.BlockSpec(memory_space=pltpu.VMEM)
SM = pl.BlockSpec(memory_space=pltpu.SMEM)
ANY = pl.BlockSpec(memory_space=pl.ANY)


def nt(a, b):
    return lax.dot_general(a, b, (((1,), (1,)), ((), ())), preferred_element_type=jnp.float32)


def nn(a, b):
    return jnp.dot(a, b, preferred_element_type=jnp.float32)


def params(limit=VMEM_BYTES):
    return pltpu.CompilerParams(vmem_limit_bytes=limit)


def fetch(pairs, sems):
    copies = [pltpu.make_async_copy(src, dst, sems.at[i]) for i, (src, dst) in enumerate(pairs)]
    for copy in copies:
        copy.start()
    return copies


def pack_kernel(counts, keys, values, doc, *rest):
    outs, (ids, blocks, tail, sems) = rest[: len(counts)], rest[len(counts) :]
    rows, width = keys.shape
    loads = fetch(
        [(doc, ids), (keys, blocks.at[0]), (values, blocks.at[1])], sems.at[pl.ds(0, 3)]
    )
    loads[0].wait()
    tail[...] = jnp.zeros_like(tail)
    tail[:, 0:rows] = jnp.broadcast_to((ids[...] + 1).astype(jnp.float32), (TAIL, rows)).astype(
        jnp.bfloat16
    )
    pairs, first = [(tail, outs[0].at[pl.ds(rows, TAIL), :])], 0
    for count, out in zip(counts, outs):
        for half in range(2):
            source = blocks.at[half, :, pl.ds(first * HEAD, count * HEAD)]
            pairs.append((source, out.at[pl.ds(0, rows), pl.ds(half * count * HEAD, count * HEAD)]))
        first += count
    loads[1].wait()
    loads[2].wait()
    for copy in fetch(pairs, sems.at[pl.ds(3, len(pairs))]):
        copy.wait()


def pack(keys, values, doc, counts):
    rows, width = keys.shape
    shapes = [
        jax.ShapeDtypeStruct((rows + (0 if i else TAIL), 2 * count * HEAD), jnp.bfloat16)
        for i, count in enumerate(counts)
    ]
    return pl.pallas_call(
        functools.partial(pack_kernel, counts),
        out_shape=shapes,
        in_specs=[ANY] * 3,
        out_specs=[ANY] * len(counts),
        scratch_shapes=[
            pltpu.VMEM((1, rows), jnp.int32),
            pltpu.VMEM((2, rows, width), jnp.bfloat16),
            pltpu.VMEM((TAIL, shapes[0].shape[1]), jnp.bfloat16),
            pltpu.SemaphoreType.DMA((4 + 2 * len(counts),)),
        ],
        compiler_params=params(VMEM_MOST),
        cost_estimate=pl.CostEstimate(flops=0, bytes_accessed=8 * rows * width, transcendentals=0),
        name="pack_keys_values",
    )(keys, values, doc)


def relay_kernel(own, got, after, out, held, sems):
    sub = lax.axis_index("sub")

    def move(source):
        load = pltpu.make_async_copy(source, held, sems.at[0])
        load.start()
        load.wait()

    @pl.when(sub == 0)
    def _():
        move(own)

    @pl.when(sub != 0)
    def _():
        move(got)

    store = pltpu.make_async_copy(held, out, sems.at[1])
    store.start()
    store.wait()


def relay(own, got, after):
    return pl.pallas_call(
        relay_kernel,
        out_shape=jax.ShapeDtypeStruct(own.shape, own.dtype),
        in_specs=[ANY, ANY, ANY],
        out_specs=ANY,
        scratch_shapes=[pltpu.VMEM(own.shape, own.dtype), pltpu.SemaphoreType.DMA((2,))],
        compiler_params=params(),
        cost_estimate=pl.CostEstimate(flops=0, bytes_accessed=4 * own.size, transcendentals=0),
        name="relay_block",
    )(own, got, after)


def selector_of(owner, tenants, rank):
    rows = owner.shape[1]
    tenant = lax.broadcasted_iota(jnp.int32, (tenants * rank, rows), 0) // rank
    return tenant == owner


def fold(full, owner, tenants, rank):
    kept = jnp.where(selector_of(owner, tenants, rank), full, 0.0)
    total = kept[0:rank]
    for t in range(1, tenants):
        total = total + kept[t * rank : (t + 1) * rank]
    return total


def unfold(compact, owner, tenants, rank):
    spread = jnp.concatenate([compact] * tenants, axis=0)
    return jnp.where(selector_of(owner, tenants, rank), spread, 0.0)


def down_kernel(tenants, rank, x_hbm, adapter_hbm, doc_hbm, tenant_of, info, x, adapter, doc, sems):
    copies = fetch([(doc_hbm, doc), (x_hbm, x), (adapter_hbm, adapter)], sems)
    copies[0].wait()
    ids = doc[...]
    found = jnp.zeros(ids.shape, jnp.int32)
    for s in range(tenant_of.shape[0]):
        found = jnp.where(ids == s, tenant_of[s], found)
    info[rank:, :] = jnp.broadcast_to(found.astype(jnp.float32), (info.shape[0] - rank, ids.shape[1]))
    copies[1].wait()
    copies[2].wait()
    info[0:rank, :] = fold(nt(x[...], adapter[...]).T, found, tenants, rank)


def down_project(x, adapter, doc, tenant_of, tenants, rank):
    rows, width = x.shape
    return pl.pallas_call(
        functools.partial(down_kernel, tenants, rank),
        out_shape=jax.ShapeDtypeStruct((rank + 8, rows), jnp.float32),
        in_specs=[ANY, ANY, ANY, SM],
        out_specs=VM,
        scratch_shapes=[
            pltpu.VMEM(x.shape, x.dtype),
            pltpu.VMEM(adapter.shape, adapter.dtype),
            pltpu.VMEM(doc.shape, doc.dtype),
            pltpu.SemaphoreType.DMA((3,)),
        ],
        compiler_params=params(VMEM_MOST),
        cost_estimate=pl.CostEstimate(
            flops=2 * rows * width * tenants * rank,
            bytes_accessed=2 * width * (rows + tenants * rank),
            transcendentals=0,
        ),
        name="down_project",
    )(x, adapter, doc, tenant_of)


def owner_of(info, rank):
    return info[rank : rank + 1, :].astype(jnp.int32)


def attention(
    head, at, base, grad, up, blocks, first, info, terms, before, after, tenants, rank
):
    rows, width = base.shape
    count = blocks[0].shape[1] // (2 * HEAD)
    window = (REACH + 1) * rows
    tall = tenants * rank
    heads = up.shape[1] // HEAD
    group = heads // (first[4])
    span = group * HEAD
    pair = min(4, group)
    scale = HEAD**-0.5
    operands = [base, grad, up, *blocks, *first[:4], info, *terms]
    if before is not None:
        operands += [before[1], before[0]]
    operands += after
    held = dict(
        base=pltpu.VMEM((rows, span), jnp.bfloat16),
        grad=pltpu.VMEM((rows, span), jnp.bfloat16),
        up=pltpu.VMEM((tall, span), jnp.bfloat16),
        kw=pltpu.VMEM((window, HEAD), jnp.bfloat16),
        vw=pltpu.VMEM((window, HEAD), jnp.bfloat16),
        kt=pltpu.VMEM((HEAD, window), jnp.bfloat16),
        vt=pltpu.VMEM((HEAD + TAIL, window), jnp.bfloat16),
        ids=pltpu.VMEM((4, TAIL, rows), jnp.bfloat16),
        info=pltpu.VMEM((3, *info.shape), jnp.float32),
        summed=pltpu.VMEM((rank, rows), jnp.float32),
        bias=pltpu.VMEM((window, rows), jnp.float32),
        query=pltpu.VMEM((span, rows), jnp.bfloat16),
        gt=pltpu.VMEM((span, rows), jnp.bfloat16),
        gquery=pltpu.VMEM((span, rows), jnp.bfloat16),
        scores=pltpu.VMEM((pair, window, rows), jnp.float32),
        out=pltpu.VMEM((rows, span), jnp.bfloat16),
        part=pltpu.VMEM((tall, span), jnp.bfloat16),
        reach=pltpu.SMEM((1,), jnp.int32),
        sems=pltpu.SemaphoreType.DMA((22,)),
    )

    def kernel(*refs):
        base_h, grad_h, up_h = refs[0:3]
        blocks_h, tails_h, info_h, terms_h = refs[3:7], refs[7:11], refs[11], refs[12:14]
        before_h = refs[14] if before is not None else None
        out_h, keep_h, send_h, summed_h = refs[len(operands) : len(operands) + 4]
        r = dict(zip(held, refs[len(operands) + 4 :]))
        base, grad, up, kw, vw, kt, vt = (r[n] for n in ("base", "grad", "up", "kw", "vw", "kt", "vt"))
        bias, query, gt, gquery, scores, sems = (
            r[n] for n in ("bias", "query", "gt", "gquery", "scores", "sems")
        )
        sub = lax.axis_index("sub")
        near = jnp.where(sub == 0, REACH - 1, REACH - 3)
        far = jnp.where(sub == 0, REACH - 3, REACH - 1)
        slots = (REACH, REACH - 2, near, far)
        cols = pl.ds(head * span, span)
        early = [(info_h, r["info"].at[0]), (terms_h[0], r["info"].at[1]), (terms_h[1], r["info"].at[2])]
        for slot, tail in zip(slots, tails_h):
            early.append((tail.at[pl.ds(rows, TAIL), pl.ds(0, rows)], r["ids"].at[slot]))
        early += [(base_h.at[:, cols], base), (up_h.at[:, cols], up)]
        late = []
        for slot, block in zip(slots, blocks_h):
            to = pl.ds(pl.multiple_of(slot * rows, rows), rows)
            late.append((block.at[pl.ds(0, rows), pl.ds(at * HEAD, HEAD)], kw.at[to, :]))
            late.append((block.at[pl.ds(0, rows), pl.ds((count + at) * HEAD, HEAD)], vw.at[to, :]))
        late.append((grad_h.at[:, cols], grad))
        if before_h is not None:
            late.append((before_h, r["summed"]))
        early = fetch(early, sems.at[pl.ds(0, len(early))])
        late = fetch(late, sems.at[pl.ds(len(early), len(late))])
        for copy in early:
            copy.wait()

        owner = owner_of(r["info"][0], rank)
        lifted = unfold((r["info"][1] + r["info"][2])[0:rank], owner, tenants, rank)
        bottle_t = lifted.astype(jnp.bfloat16)
        bottle = lifted.T.astype(jnp.bfloat16)
        query[...] = (
            (base[...].astype(jnp.float32) + LIFT * nn(bottle, up[...])).astype(jnp.bfloat16).T
        )
        mine = r["ids"][REACH].astype(jnp.float32)[0:1, :]
        lowest = jnp.min(mine)
        reach = 0
        for slot in range(REACH, -1, -1):
            ids = r["ids"][slot].astype(jnp.float32)
            same = ids.T[:, 0:1] == mine
            if slot == REACH:
                same = same & (
                    lax.broadcasted_iota(jnp.int32, (rows, rows), 0)
                    <= lax.broadcasted_iota(jnp.int32, (rows, rows), 1)
                )
            else:
                reach = jnp.where(jnp.max(ids[0:1, :]) == lowest, REACH - slot, reach)
            bias[slot * rows : (slot + 1) * rows, :] = jnp.where(same, 0.0, NEG)
        r["reach"][0] = reach
        for copy in late:
            copy.wait()
        gt[...] = grad[...].T
        kt[...] = kw[...].T
        vt[0:HEAD, :] = vw[...].T
        vt[HEAD:, :] = jnp.ones((TAIL, window), jnp.bfloat16)

        def run(reached, numbers):
            chunks = [slice(c * rows, (c + 1) * rows) for c in range(REACH - reached, REACH + 1)]
            spans = [pl.ds(pl.multiple_of(h * HEAD, HEAD), HEAD) for h in numbers]
            peaks = []
            for i, span_i in enumerate(spans):
                q, peak = query[span_i, :], None
                for c in chunks:
                    s = nn(kw[c, :], q) + bias[c, :]
                    scores[i, c, :] = s
                    top = jnp.max(s, axis=0, keepdims=True)
                    peak = top if peak is None else jnp.maximum(peak, top)
                peaks.append(peak)
            inverses, rowdots = [], []
            for i, span_i in enumerate(spans):
                total = None
                for c in chunks:
                    w = jnp.exp2((scores[i, c, :] - peaks[i]) * (scale * LOG2E))
                    scores[i, c, :] = w
                    o = nn(vt[:, c], w.astype(jnp.bfloat16))
                    total = o if total is None else total + o
                inverse = 1.0 / total[HEAD : HEAD + 1, :]
                attn = (total[0:HEAD, :] * inverse).astype(jnp.bfloat16)
                r["out"][:, span_i] = attn.T
                product = gt[span_i, :].astype(jnp.float32) * attn.astype(jnp.float32)
                rowdots.append(jnp.sum(product, axis=0, keepdims=True))
                inverses.append(inverse)
            for i, span_i in enumerate(spans):
                g, moved = gt[span_i, :], None
                for c in chunks:
                    dprob = nn(vw[c, :], g)
                    ds = (scores[i, c, :] * (dprob - rowdots[i])).astype(jnp.bfloat16)
                    dq = nn(kt[:, c], ds)
                    moved = dq if moved is None else moved + dq
                gquery[span_i, :] = (moved * (inverses[i] * (LIFT * scale))).astype(jnp.bfloat16)

        for reached in range(REACH + 1):

            @pl.when(r["reach"][0] == reached)
            def _():
                @pl.loop(0, group // pair)
                def _(i):
                    run(reached, [i * pair + k for k in range(pair)])

        done = fetch([(r["out"], out_h.at[:, cols])], sems.at[pl.ds(0, 1)])
        r["part"][...] = nt(bottle_t, gquery[...]).astype(jnp.bfloat16)
        half = tall // 2
        here = pl.ds(pl.multiple_of(sub * half, half), half)
        there = pl.ds(pl.multiple_of((1 - sub) * half, half), half)
        done += fetch(
            [(r["part"].at[here, :], keep_h), (r["part"].at[there, :], send_h)], sems.at[pl.ds(1, 2)]
        )
        total = fold(nn(up[...], gquery[...]), owner, tenants, rank)
        r["summed"][...] = total if before_h is None else total + r["summed"][...]
        done += fetch([(r["summed"], summed_h)], sems.at[pl.ds(3, 1)])
        for copy in done:
            copy.wait()

    return pl.pallas_call(
        kernel,
        out_shape=[
            jax.ShapeDtypeStruct((rows, width), jnp.bfloat16),
            *halves_of(tall, span),
            jax.ShapeDtypeStruct((rank, rows), jnp.float32),
        ],
        in_specs=[ANY] * len(operands),
        out_specs=[ANY] * 4,
        scratch_shapes=list(held.values()),
        input_output_aliases={15: 0} if before is not None else {},
        compiler_params=params(VMEM_MOST),
        cost_estimate=pl.CostEstimate(
            flops=8 * rows * window * span,
            bytes_accessed=6 * rows * span,
            transcendentals=rows * window * group,
        ),
        name="attention",
    )(*operands)


def small_call(kernel, name, shapes, *operands, after=(), through=(), scratch=()):
    size = sum(2 * a.size for a in operands)
    count, results = len(operands), jax.tree.leaves(shapes)
    given = (*operands, *after, *through)
    outs = len(given) + len(results)
    calls = pl.pallas_call(
        lambda *refs: kernel(
            *refs[:count], *refs[len(given) : outs], *refs[outs + len(through) :]
        ),
        out_shape=results + [jax.ShapeDtypeStruct(a.shape, a.dtype) for a in through],
        in_specs=[VM] * count + [ANY] * (len(after) + len(through)),
        out_specs=[VM] * len(results) + [ANY] * len(through),
        scratch_shapes=list(scratch),
        input_output_aliases={
            count + len(after) + i: len(results) + i for i in range(len(through))
        },
        compiler_params=params(),
        cost_estimate=pl.CostEstimate(flops=size, bytes_accessed=2 * size, transcendentals=0),
        name=name,
    )(*given)
    return calls if isinstance(shapes, list) or through else calls[0]


def grad_a_of(tenants, rank, one, other, info, x):
    g = unfold((one[...] + other[...]), owner_of(info[...], rank), tenants, rank)
    return nn(g.astype(jnp.bfloat16), x[...]).astype(jnp.bfloat16)


def grad_a_kernel(tenants, rank, one, other, info, x, out):
    out[...] = grad_a_of(tenants, rank, one, other, info, x)


def split_kernel(tenants, rank, one, other, info, x, keep, send):
    part = grad_a_of(tenants, rank, one, other, info, x)
    half = keep.shape[0]
    sub = lax.axis_index("sub")

    @pl.when(sub == 0)
    def _():
        keep[...] = part[0:half, :]
        send[...] = part[half:, :]

    @pl.when(sub != 0)
    def _():
        keep[...] = part[half:, :]
        send[...] = part[0:half, :]


def scatter_kernel(size, count, *refs):
    mine, *sends, total = refs[2 * count :]
    col = 0
    for keep, got in zip(refs[0 : 2 * count : 2], refs[1 : 2 * count : 2]):
        both = keep[...].astype(jnp.float32) + got[...].astype(jnp.float32)
        total[:, col : col + keep.shape[1]] = both.astype(jnp.bfloat16)
        col += keep.shape[1]
    me = lax.axis_index("seq")
    rows = mine.shape[0]
    for d, out in enumerate((mine, *sends)):
        at = pl.multiple_of(lax.rem(me + d, size) * rows, rows)
        out[...] = total[pl.ds(at, rows), :]


def sum_kernel(*refs):
    total = refs[0][...].astype(jnp.float32)
    for ref in refs[1:-1]:
        total = total + ref[...].astype(jnp.float32)
    refs[-1][...] = total.astype(jnp.bfloat16)


def gather_kernel(size, widths, *refs):
    out, col = refs[-1], 0
    me = lax.axis_index("seq")
    rows = refs[0].shape[0]
    for p, width in enumerate(widths):
        for d in range(size):
            at = pl.multiple_of(lax.rem(me + size - d, size) * rows, rows)
            out[pl.ds(at, rows), col : col + width] = refs[p * size + d][...]
        col += width


def finish_kernel(half_ref, other_ref, grad_b, grad_a):
    sub = lax.axis_index("sub")
    half = half_ref.shape[0]
    wide = grad_b.shape[1]

    def put(ref, at):
        grad_b[at : at + half, :] = ref[:, 0:wide].astype(jnp.float32)
        grad_a[at : at + half, :] = ref[:, wide:].astype(jnp.float32)

    @pl.when(sub == 0)
    def _():
        put(half_ref, 0)
        put(other_ref, half)

    @pl.when(sub != 0)
    def _():
        put(half_ref, half)
        put(other_ref, 0)


def halves_of(rows, width):
    return [jax.ShapeDtypeStruct((rows // 2, width), jnp.bfloat16)] * 2


def scatter(*pairs, after=()):
    size = lax.axis_size("seq")
    rows, width = pairs[0][0].shape[0], sum(keep.shape[1] for keep, _ in pairs)
    shard = jax.ShapeDtypeStruct((rows // size, width), jnp.bfloat16)
    return small_call(
        functools.partial(scatter_kernel, size, len(pairs)), "scatter_grads", [shard] * size,
        *[block for pair in pairs for block in pair],
        after=after, scratch=[pltpu.VMEM((rows, width), jnp.bfloat16)],
    )


def exchange(shards):
    return [shards[0]] + [rotate_over(block, "seq", d + 1) for d, block in enumerate(shards[1:])]


def add_up(pieces, after=(), through=()):
    shape = jax.ShapeDtypeStruct(pieces[0].shape, pieces[0].dtype)
    return small_call(sum_kernel, "sum_grads", shape, *pieces, after=after, through=through)


def spread(shard):
    return [shard] + [rotate_over(shard, "seq", d) for d in range(1, lax.axis_size("seq"))]


def swap_over(block, axis):
    return lax.ppermute(block, axis, [(0, 1), (1, 0)])


def rotate_over(block, axis, d):
    size = lax.axis_size(axis)
    return lax.ppermute(block, axis, [(i, (i + d) % size) for i in range(size)])


def terms_over(block, axis):
    if lax.axis_size(axis) == 2:
        return block, swap_over(block, axis)
    return lax.psum(block, axis), jnp.zeros_like(block)


def shift_over(block, axis):
    size = lax.axis_size(axis)
    return lax.ppermute(block, axis, [(i, i + 1) for i in range(size - 1)])


def body(
    normed_inputs, base_queries, base_keys, base_values, adapter_down, adapter_up,
    position_document, document_tenant, output_gradient,
):
    rows, width = normed_inputs.shape
    tenants, _, rank = adapter_down.shape
    tall, up_width = tenants * rank, adapter_up.shape[2]
    doc = position_document.reshape(1, rows)
    adapter = jnp.transpose(adapter_down, (0, 2, 1)).reshape(tall, width)
    up = adapter_up.reshape(tall, up_width)
    key_heads = base_keys.shape[1] // HEAD
    counts = (1, 1, 2) if key_heads == 4 else (1,) * key_heads
    places = [(c, i) for c, count in enumerate(counts) for i in range(count)]
    size = lax.axis_size("seq")
    by_hand = key_heads == 4 and tall % (2 * TAIL * size) == 0

    own = pack(base_keys, base_values, doc, counts)
    two = [shift_over(block, "seq") for block in own]
    info = down_project(normed_inputs, adapter, doc, document_tenant, tenants, rank)
    swapped = [swap_over(block, "sub") for block in two]
    passed = [shift_over(relay(o, t, info), ("seq", "sub")) for o, t in zip(own, two)]
    terms = terms_over(info, "mp")
    first = (own[0], two[0], swapped[0], passed[0], key_heads)

    def attend(head, before, after=()):
        c, at = places[head]
        out, keep, send, gdown = attention(
            head, at, base_queries, output_gradient, up,
            (own[c], two[c], swapped[c], passed[c]), first, info, terms, before, after, tenants, rank,
        )
        return (out, gdown), keep, send

    state, keep0, send0 = attend(0, None)
    if by_hand:
        got0 = swap_over(send0, "sub")
        state, keep1, send1 = attend(1, state)
        shards0 = scatter((keep0, got0), after=[keep1])
        pieces0 = exchange(shards0)
        got1 = swap_over(send1, "sub")
        state, keep2, send2 = attend(2, state, shards0[:1])
        sum0 = add_up(pieces0, after=[keep2])
        all0 = spread(sum0)
        shards1 = scatter((keep1, got1), after=[sum0])
        pieces1 = exchange(shards1)
        (out, gdown), keep3, send3 = attend(3, state, shards1[:1])
        sum1, gdown, send2, send3 = add_up(pieces1, after=all0, through=[gdown, send2, send3])
        all1 = spread(sum1)
        got2, got3 = swap_over(send2, "sub"), swap_over(send3, "sub")
        one, other = terms_over(gdown, "mp")
        keep4, send4 = small_call(
            functools.partial(split_kernel, tenants, rank), "split_grads", halves_of(tall, width),
            one, other, info, normed_inputs, after=[got2, got3, *all1[1:]],
        )
        shards2 = scatter((keep2, got2), (keep3, got3), (keep4, swap_over(send4, "sub")))
        all2 = spread(add_up(exchange(shards2)))
        widths = [pieces[0].shape[1] for pieces in (all0, all1, all2)]
        half = small_call(
            functools.partial(gather_kernel, size, widths), "gather_grads",
            jax.ShapeDtypeStruct((tall // 2, sum(widths)), jnp.bfloat16), *all0, *all1, *all2,
        )
        grad_b, grad_a = small_call(
            finish_kernel, "finish_grads",
            [
                jax.ShapeDtypeStruct((tall, up_width), jnp.float32),
                jax.ShapeDtypeStruct((tall, width), jnp.float32),
            ],
            half, swap_over(half, "sub"),
        )
    else:
        pairs = [(keep0, send0)]
        for head in range(1, key_heads):
            state, *pair = attend(head, state)
            pairs.append(pair)
        out, gdown = state
        one, other = terms_over(gdown, "mp")
        part_a = small_call(
            functools.partial(grad_a_kernel, tenants, rank), "grad_a_part",
            jax.ShapeDtypeStruct((tall, width), jnp.bfloat16), one, other, info, normed_inputs,
        )
        grad_a = lax.psum(part_a, ("seq", "sub")).astype(jnp.float32)
        keeps = jnp.concatenate([keep for keep, _ in pairs], axis=1)
        sends = jnp.concatenate([send for _, send in pairs], axis=1)
        low = lax.axis_index("sub") == 0
        part_b = jnp.concatenate([jnp.where(low, keeps, sends), jnp.where(low, sends, keeps)])
        grad_b = lax.psum(part_b, ("seq", "sub")).astype(jnp.float32)
    grad_a = jnp.transpose(grad_a.reshape(tenants, rank, width), (0, 2, 1))
    return out, grad_a, grad_b.reshape(tenants, rank, up_width)


def solution(mesh):
    split = P(("rep", "seq", "sub"), "mp")
    in_specs = (
        split, split, split, split, P(None, "mp", None), P(None, None, "mp"),
        P(("rep", "seq", "sub")), P("rep"), split,
    )
    out_specs = (split, P("rep", "mp", None), P("rep", None, "mp"))
    return jax.shard_map(body, mesh=mesh, in_specs=in_specs, out_specs=out_specs, check_vma=False)
```

```python
import functools

import jax
import jax.numpy as jnp
from jax import lax
from jax.experimental import pallas as pl
from jax.experimental.pallas import tpu as pltpu
from jax.sharding import PartitionSpec as P

HEAD = 128
REACH = 3
NEG = -1e30
LIFT = 2.0
LOG2E = 1.4426950408889634
TAIL = 16
VMEM_BYTES = 48 * 1024 * 1024
VMEM_MOST = 60 * 1024 * 1024
VMEM_HEADS = 57 * 1024 * 1024

VM = pl.BlockSpec(memory_space=pltpu.VMEM)
SM = pl.BlockSpec(memory_space=pltpu.SMEM)
ANY = pl.BlockSpec(memory_space=pl.ANY)


def nt(a, b):
    return lax.dot_general(a, b, (((1,), (1,)), ((), ())), preferred_element_type=jnp.float32)


def nn(a, b):
    return jnp.dot(a, b, preferred_element_type=jnp.float32)


def params(limit=VMEM_BYTES):
    return pltpu.CompilerParams(vmem_limit_bytes=limit)


def fetch(pairs, sems):
    copies = [pltpu.make_async_copy(src, dst, sems.at[i]) for i, (src, dst) in enumerate(pairs)]
    for copy in copies:
        copy.start()
    return copies


def pack_kernel(counts, keys, values, doc, *rest):
    outs, (ids, blocks, tail, sems) = rest[: len(counts)], rest[len(counts) :]
    rows, width = keys.shape
    loads = fetch(
        [(doc, ids), (keys, blocks.at[0]), (values, blocks.at[1])], sems.at[pl.ds(0, 3)]
    )
    loads[0].wait()
    tail[...] = jnp.zeros_like(tail)
    tail[:, 0:rows] = jnp.broadcast_to((ids[...] + 1).astype(jnp.float32), (TAIL, rows)).astype(
        jnp.bfloat16
    )
    pairs, first = [(tail, outs[0].at[pl.ds(rows, TAIL), :])], 0
    for count, out in zip(counts, outs):
        for half in range(2):
            source = blocks.at[half, :, pl.ds(first * HEAD, count * HEAD)]
            pairs.append((source, out.at[pl.ds(0, rows), pl.ds(half * count * HEAD, count * HEAD)]))
        first += count
    loads[1].wait()
    loads[2].wait()
    for copy in fetch(pairs, sems.at[pl.ds(3, len(pairs))]):
        copy.wait()


def pack(keys, values, doc, counts):
    rows, width = keys.shape
    shapes = [
        jax.ShapeDtypeStruct((rows + (0 if i else TAIL), 2 * count * HEAD), jnp.bfloat16)
        for i, count in enumerate(counts)
    ]
    return pl.pallas_call(
        functools.partial(pack_kernel, counts),
        out_shape=shapes,
        in_specs=[ANY] * 3,
        out_specs=[ANY] * len(counts),
        scratch_shapes=[
            pltpu.VMEM((1, rows), jnp.int32),
            pltpu.VMEM((2, rows, width), jnp.bfloat16),
            pltpu.VMEM((TAIL, shapes[0].shape[1]), jnp.bfloat16),
            pltpu.SemaphoreType.DMA((4 + 2 * len(counts),)),
        ],
        compiler_params=params(VMEM_MOST),
        cost_estimate=pl.CostEstimate(flops=0, bytes_accessed=8 * rows * width, transcendentals=0),
        name="pack_keys_values",
    )(keys, values, doc)


def relay_kernel(own, got, after, out, held, sems):
    sub = lax.axis_index("sub")

    def move(source):
        load = pltpu.make_async_copy(source, held, sems.at[0])
        load.start()
        load.wait()

    @pl.when(sub == 0)
    def _():
        move(own)

    @pl.when(sub != 0)
    def _():
        move(got)

    store = pltpu.make_async_copy(held, out, sems.at[1])
    store.start()
    store.wait()


def relay(own, got, after):
    return pl.pallas_call(
        relay_kernel,
        out_shape=jax.ShapeDtypeStruct(own.shape, own.dtype),
        in_specs=[ANY, ANY, ANY],
        out_specs=ANY,
        scratch_shapes=[pltpu.VMEM(own.shape, own.dtype), pltpu.SemaphoreType.DMA((2,))],
        compiler_params=params(),
        cost_estimate=pl.CostEstimate(flops=0, bytes_accessed=4 * own.size, transcendentals=0),
        name="relay_block",
    )(own, got, after)


def selector_of(owner, tenants, rank):
    rows = owner.shape[1]
    tenant = lax.broadcasted_iota(jnp.int32, (tenants * rank, rows), 0) // rank
    return tenant == owner


def fold(full, owner, tenants, rank):
    kept = jnp.where(selector_of(owner, tenants, rank), full, 0.0)
    total = kept[0:rank]
    for t in range(1, tenants):
        total = total + kept[t * rank : (t + 1) * rank]
    return total


def unfold(compact, owner, tenants, rank):
    spread = jnp.concatenate([compact] * tenants, axis=0)
    return jnp.where(selector_of(owner, tenants, rank), spread, 0.0)


def down_kernel(tenants, rank, x_hbm, adapter_hbm, doc_hbm, tenant_of, info, x, adapter, doc, sems):
    copies = fetch([(doc_hbm, doc), (x_hbm, x), (adapter_hbm, adapter)], sems)
    copies[0].wait()
    ids = doc[...]
    found = jnp.zeros(ids.shape, jnp.int32)
    for s in range(tenant_of.shape[0]):
        found = jnp.where(ids == s, tenant_of[s], found)
    info[rank:, :] = jnp.broadcast_to(found.astype(jnp.float32), (info.shape[0] - rank, ids.shape[1]))
    copies[1].wait()
    copies[2].wait()
    info[0:rank, :] = fold(nt(x[...], adapter[...]).T, found, tenants, rank)


def down_project(x, adapter, doc, tenant_of, tenants, rank):
    rows, width = x.shape
    return pl.pallas_call(
        functools.partial(down_kernel, tenants, rank),
        out_shape=jax.ShapeDtypeStruct((rank + 8, rows), jnp.float32),
        in_specs=[ANY, ANY, ANY, SM],
        out_specs=VM,
        scratch_shapes=[
            pltpu.VMEM(x.shape, x.dtype),
            pltpu.VMEM(adapter.shape, adapter.dtype),
            pltpu.VMEM(doc.shape, doc.dtype),
            pltpu.SemaphoreType.DMA((3,)),
        ],
        compiler_params=params(VMEM_MOST),
        cost_estimate=pl.CostEstimate(
            flops=2 * rows * width * tenants * rank,
            bytes_accessed=2 * width * (rows + tenants * rank),
            transcendentals=0,
        ),
        name="down_project",
    )(x, adapter, doc, tenant_of)


def owner_of(info, rank):
    return info[rank : rank + 1, :].astype(jnp.int32)


def attention(chunk, chunks, base, grad, up, blocks, first, info, terms, before, tenants, rank):
    rows, width = base.shape
    count = blocks[0].shape[1] // (2 * HEAD)
    window = (REACH + 1) * rows
    tall = tenants * rank
    half = tall // 2
    group = width // HEAD // (count * chunks)
    span = group * HEAD
    pair = min(4, group)
    scale = HEAD**-0.5
    offset = chunk * count
    wide = lambda r: pl.BlockSpec((r, span), lambda i: (0, i + offset))
    narrow = pl.BlockSpec((half, span), lambda i: (0, i))
    keys = pl.BlockSpec((rows, HEAD), lambda i: (0, i))
    values = pl.BlockSpec((rows, HEAD), lambda i: (0, i + count))
    ids = pl.BlockSpec((TAIL, rows), lambda i: (rows // TAIL, 0))
    same = lambda a: pl.BlockSpec(a.shape, lambda i: (0, 0))
    operands, specs = [base, grad, up], [wide(rows), wide(rows), wide(tall)]
    for block in blocks:
        operands += [block, block]
        specs += [keys, values]
    operands += [*first, info, *terms]
    specs += [ids] * 4 + [same(info)] * 3
    if before is not None:
        operands += [before[1], before[0]]
        specs += [same(before[1]), ANY]
    held = dict(
        kw=pltpu.VMEM((window, HEAD), jnp.bfloat16),
        vw=pltpu.VMEM((window, HEAD), jnp.bfloat16),
        kt=pltpu.VMEM((HEAD, window), jnp.bfloat16),
        vt=pltpu.VMEM((HEAD + TAIL, window), jnp.bfloat16),
        bottle=pltpu.VMEM((rows, tall), jnp.bfloat16),
        bottle_t=pltpu.VMEM((tall, rows), jnp.bfloat16),
        bias=pltpu.VMEM((window, rows), jnp.float32),
        query=pltpu.VMEM((rows, span), jnp.bfloat16),
        gquery=pltpu.VMEM((span, rows), jnp.bfloat16),
        scores=pltpu.VMEM((pair, window, rows), jnp.float32),
        part=pltpu.VMEM((tall, span), jnp.bfloat16),
        total=pltpu.VMEM((tall, rows), jnp.float32),
        reach=pltpu.SMEM((1,), jnp.int32),
    )

    def kernel(*refs):
        base, grad, up = refs[0:3]
        kv, tails, info, terms = refs[3:11], refs[11:15], refs[15], refs[16:18]
        out, keep, send, projected = refs[len(operands) : len(operands) + 4]
        r = dict(zip(held, refs[len(operands) + 4 :]))
        kw, vw, kt, vt = (r[n] for n in ("kw", "vw", "kt", "vt"))
        bias, query, gquery, scores = (r[n] for n in ("bias", "query", "gquery", "scores"))
        sub = lax.axis_index("sub")
        step = pl.program_id(0)

        @pl.when(step == 0)
        def _():
            owner = owner_of(info, rank)
            lifted = unfold((terms[0][...] + terms[1][...])[0:rank], owner, tenants, rank)
            r["bottle_t"][...] = lifted.astype(jnp.bfloat16)
            r["bottle"][...] = lifted.T.astype(jnp.bfloat16)
            r["total"][...] = jnp.zeros((tall, rows), jnp.float32)
            vt[HEAD:, :] = jnp.ones((TAIL, window), jnp.bfloat16)
            own, two, swap, passed = (ref[...].astype(jnp.float32) for ref in tails)
            near = jnp.where(sub == 0, swap, passed)
            far = jnp.where(sub == 0, passed, swap)
            mine = own[0:1, :]
            lowest = jnp.min(mine)
            reach = 0
            for slot, block in ((REACH, own), (2, near), (1, two), (0, far)):
                same = block.T[:, 0:1] == mine
                if slot == REACH:
                    same = same & (
                        lax.broadcasted_iota(jnp.int32, (rows, rows), 0)
                        <= lax.broadcasted_iota(jnp.int32, (rows, rows), 1)
                    )
                else:
                    reach = jnp.where(jnp.max(block[0:1, :]) == lowest, REACH - slot, reach)
                bias[slot * rows : (slot + 1) * rows, :] = jnp.where(same, 0.0, NEG)
            r["reach"][0] = reach

        def place(slot, k_ref, v_ref):
            at = slice(slot * rows, (slot + 1) * rows)
            k, v = k_ref[...], v_ref[...]
            kw[at, :] = k
            vw[at, :] = v
            kt[:, at] = k.T
            vt[0:HEAD, at] = v.T

        place(REACH, *kv[0:2])
        place(1, *kv[2:4])

        @pl.when(sub == 0)
        def _():
            place(2, *kv[4:6])
            place(0, *kv[6:8])

        @pl.when(sub != 0)
        def _():
            place(2, *kv[6:8])
            place(0, *kv[4:6])

        query[...] = (
            base[...].astype(jnp.float32) + LIFT * nn(r["bottle"][...], up[...])
        ).astype(jnp.bfloat16)
        ones = jnp.ones((TAIL, 2 * HEAD), jnp.bfloat16)

        def run(reached, numbers):
            chunks = [slice(c * rows, (c + 1) * rows) for c in range(REACH - reached, REACH + 1)]
            spans = [pl.ds(pl.multiple_of(h * HEAD, HEAD), HEAD) for h in numbers]
            peaks = []
            for i, span_i in enumerate(spans):
                q, peak = query[:, span_i], None
                for c in chunks:
                    s = nt(kw[c, :], q) + bias[c, :]
                    scores[i, c, :] = s
                    top = jnp.max(s, axis=0, keepdims=True)
                    peak = top if peak is None else jnp.maximum(peak, top)
                peaks.append(peak)
            inverses, rowdots = [], []
            for i, span_i in enumerate(spans):
                total = None
                for c in chunks:
                    w = jnp.exp2((scores[i, c, :] - peaks[i]) * (scale * LOG2E))
                    scores[i, c, :] = w
                    o = nn(vt[:, c], w.astype(jnp.bfloat16))
                    total = o if total is None else total + o
                inverse = 1.0 / total[HEAD : HEAD + 1, :]
                attn = (total[0:HEAD, :] * inverse).astype(jnp.bfloat16).T
                out[:, span_i] = attn
                product = grad[:, span_i].astype(jnp.float32) * attn.astype(jnp.float32)
                high = product.astype(jnp.bfloat16)
                low = (product - high.astype(jnp.float32)).astype(jnp.bfloat16)
                rowdots.append(nt(ones, jnp.concatenate([high, low], axis=1))[0:1, :])
                inverses.append(inverse)
            for i, span_i in enumerate(spans):
                g, moved = grad[:, span_i], None
                for c in chunks:
                    dprob = nt(vw[c, :], g)
                    ds = (scores[i, c, :] * (dprob - rowdots[i])).astype(jnp.bfloat16)
                    dq = nn(kt[:, c], ds)
                    moved = dq if moved is None else moved + dq
                gquery[span_i, :] = (moved * (inverses[i] * (LIFT * scale))).astype(jnp.bfloat16)

        for reached in range(REACH + 1):

            @pl.when(r["reach"][0] == reached)
            def _():
                @pl.loop(0, group // pair)
                def _(i):
                    run(reached, [i * pair + k for k in range(pair)])

        r["part"][...] = nt(r["bottle_t"][...], gquery[...]).astype(jnp.bfloat16)
        keep[...] = r["part"][pl.ds(pl.multiple_of(sub * half, half), half), :]
        send[...] = r["part"][pl.ds(pl.multiple_of((1 - sub) * half, half), half), :]
        r["total"][...] += nn(up[...], gquery[...])

        @pl.when(step == count - 1)
        def _():
            folded = fold(r["total"][...], owner_of(info, rank), tenants, rank)
            projected[...] = folded if before is None else folded + refs[18][...]

    return pl.pallas_call(
        kernel,
        grid=(count,),
        out_shape=[
            jax.ShapeDtypeStruct((rows, width), jnp.bfloat16),
            *halves_of(tall, count * span),
            jax.ShapeDtypeStruct((rank, rows), jnp.float32),
        ],
        in_specs=specs,
        out_specs=[wide(rows), narrow, narrow, pl.BlockSpec((rank, rows), lambda i: (0, 0))],
        scratch_shapes=list(held.values()),
        input_output_aliases={19: 0} if before is not None else {},
        compiler_params=params(VMEM_HEADS),
        cost_estimate=pl.CostEstimate(
            flops=8 * rows * window * span * count,
            bytes_accessed=6 * rows * span * count,
            transcendentals=rows * window * group * count,
        ),
        name="attention",
    )(*operands)


def small_call(kernel, name, shapes, *operands, after=(), through=(), scratch=()):
    size = sum(2 * a.size for a in operands)
    count, results = len(operands), jax.tree.leaves(shapes)
    given = (*operands, *after, *through)
    outs = len(given) + len(results)
    calls = pl.pallas_call(
        lambda *refs: kernel(
            *refs[:count], *refs[len(given) : outs], *refs[outs + len(through) :]
        ),
        out_shape=results + [jax.ShapeDtypeStruct(a.shape, a.dtype) for a in through],
        in_specs=[VM] * count + [ANY] * (len(after) + len(through)),
        out_specs=[VM] * len(results) + [ANY] * len(through),
        scratch_shapes=list(scratch),
        input_output_aliases={
            count + len(after) + i: len(results) + i for i in range(len(through))
        },
        compiler_params=params(),
        cost_estimate=pl.CostEstimate(flops=size, bytes_accessed=2 * size, transcendentals=0),
        name=name,
    )(*given)
    return calls if isinstance(shapes, list) or through else calls[0]


def grad_a_of(tenants, rank, one, other, info, x):
    g = unfold((one[...] + other[...]), owner_of(info[...], rank), tenants, rank)
    return nn(g.astype(jnp.bfloat16), x[...]).astype(jnp.bfloat16)


def grad_a_kernel(tenants, rank, one, other, info, x, out):
    out[...] = grad_a_of(tenants, rank, one, other, info, x)


def split_kernel(tenants, rank, one, other, info, x, keep, send):
    part = grad_a_of(tenants, rank, one, other, info, x)
    half = keep.shape[0]
    sub = lax.axis_index("sub")

    @pl.when(sub == 0)
    def _():
        keep[...] = part[0:half, :]
        send[...] = part[half:, :]

    @pl.when(sub != 0)
    def _():
        keep[...] = part[half:, :]
        send[...] = part[0:half, :]


def scatter_kernel(size, count, *refs):
    mine, *sends, total = refs[2 * count :]
    col = 0
    for keep, got in zip(refs[0 : 2 * count : 2], refs[1 : 2 * count : 2]):
        both = keep[...].astype(jnp.float32) + got[...].astype(jnp.float32)
        total[:, col : col + keep.shape[1]] = both.astype(jnp.bfloat16)
        col += keep.shape[1]
    me = lax.axis_index("seq")
    rows = mine.shape[0]
    for d, out in enumerate((mine, *sends)):
        at = pl.multiple_of(lax.rem(me + d, size) * rows, rows)
        out[...] = total[pl.ds(at, rows), :]


def sum_kernel(*refs):
    total = refs[0][...].astype(jnp.float32)
    for ref in refs[1:-1]:
        total = total + ref[...].astype(jnp.float32)
    refs[-1][...] = total.astype(jnp.bfloat16)


def gather_kernel(size, *refs):
    pieces, out = refs[:-1], refs[-1]
    me = lax.axis_index("seq")
    rows = pieces[0].shape[0]
    for d, piece in enumerate(pieces):
        at = pl.multiple_of(lax.rem(me + size - d, size) * rows, rows)
        out[pl.ds(at, rows), :] = piece[...]


def gather(pieces, after=()):
    size, (rows, width) = len(pieces), pieces[0].shape
    return small_call(
        functools.partial(gather_kernel, size), "gather_grads",
        jax.ShapeDtypeStruct((rows * size, width), jnp.bfloat16), *pieces, after=after,
    )


def finish_kernel(half_ref, other_ref, out):
    sub = lax.axis_index("sub")
    half = half_ref.shape[0]
    here = pl.ds(pl.multiple_of(sub * half, half), half)
    there = pl.ds(pl.multiple_of((1 - sub) * half, half), half)
    out[here, :] = half_ref[...].astype(jnp.float32)
    out[there, :] = other_ref[...].astype(jnp.float32)


def finish(half, other):
    rows, width = half.shape
    return small_call(
        finish_kernel, "finish_grads", jax.ShapeDtypeStruct((2 * rows, width), jnp.float32),
        half, other,
    )


def halves_of(rows, width):
    return [jax.ShapeDtypeStruct((rows // 2, width), jnp.bfloat16)] * 2


def scatter(*pairs, after=()):
    size = lax.axis_size("seq")
    rows, width = pairs[0][0].shape[0], sum(keep.shape[1] for keep, _ in pairs)
    shard = jax.ShapeDtypeStruct((rows // size, width), jnp.bfloat16)
    return small_call(
        functools.partial(scatter_kernel, size, len(pairs)), "scatter_grads", [shard] * size,
        *[block for pair in pairs for block in pair],
        after=after, scratch=[pltpu.VMEM((rows, width), jnp.bfloat16)],
    )


def exchange(shards):
    return [shards[0]] + [rotate_over(block, "seq", d + 1) for d, block in enumerate(shards[1:])]


def add_up(pieces, after=(), through=()):
    shape = jax.ShapeDtypeStruct(pieces[0].shape, pieces[0].dtype)
    return small_call(sum_kernel, "sum_grads", shape, *pieces, after=after, through=through)


def spread(shard):
    return [shard] + [rotate_over(shard, "seq", d) for d in range(1, lax.axis_size("seq"))]


def swap_over(block, axis):
    return lax.ppermute(block, axis, [(0, 1), (1, 0)])


def rotate_over(block, axis, d):
    size = lax.axis_size(axis)
    return lax.ppermute(block, axis, [(i, (i + d) % size) for i in range(size)])


def terms_over(block, axis):
    if lax.axis_size(axis) == 2:
        return block, swap_over(block, axis)
    return lax.psum(block, axis), jnp.zeros_like(block)


def shift_over(block, axis):
    size = lax.axis_size(axis)
    return lax.ppermute(block, axis, [(i, i + 1) for i in range(size - 1)])


def body(
    normed_inputs, base_queries, base_keys, base_values, adapter_down, adapter_up,
    position_document, document_tenant, output_gradient,
):
    rows, width = normed_inputs.shape
    tenants, _, rank = adapter_down.shape
    tall, up_width = tenants * rank, adapter_up.shape[2]
    doc = position_document.reshape(1, rows)
    adapter = jnp.transpose(adapter_down, (0, 2, 1)).reshape(tall, width)
    up = adapter_up.reshape(tall, up_width)
    key_heads = base_keys.shape[1] // HEAD
    chunks = 2 if key_heads % 2 == 0 else 1
    counts = (key_heads // chunks,) * chunks
    size = lax.axis_size("seq")
    by_hand = tall % (2 * TAIL * size) == 0

    own = pack(base_keys, base_values, doc, counts)
    two = [shift_over(block, "seq") for block in own]
    info = down_project(normed_inputs, adapter, doc, document_tenant, tenants, rank)
    swapped = [swap_over(block, "sub") for block in two]
    passed = [shift_over(relay(o, t, info), ("seq", "sub")) for o, t in zip(own, two)]
    terms = terms_over(info, "mp")
    first = (own[0], two[0], swapped[0], passed[0])

    state, pairs = None, []
    for c in range(chunks):
        out, keep, send, gdown = attention(
            c, chunks, base_queries, output_gradient, up,
            (own[c], two[c], swapped[c], passed[c]), first, info, terms, state, tenants, rank,
        )
        state = (out, gdown)
        pairs.append((keep, send))
    one, other = terms_over(gdown, "mp")
    if by_hand:
        shards_b = scatter(*[(keep, swap_over(send, "sub")) for keep, send in pairs])
        keep, send = small_call(
            functools.partial(split_kernel, tenants, rank), "split_grads", halves_of(tall, width),
            one, other, info, normed_inputs, after=shards_b[:1],
        )
        pieces_b = exchange(shards_b)
        shards_a = scatter((keep, swap_over(send, "sub")))
        pieces_a = exchange(shards_a)
        all_b = spread(add_up(pieces_b, after=shards_a[:1]))
        sum_a = add_up(pieces_a)
        half_b = gather(all_b, after=[sum_a])
        other_b = swap_over(half_b, "sub")
        half_a = gather(spread(sum_a), after=[other_b])
        grad_b = finish(half_b, other_b)
        grad_a = finish(half_a, swap_over(half_a, "sub"))
    else:
        part_a = small_call(
            functools.partial(grad_a_kernel, tenants, rank), "grad_a_part",
            jax.ShapeDtypeStruct((tall, width), jnp.bfloat16), one, other, info, normed_inputs,
        )
        grad_a = lax.psum(part_a, ("seq", "sub")).astype(jnp.float32)
        keeps = jnp.concatenate([keep for keep, _ in pairs], axis=1)
        sends = jnp.concatenate([send for _, send in pairs], axis=1)
        low = lax.axis_index("sub") == 0
        part_b = jnp.concatenate([jnp.where(low, keeps, sends), jnp.where(low, sends, keeps)])
        grad_b = lax.psum(part_b, ("seq", "sub")).astype(jnp.float32)
    grad_a = jnp.transpose(grad_a.reshape(tenants, rank, width), (0, 2, 1))
    return out, grad_a, grad_b.reshape(tenants, rank, up_width)


def solution(mesh):
    split = P(("rep", "seq", "sub"), "mp")
    in_specs = (
        split, split, split, split, P(None, "mp", None), P(None, None, "mp"),
        P(("rep", "seq", "sub")), P("rep"), split,
    )
    out_specs = (split, P("rep", "mp", None), P("rep", None, "mp"))
    return jax.shard_map(body, mesh=mesh, in_specs=in_specs, out_specs=out_specs, check_vma=False)
```

```python
import functools

import jax
import jax.numpy as jnp
from jax import lax
from jax.experimental import pallas as pl
from jax.experimental.pallas import tpu as pltpu
from jax.sharding import PartitionSpec as P

HEAD = 128
REACH = 3
NEG = -1e30
LIFT = 2.0
LOG2E = 1.4426950408889634
TAIL = 16
VMEM_BYTES = 48 * 1024 * 1024
VMEM_MOST = 60 * 1024 * 1024
VMEM_HEADS = 57 * 1024 * 1024

VM = pl.BlockSpec(memory_space=pltpu.VMEM)
SM = pl.BlockSpec(memory_space=pltpu.SMEM)
ANY = pl.BlockSpec(memory_space=pl.ANY)


def nt(a, b):
    return lax.dot_general(a, b, (((1,), (1,)), ((), ())), preferred_element_type=jnp.float32)


def nn(a, b):
    return jnp.dot(a, b, preferred_element_type=jnp.float32)


def params(limit=VMEM_BYTES):
    return pltpu.CompilerParams(vmem_limit_bytes=limit)


def fetch(pairs, sems):
    copies = [pltpu.make_async_copy(src, dst, sems.at[i]) for i, (src, dst) in enumerate(pairs)]
    for copy in copies:
        copy.start()
    return copies


def pack_kernel(keys, values, doc, out, ids, blocks, sems):
    rows, width = keys.shape
    loads = fetch(
        [
            (doc, ids),
            (keys, blocks.at[pl.ds(0, rows), pl.ds(0, width)]),
            (values, blocks.at[pl.ds(0, rows), pl.ds(width, width)]),
        ],
        sems.at[pl.ds(0, 3)],
    )
    loads[0].wait()
    blocks[rows:, :] = jnp.zeros((TAIL, 2 * width), jnp.bfloat16)
    blocks[rows:, 0:rows] = jnp.broadcast_to((ids[...] + 1).astype(jnp.float32), (TAIL, rows)).astype(
        jnp.bfloat16
    )
    loads[1].wait()
    loads[2].wait()
    for store in fetch([(blocks, out)], sems.at[pl.ds(3, 1)]):
        store.wait()


def pack(keys, values, doc):
    rows, width = keys.shape
    shape = (rows + TAIL, 2 * width)
    return pl.pallas_call(
        pack_kernel,
        out_shape=jax.ShapeDtypeStruct(shape, jnp.bfloat16),
        in_specs=[ANY] * 3,
        out_specs=ANY,
        scratch_shapes=[
            pltpu.VMEM((1, rows), jnp.int32),
            pltpu.VMEM(shape, jnp.bfloat16),
            pltpu.SemaphoreType.DMA((4,)),
        ],
        compiler_params=params(VMEM_MOST),
        cost_estimate=pl.CostEstimate(flops=0, bytes_accessed=8 * rows * width, transcendentals=0),
        name="pack_keys_values",
    )(keys, values, doc)


def relay_kernel(own, got, after, *rest):
    outs, held, sems = rest[:-3], rest[-2], rest[-1]
    sub = lax.axis_index("sub")

    def move(source):
        load = pltpu.make_async_copy(source, held, sems.at[0])
        load.start()
        load.wait()

    @pl.when(sub == 0)
    def _():
        move(own)

    @pl.when(sub != 0)
    def _():
        move(got)

    width = held.shape[1] // 2
    part = width // len(outs)
    pairs = []
    for c, out in enumerate(outs):
        for half in range(2):
            pairs.append(
                (
                    held.at[:, pl.ds(half * width + c * part, part)],
                    out.at[:, pl.ds(half * part, part)],
                )
            )
    for store in fetch(pairs, sems.at[pl.ds(1, len(pairs))]):
        store.wait()


def relay(own, got, after, chunks):
    rows, width = own.shape
    *parts, got = pl.pallas_call(
        relay_kernel,
        out_shape=[jax.ShapeDtypeStruct((rows, width // chunks), own.dtype)] * chunks
        + [jax.ShapeDtypeStruct(own.shape, own.dtype)],
        in_specs=[ANY, ANY, ANY],
        out_specs=[ANY] * (chunks + 1),
        input_output_aliases={1: chunks},
        scratch_shapes=[
            pltpu.VMEM(own.shape, own.dtype),
            pltpu.SemaphoreType.DMA((1 + 2 * chunks,)),
        ],
        compiler_params=params(),
        cost_estimate=pl.CostEstimate(flops=0, bytes_accessed=4 * own.size, transcendentals=0),
        name="relay_block",
    )(own, got, after)
    return parts, got


def selector_of(owner, tenants, rank):
    rows = owner.shape[1]
    tenant = lax.broadcasted_iota(jnp.int32, (tenants * rank, rows), 0) // rank
    return tenant == owner


def fold(full, owner, tenants, rank):
    kept = jnp.where(selector_of(owner, tenants, rank), full, 0.0)
    total = kept[0:rank]
    for t in range(1, tenants):
        total = total + kept[t * rank : (t + 1) * rank]
    return total


def unfold(compact, owner, tenants, rank):
    spread = jnp.concatenate([compact] * tenants, axis=0)
    return jnp.where(selector_of(owner, tenants, rank), spread, 0.0)


def down_kernel(tenants, rank, x_hbm, adapter_hbm, doc_hbm, tenant_of, info, x, adapter, doc, sems):
    copies = fetch([(doc_hbm, doc), (x_hbm, x), (adapter_hbm, adapter)], sems)
    copies[0].wait()
    ids = doc[...]
    found = jnp.zeros(ids.shape, jnp.int32)
    for s in range(tenant_of.shape[0]):
        found = jnp.where(ids == s, tenant_of[s], found)
    info[rank:, :] = jnp.broadcast_to(found.astype(jnp.float32), (info.shape[0] - rank, ids.shape[1]))
    copies[1].wait()
    copies[2].wait()
    info[0:rank, :] = fold(nt(x[...], adapter[...]).T, found, tenants, rank)


def down_project(x, adapter, doc, tenant_of, tenants, rank):
    rows, width = x.shape
    return pl.pallas_call(
        functools.partial(down_kernel, tenants, rank),
        out_shape=jax.ShapeDtypeStruct((rank + 8, rows), jnp.float32),
        in_specs=[ANY, ANY, ANY, SM],
        out_specs=VM,
        scratch_shapes=[
            pltpu.VMEM(x.shape, x.dtype),
            pltpu.VMEM(adapter.shape, adapter.dtype),
            pltpu.VMEM(doc.shape, doc.dtype),
            pltpu.SemaphoreType.DMA((3,)),
        ],
        compiler_params=params(VMEM_MOST),
        cost_estimate=pl.CostEstimate(
            flops=2 * rows * width * tenants * rank,
            bytes_accessed=2 * width * (rows + tenants * rank),
            transcendentals=0,
        ),
        name="down_project",
    )(x, adapter, doc, tenant_of)


def owner_of(info, rank):
    return info[rank : rank + 1, :].astype(jnp.int32)


def attention(chunk, chunks, base, grad, up, blocks, with_ids, info, terms, before, tenants, rank):
    rows, width = base.shape
    count = blocks[3].shape[1] // (2 * HEAD)
    window = (REACH + 1) * rows
    tall = tenants * rank
    half = tall // 2
    group = width // HEAD // (count * chunks)
    span = group * HEAD
    pair = min(4, group)
    scale = HEAD**-0.5
    offset = chunk * count
    wide = lambda r: pl.BlockSpec((r, span), lambda i: (0, i + offset))
    narrow = pl.BlockSpec((half, span), lambda i: (0, i))
    column = lambda at: pl.BlockSpec((rows, HEAD), lambda i: (0, i + at))
    ids = pl.BlockSpec((TAIL, rows), lambda i: (rows // TAIL, 0))
    same = lambda a: pl.BlockSpec(a.shape, lambda i: (0, 0))
    operands, specs = [base, grad, up], [wide(rows), wide(rows), wide(tall)]
    for block in blocks:
        operands += [block, block]
        skip = 0 if block is blocks[3] else offset
        specs += [column(skip), column(skip + block.shape[1] // (2 * HEAD))]
    operands += [*with_ids, info, *terms]
    specs += [ids] * 4 + [same(info)] * 3
    if before is not None:
        operands += [before[1], before[0]]
        specs += [same(before[1]), ANY]
    held = dict(
        kw=pltpu.VMEM((window, HEAD), jnp.bfloat16),
        vw=pltpu.VMEM((window, HEAD), jnp.bfloat16),
        kt=pltpu.VMEM((HEAD, window), jnp.bfloat16),
        vt=pltpu.VMEM((HEAD + TAIL, window), jnp.bfloat16),
        bottle=pltpu.VMEM((rows, tall), jnp.bfloat16),
        bottle_t=pltpu.VMEM((tall, rows), jnp.bfloat16),
        bias=pltpu.VMEM((window, rows), jnp.float32),
        query=pltpu.VMEM((span, rows), jnp.bfloat16),
        gt=pltpu.VMEM((span, rows), jnp.bfloat16),
        gquery=pltpu.VMEM((span, rows), jnp.bfloat16),
        scores=pltpu.VMEM((pair, window, rows), jnp.float32),
        part=pltpu.VMEM((tall, span), jnp.bfloat16),
        total=pltpu.VMEM((tall, rows), jnp.float32),
        reach=pltpu.SMEM((1,), jnp.int32),
    )

    def kernel(*refs):
        base, grad, up = refs[0:3]
        kv, tails, info, terms = refs[3:11], refs[11:15], refs[15], refs[16:18]
        out, keep, send, projected = refs[len(operands) : len(operands) + 4]
        r = dict(zip(held, refs[len(operands) + 4 :]))
        kw, vw, kt, vt = (r[n] for n in ("kw", "vw", "kt", "vt"))
        bias, query, gt, gquery, scores = (
            r[n] for n in ("bias", "query", "gt", "gquery", "scores")
        )
        sub = lax.axis_index("sub")
        step = pl.program_id(0)

        @pl.when(step == 0)
        def _():
            owner = owner_of(info, rank)
            lifted = unfold((terms[0][...] + terms[1][...])[0:rank], owner, tenants, rank)
            r["bottle_t"][...] = lifted.astype(jnp.bfloat16)
            r["bottle"][...] = lifted.T.astype(jnp.bfloat16)
            r["total"][...] = jnp.zeros((tall, rows), jnp.float32)
            vt[HEAD:, :] = jnp.ones((TAIL, window), jnp.bfloat16)
            own, two, swap, passed = (ref[...].astype(jnp.float32) for ref in tails)
            near = jnp.where(sub == 0, swap, passed)
            far = jnp.where(sub == 0, passed, swap)
            mine = own[0:1, :]
            lowest = jnp.min(mine)
            reach = 0
            for slot, block in ((REACH, own), (2, near), (1, two), (0, far)):
                same = block.T[:, 0:1] == mine
                if slot == REACH:
                    same = same & (
                        lax.broadcasted_iota(jnp.int32, (rows, rows), 0)
                        <= lax.broadcasted_iota(jnp.int32, (rows, rows), 1)
                    )
                else:
                    reach = jnp.where(jnp.max(block[0:1, :]) == lowest, REACH - slot, reach)
                bias[slot * rows : (slot + 1) * rows, :] = jnp.where(same, 0.0, NEG)
            r["reach"][0] = reach

        def place(slot, k_ref, v_ref):
            at = slice(slot * rows, (slot + 1) * rows)
            k, v = k_ref[...], v_ref[...]
            kw[at, :] = k
            vw[at, :] = v
            kt[:, at] = k.T
            vt[0:HEAD, at] = v.T

        place(REACH, *kv[0:2])
        place(1, *kv[2:4])

        @pl.when(sub == 0)
        def _():
            place(2, *kv[4:6])
            place(0, *kv[6:8])

        @pl.when(sub != 0)
        def _():
            place(2, *kv[6:8])
            place(0, *kv[4:6])

        lift = LIFT * nn(r["bottle"][...], up[...])
        query[...] = (base[...].astype(jnp.float32) + lift).astype(jnp.bfloat16).T
        gt[...] = grad[...].T

        def run(reached, numbers):
            chunks = [slice(c * rows, (c + 1) * rows) for c in range(REACH - reached, REACH + 1)]
            spans = [pl.ds(pl.multiple_of(h * HEAD, HEAD), HEAD) for h in numbers]
            peaks = []
            for i, span_i in enumerate(spans):
                q, peak = query[span_i, :], None
                for c in chunks:
                    s = nn(kw[c, :], q) + bias[c, :]
                    scores[i, c, :] = s
                    top = jnp.max(s, axis=0, keepdims=True)
                    peak = top if peak is None else jnp.maximum(peak, top)
                peaks.append(peak)
            inverses, rowdots = [], []
            for i, span_i in enumerate(spans):
                total = None
                for c in chunks:
                    w = jnp.exp2((scores[i, c, :] - peaks[i]) * (scale * LOG2E))
                    scores[i, c, :] = w
                    o = nn(vt[:, c], w.astype(jnp.bfloat16))
                    total = o if total is None else total + o
                inverse = 1.0 / total[HEAD : HEAD + 1, :]
                attn = (total[0:HEAD, :] * inverse).astype(jnp.bfloat16)
                out[:, span_i] = attn.T
                product = gt[span_i, :].astype(jnp.float32) * attn.astype(jnp.float32)
                rowdots.append(jnp.sum(product, axis=0, keepdims=True))
                inverses.append(inverse)
            for i, span_i in enumerate(spans):
                g, moved = gt[span_i, :], None
                for c in chunks:
                    dprob = nn(vw[c, :], g)
                    ds = (scores[i, c, :] * (dprob - rowdots[i])).astype(jnp.bfloat16)
                    dq = nn(kt[:, c], ds)
                    moved = dq if moved is None else moved + dq
                gquery[span_i, :] = (moved * (inverses[i] * (LIFT * scale))).astype(jnp.bfloat16)

        for reached in range(REACH + 1):

            @pl.when(r["reach"][0] == reached)
            def _():
                @pl.loop(0, group // pair)
                def _(i):
                    run(reached, [i * pair + k for k in range(pair)])

        r["part"][...] = nt(r["bottle_t"][...], gquery[...]).astype(jnp.bfloat16)
        keep[...] = r["part"][pl.ds(pl.multiple_of(sub * half, half), half), :]
        send[...] = r["part"][pl.ds(pl.multiple_of((1 - sub) * half, half), half), :]
        r["total"][...] += nn(up[...], gquery[...])

        @pl.when(step == count - 1)
        def _():
            folded = fold(r["total"][...], owner_of(info, rank), tenants, rank)
            projected[...] = folded if before is None else folded + refs[18][...]

    return pl.pallas_call(
        kernel,
        grid=(count,),
        out_shape=[
            jax.ShapeDtypeStruct((rows, width), jnp.bfloat16),
            *halves_of(tall, count * span),
            jax.ShapeDtypeStruct((rank, rows), jnp.float32),
        ],
        in_specs=specs,
        out_specs=[wide(rows), narrow, narrow, pl.BlockSpec((rank, rows), lambda i: (0, 0))],
        scratch_shapes=list(held.values()),
        input_output_aliases={19: 0} if before is not None else {},
        compiler_params=params(VMEM_HEADS),
        cost_estimate=pl.CostEstimate(
            flops=8 * rows * window * span * count,
            bytes_accessed=6 * rows * span * count,
            transcendentals=rows * window * group * count,
        ),
        name="attention",
    )(*operands)


def small_call(kernel, name, shapes, *operands, after=(), through=(), scratch=()):
    size = sum(2 * a.size for a in operands)
    count, results = len(operands), jax.tree.leaves(shapes)
    given = (*operands, *after, *through)
    outs = len(given) + len(results)
    calls = pl.pallas_call(
        lambda *refs: kernel(
            *refs[:count], *refs[len(given) : outs], *refs[outs + len(through) :]
        ),
        out_shape=results + [jax.ShapeDtypeStruct(a.shape, a.dtype) for a in through],
        in_specs=[VM] * count + [ANY] * (len(after) + len(through)),
        out_specs=[VM] * len(results) + [ANY] * len(through),
        scratch_shapes=list(scratch),
        input_output_aliases={
            count + len(after) + i: len(results) + i for i in range(len(through))
        },
        compiler_params=params(),
        cost_estimate=pl.CostEstimate(flops=size, bytes_accessed=2 * size, transcendentals=0),
        name=name,
    )(*given)
    return calls if isinstance(shapes, list) or through else calls[0]


def grad_a_of(tenants, rank, one, other, info, x):
    g = unfold((one[...] + other[...]), owner_of(info[...], rank), tenants, rank)
    return nn(g.astype(jnp.bfloat16), x[...]).astype(jnp.bfloat16)


def grad_a_kernel(tenants, rank, one, other, info, x, out):
    out[...] = grad_a_of(tenants, rank, one, other, info, x)


def split_kernel(tenants, rank, one, other, info, x, keep, send):
    part = grad_a_of(tenants, rank, one, other, info, x)
    half = keep.shape[0]
    sub = lax.axis_index("sub")

    @pl.when(sub == 0)
    def _():
        keep[...] = part[0:half, :]
        send[...] = part[half:, :]

    @pl.when(sub != 0)
    def _():
        keep[...] = part[half:, :]
        send[...] = part[0:half, :]


def scatter_kernel(size, count, *refs):
    mine, *sends, total = refs[2 * count :]
    col = 0
    for keep, got in zip(refs[0 : 2 * count : 2], refs[1 : 2 * count : 2]):
        both = keep[...].astype(jnp.float32) + got[...].astype(jnp.float32)
        total[:, col : col + keep.shape[1]] = both.astype(jnp.bfloat16)
        col += keep.shape[1]
    me = lax.axis_index("seq")
    rows = mine.shape[0]
    for d, out in enumerate((mine, *sends)):
        at = pl.multiple_of(lax.rem(me + d, size) * rows, rows)
        out[...] = total[pl.ds(at, rows), :]


def sum_kernel(*refs):
    total = refs[0][...].astype(jnp.float32)
    for ref in refs[1:-1]:
        total = total + ref[...].astype(jnp.float32)
    refs[-1][...] = total.astype(jnp.bfloat16)


def gather_kernel(size, *refs):
    pieces, out = refs[:-1], refs[-1]
    me = lax.axis_index("seq")
    rows = pieces[0].shape[0]
    for d, piece in enumerate(pieces):
        at = pl.multiple_of(lax.rem(me + size - d, size) * rows, rows)
        out[pl.ds(at, rows), :] = piece[...]


def gather(pieces, after=()):
    size, (rows, width) = len(pieces), pieces[0].shape
    return small_call(
        functools.partial(gather_kernel, size), "gather_grads",
        jax.ShapeDtypeStruct((rows * size, width), jnp.bfloat16), *pieces, after=after,
    )


def finish_kernel(count, *refs):
    grad_b, grad_a = refs[2 * count :]
    sub = lax.axis_index("sub")
    half, wide = refs[0].shape[0], grad_b.shape[1]
    here = pl.ds(pl.multiple_of(sub * half, half), half)
    there = pl.ds(pl.multiple_of((1 - sub) * half, half), half)
    for at, group in ((here, refs[0 : 2 * count : 2]), (there, refs[1 : 2 * count : 2])):
        col = 0
        for ref in group:
            width = ref.shape[1]
            first = min(width, wide - col)
            grad_b[at, col : col + first] = ref[:, 0:first].astype(jnp.float32)
            if first < width:
                grad_a[at, :] = ref[:, first:].astype(jnp.float32)
            col += width


def finish(pairs, wide):
    rows, width = pairs[0][0].shape[0] * 2, sum(half.shape[1] for half, _ in pairs)
    return small_call(
        functools.partial(finish_kernel, len(pairs)), "finish_grads",
        [
            jax.ShapeDtypeStruct((rows, wide), jnp.float32),
            jax.ShapeDtypeStruct((rows, width - wide), jnp.float32),
        ],
        *[block for pair in pairs for block in pair],
    )


def halves_of(rows, width):
    return [jax.ShapeDtypeStruct((rows // 2, width), jnp.bfloat16)] * 2


def scatter(*pairs, after=()):
    size = lax.axis_size("seq")
    rows, width = pairs[0][0].shape[0], sum(keep.shape[1] for keep, _ in pairs)
    shard = jax.ShapeDtypeStruct((rows // size, width), jnp.bfloat16)
    return small_call(
        functools.partial(scatter_kernel, size, len(pairs)), "scatter_grads", [shard] * size,
        *[block for pair in pairs for block in pair],
        after=after, scratch=[pltpu.VMEM((rows, width), jnp.bfloat16)],
    )


def exchange(shards):
    return [shards[0]] + [rotate_over(block, "seq", d + 1) for d, block in enumerate(shards[1:])]


def add_up(pieces, after=(), through=()):
    shape = jax.ShapeDtypeStruct(pieces[0].shape, pieces[0].dtype)
    return small_call(sum_kernel, "sum_grads", shape, *pieces, after=after, through=through)


def spread(shard):
    return [shard] + [rotate_over(shard, "seq", d) for d in range(1, lax.axis_size("seq"))]


def swap_over(block, axis):
    return lax.ppermute(block, axis, [(0, 1), (1, 0)])


def rotate_over(block, axis, d):
    size = lax.axis_size(axis)
    return lax.ppermute(block, axis, [(i, (i + d) % size) for i in range(size)])


def terms_over(block, axis):
    if lax.axis_size(axis) == 2:
        return block, swap_over(block, axis)
    return lax.psum(block, axis), jnp.zeros_like(block)


def shift_over(block, axis):
    size = lax.axis_size(axis)
    return lax.ppermute(block, axis, [(i, i + 1) for i in range(size - 1)])


def body(
    normed_inputs, base_queries, base_keys, base_values, adapter_down, adapter_up,
    position_document, document_tenant, output_gradient,
):
    rows, width = normed_inputs.shape
    tenants, _, rank = adapter_down.shape
    tall, up_width = tenants * rank, adapter_up.shape[2]
    doc = position_document.reshape(1, rows)
    adapter = jnp.transpose(adapter_down, (0, 2, 1)).reshape(tall, width)
    up = adapter_up.reshape(tall, up_width)
    key_heads = base_keys.shape[1] // HEAD
    chunks = 2 if key_heads % 2 == 0 else 1
    size = lax.axis_size("seq")
    by_hand = chunks == 2 and tall % (2 * TAIL * size) == 0

    own = pack(base_keys, base_values, doc)
    two = shift_over(own, "seq")
    info = down_project(normed_inputs, adapter, doc, document_tenant, tenants, rank)
    terms = terms_over(info, "mp")
    parts, two = relay(own, two, terms[1], chunks)
    passed = [shift_over(part, ("seq", "sub")) for part in parts]
    swapped = swap_over(two, "sub")
    with_ids = (own, two, swapped, passed[0])

    state, pairs = None, []
    for c in range(chunks):
        out, keep, send, gdown = attention(
            c, chunks, base_queries, output_gradient, up, (own, two, swapped, passed[c]),
            with_ids, info, terms, state, tenants, rank,
        )
        state = (out, gdown)
        pairs.append((keep, send))
    if by_hand:
        (keep, send), (keep_late, send_late) = pairs
        one, other = terms_over(gdown, "mp")
        pieces = exchange(scatter((keep, swap_over(send, "sub")), after=[keep_late]))
        early = add_up(pieces)
        keep_a, send_a = small_call(
            functools.partial(split_kernel, tenants, rank), "split_grads", halves_of(tall, width),
            one, other, info, normed_inputs, after=pieces[1:2],
        )
        shards = scatter(
            (keep_late, swap_over(send_late, "sub")), (keep_a, swap_over(send_a, "sub")), after=[early]
        )
        late = add_up(exchange(shards))
        half_early = gather(spread(early), after=[late])
        other_early = swap_over(half_early, "sub")
        half_late = gather(spread(late), after=[other_early])
        grad_b, grad_a = finish(
            [(half_early, other_early), (half_late, swap_over(half_late, "sub"))], up_width
        )
    else:
        one, other = terms_over(gdown, "mp")
        part_a = small_call(
            functools.partial(grad_a_kernel, tenants, rank), "grad_a_part",
            jax.ShapeDtypeStruct((tall, width), jnp.bfloat16), one, other, info, normed_inputs,
        )
        grad_a = lax.psum(part_a, ("seq", "sub")).astype(jnp.float32)
        keeps = jnp.concatenate([keep for keep, _ in pairs], axis=1)
        sends = jnp.concatenate([send for _, send in pairs], axis=1)
        low = lax.axis_index("sub") == 0
        part_b = jnp.concatenate([jnp.where(low, keeps, sends), jnp.where(low, sends, keeps)])
        grad_b = lax.psum(part_b, ("seq", "sub")).astype(jnp.float32)
    grad_a = jnp.transpose(grad_a.reshape(tenants, rank, width), (0, 2, 1))
    return out, grad_a, grad_b.reshape(tenants, rank, up_width)


def solution(mesh):
    split = P(("rep", "seq", "sub"), "mp")
    in_specs = (
        split, split, split, split, P(None, "mp", None), P(None, None, "mp"),
        P(("rep", "seq", "sub")), P("rep"), split,
    )
    out_specs = (split, P("rep", "mp", None), P("rep", None, "mp"))
    return jax.shard_map(body, mesh=mesh, in_specs=in_specs, out_specs=out_specs, check_vma=False)
```

```python
import functools

import jax
import jax.numpy as jnp
from jax import lax
from jax.experimental import pallas as pl
from jax.experimental.pallas import tpu as pltpu
from jax.sharding import PartitionSpec as P

HEAD = 128
REACH = 3
NEG = -1e30
LIFT = 2.0
LOG2E = 1.4426950408889634
TAIL = 16
VMEM_BYTES = 48 * 1024 * 1024
VMEM_MOST = 60 * 1024 * 1024
VMEM_HEADS = 57 * 1024 * 1024

VM = pl.BlockSpec(memory_space=pltpu.VMEM)
SM = pl.BlockSpec(memory_space=pltpu.SMEM)
ANY = pl.BlockSpec(memory_space=pl.ANY)


def nt(a, b):
    return lax.dot_general(a, b, (((1,), (1,)), ((), ())), preferred_element_type=jnp.float32)


def nn(a, b):
    return jnp.dot(a, b, preferred_element_type=jnp.float32)


def params(limit=VMEM_BYTES):
    return pltpu.CompilerParams(vmem_limit_bytes=limit)


def fetch(pairs, sems):
    copies = [pltpu.make_async_copy(src, dst, sems.at[i]) for i, (src, dst) in enumerate(pairs)]
    for copy in copies:
        copy.start()
    return copies


def pack_kernel(keys, values, doc, *rest):
    outs, (ids, blocks, sems) = rest[:-3], rest[-3:]
    rows, width = keys.shape
    part = width // len(outs)
    pairs = [(doc, ids)]
    for c in range(len(outs)):
        cols = pl.ds(c * part, part)
        pairs.append((keys.at[:, cols], blocks.at[c, pl.ds(0, rows), pl.ds(0, part)]))
        pairs.append((values.at[:, cols], blocks.at[c, pl.ds(0, rows), pl.ds(part, part)]))
    loads = fetch(pairs, sems.at[pl.ds(0, len(pairs))])
    loads[0].wait()
    tail = jnp.broadcast_to((ids[...] + 1).astype(jnp.float32), (TAIL, rows)).astype(jnp.bfloat16)
    stores = []
    for c, out in enumerate(outs):
        blocks[c, rows:, :] = jnp.zeros((TAIL, 2 * part), jnp.bfloat16)
        blocks[c, rows:, 0:rows] = tail
        loads[1 + 2 * c].wait()
        loads[2 + 2 * c].wait()
        stores += fetch([(blocks.at[c], out)], sems.at[pl.ds(len(pairs) + c, 1)])
    for store in stores:
        store.wait()


def pack(keys, values, doc, chunks):
    rows, width = keys.shape
    shape = (rows + TAIL, 2 * width // chunks)
    return pl.pallas_call(
        pack_kernel,
        out_shape=[jax.ShapeDtypeStruct(shape, jnp.bfloat16)] * chunks,
        in_specs=[ANY] * 3,
        out_specs=[ANY] * chunks,
        scratch_shapes=[
            pltpu.VMEM((1, rows), jnp.int32),
            pltpu.VMEM((chunks, *shape), jnp.bfloat16),
            pltpu.SemaphoreType.DMA((1 + 3 * chunks,)),
        ],
        compiler_params=params(VMEM_MOST),
        cost_estimate=pl.CostEstimate(flops=0, bytes_accessed=8 * rows * width, transcendentals=0),
        name="pack_keys_values",
    )(keys, values, doc)


def relay_kernel(own, got, after, out, got_out, held, sems):
    sub = lax.axis_index("sub")

    def move(source):
        load = pltpu.make_async_copy(source, held, sems.at[0])
        load.start()
        load.wait()

    @pl.when(sub == 0)
    def _():
        move(own)

    @pl.when(sub != 0)
    def _():
        move(got)

    store = pltpu.make_async_copy(held, out, sems.at[1])
    store.start()
    store.wait()


def relay(own, got, after):
    shape = jax.ShapeDtypeStruct(own.shape, own.dtype)
    return pl.pallas_call(
        relay_kernel,
        out_shape=[shape, shape],
        in_specs=[ANY, ANY, ANY],
        out_specs=[ANY, ANY],
        input_output_aliases={1: 1},
        scratch_shapes=[pltpu.VMEM(own.shape, own.dtype), pltpu.SemaphoreType.DMA((2,))],
        compiler_params=params(),
        cost_estimate=pl.CostEstimate(flops=0, bytes_accessed=4 * own.size, transcendentals=0),
        name="relay_block",
    )(own, got, after)


def selector_of(owner, tenants, rank):
    rows = owner.shape[1]
    tenant = lax.broadcasted_iota(jnp.int32, (tenants * rank, rows), 0) // rank
    return tenant == owner


def fold(full, owner, tenants, rank):
    kept = jnp.where(selector_of(owner, tenants, rank), full, 0.0)
    total = kept[0:rank]
    for t in range(1, tenants):
        total = total + kept[t * rank : (t + 1) * rank]
    return total


def unfold(compact, owner, tenants, rank):
    spread = jnp.concatenate([compact] * tenants, axis=0)
    return jnp.where(selector_of(owner, tenants, rank), spread, 0.0)


def down_kernel(tenants, rank, x_hbm, adapter_hbm, doc_hbm, tenant_of, info, x, adapter, doc, sems):
    copies = fetch([(doc_hbm, doc), (x_hbm, x), (adapter_hbm, adapter)], sems)
    copies[0].wait()
    ids = doc[...]
    found = jnp.zeros(ids.shape, jnp.int32)
    for s in range(tenant_of.shape[0]):
        found = jnp.where(ids == s, tenant_of[s], found)
    info[rank:, :] = jnp.broadcast_to(found.astype(jnp.float32), (info.shape[0] - rank, ids.shape[1]))
    copies[1].wait()
    copies[2].wait()
    info[0:rank, :] = fold(nt(x[...], adapter[...]).T, found, tenants, rank)


def down_project(x, adapter, doc, tenant_of, tenants, rank):
    rows, width = x.shape
    return pl.pallas_call(
        functools.partial(down_kernel, tenants, rank),
        out_shape=jax.ShapeDtypeStruct((rank + 8, rows), jnp.float32),
        in_specs=[ANY, ANY, ANY, SM],
        out_specs=VM,
        scratch_shapes=[
            pltpu.VMEM(x.shape, x.dtype),
            pltpu.VMEM(adapter.shape, adapter.dtype),
            pltpu.VMEM(doc.shape, doc.dtype),
            pltpu.SemaphoreType.DMA((3,)),
        ],
        compiler_params=params(VMEM_MOST),
        cost_estimate=pl.CostEstimate(
            flops=2 * rows * width * tenants * rank,
            bytes_accessed=2 * width * (rows + tenants * rank),
            transcendentals=0,
        ),
        name="down_project",
    )(x, adapter, doc, tenant_of)


def owner_of(info, rank):
    return info[rank : rank + 1, :].astype(jnp.int32)


def turn(x, eye):
    size = x.shape[1]
    return nt(eye[0:size, 0:size], x).astype(jnp.bfloat16)


def attention(
    head, at, count, group, base, grad, up, blocks, with_ids, info, terms, before, tenants, rank
):
    rows, width = base.shape
    window = (REACH + 1) * rows
    tall = tenants * rank
    half = tall // 2
    span = group * HEAD
    pair = min(4, group)
    scale = HEAD**-0.5
    wide = lambda r: pl.BlockSpec((r, span), lambda i: (0, i + head))
    narrow = pl.BlockSpec((half, span), lambda i: (0, i))
    keys = pl.BlockSpec((rows, HEAD), lambda i: (0, i + at))
    skip = blocks[0].shape[1] // (2 * HEAD)
    values = pl.BlockSpec((rows, HEAD), lambda i: (0, i + at + skip))
    ids = pl.BlockSpec((TAIL, rows), lambda i: (rows // TAIL, 0))
    same = lambda a: pl.BlockSpec(a.shape, lambda i: (0, 0))
    operands, specs = [base, grad, up], [wide(rows), wide(rows), wide(tall)]
    for block in blocks:
        operands += [block, block]
        specs += [keys, values]
    operands += [*with_ids, info, *terms]
    specs += [ids] * 4 + [same(info)] * 3
    if before is not None:
        operands += [before[1], before[0]]
        specs += [same(before[1]), ANY]
    held = dict(
        kw=pltpu.VMEM((window, HEAD), jnp.bfloat16),
        vw=pltpu.VMEM((window, HEAD), jnp.bfloat16),
        kt=pltpu.VMEM((HEAD, window), jnp.bfloat16),
        vt=pltpu.VMEM((HEAD + TAIL, window), jnp.bfloat16),
        eye=pltpu.VMEM((rows, rows), jnp.bfloat16),
        bottle=pltpu.VMEM((rows, tall), jnp.bfloat16),
        bottle_t=pltpu.VMEM((tall, rows), jnp.bfloat16),
        bias=pltpu.VMEM((window, rows), jnp.float32),
        query=pltpu.VMEM((rows, span), jnp.bfloat16),
        gt=pltpu.VMEM((span, rows), jnp.bfloat16),
        gquery=pltpu.VMEM((span, rows), jnp.bfloat16),
        scores=pltpu.VMEM((pair, window, rows), jnp.float32),
        rounded=pltpu.VMEM((pair, window, rows), jnp.bfloat16),
        part=pltpu.VMEM((tall, span), jnp.bfloat16),
        total=pltpu.VMEM((tall, rows), jnp.float32),
        reach=pltpu.SMEM((1,), jnp.int32),
    )

    def kernel(*refs):
        base, grad, up = refs[0:3]
        kv, tails, info, terms = refs[3:11], refs[11:15], refs[15], refs[16:18]
        out, keep, send, projected = refs[len(operands) : len(operands) + 4]
        r = dict(zip(held, refs[len(operands) + 4 :]))
        kw, vw, kt, vt = (r[n] for n in ("kw", "vw", "kt", "vt"))
        bias, query, gt, gquery, scores, rounded = (
            r[n] for n in ("bias", "query", "gt", "gquery", "scores", "rounded")
        )
        sub = lax.axis_index("sub")
        step = pl.program_id(0)

        @pl.when(step == 0)
        def _():
            at = lax.broadcasted_iota(jnp.int32, (rows, rows), 0)
            diagonal = at == lax.broadcasted_iota(jnp.int32, (rows, rows), 1)
            r["eye"][...] = jnp.where(diagonal, 1.0, 0.0).astype(jnp.bfloat16)
            owner = owner_of(info, rank)
            lifted = unfold((terms[0][...] + terms[1][...])[0:rank], owner, tenants, rank)
            r["bottle_t"][...] = lifted.astype(jnp.bfloat16)
            r["bottle"][...] = lifted.T.astype(jnp.bfloat16)
            r["total"][...] = jnp.zeros((tall, rows), jnp.float32)
            vt[HEAD:, :] = jnp.ones((TAIL, window), jnp.bfloat16)
            own, two, swap, passed = (ref[...].astype(jnp.float32) for ref in tails)
            near = jnp.where(sub == 0, swap, passed)
            far = jnp.where(sub == 0, passed, swap)
            mine = own[0:1, :]
            lowest = jnp.min(mine)
            reach = 0
            for slot, block in ((REACH, own), (2, near), (1, two), (0, far)):
                same = block.T[:, 0:1] == mine
                if slot == REACH:
                    same = same & (
                        lax.broadcasted_iota(jnp.int32, (rows, rows), 0)
                        <= lax.broadcasted_iota(jnp.int32, (rows, rows), 1)
                    )
                else:
                    reach = jnp.where(jnp.max(block[0:1, :]) == lowest, REACH - slot, reach)
                bias[slot * rows : (slot + 1) * rows, :] = jnp.where(same, 0.0, NEG)
            r["reach"][0] = reach

        def place(slot, k_ref, v_ref):
            at = slice(slot * rows, (slot + 1) * rows)
            k, v = k_ref[...], v_ref[...]
            kw[at, :] = k
            vw[at, :] = v
            kt[:, at] = turn(k, r["eye"])
            vt[0:HEAD, at] = turn(v, r["eye"])

        place(REACH, *kv[0:2])
        place(1, *kv[2:4])

        @pl.when(sub == 0)
        def _():
            place(2, *kv[4:6])
            place(0, *kv[6:8])

        @pl.when(sub != 0)
        def _():
            place(2, *kv[6:8])
            place(0, *kv[4:6])

        lift = LIFT * nn(r["bottle"][...], up[...])
        query[...] = (base[...].astype(jnp.float32) + lift).astype(jnp.bfloat16)

        def run(reached, numbers):
            low = (REACH - reached) * rows
            chunks = [slice(at, at + rows) for at in range(low, window, rows)]
            spans = [pl.ds(pl.multiple_of(h * HEAD, HEAD), HEAD) for h in numbers]
            peaks = []
            for i, span_i in enumerate(spans):
                s = nt(kw[low:, :], query[:, span_i]) + bias[low:, :]
                scores[i, low:, :] = s
                peaks.append(jnp.max(s, axis=0, keepdims=True))
                gt[span_i, :] = turn(grad[:, span_i], r["eye"])
            inverses, rowdots = [], []
            for i, span_i in enumerate(spans):
                for c in chunks:
                    w = jnp.exp2((scores[i, c, :] - peaks[i]) * (scale * LOG2E))
                    scores[i, c, :] = w
                    rounded[i, c, :] = w.astype(jnp.bfloat16)
                total = nn(vt[:, low:], rounded[i, low:, :])
                inverse = 1.0 / total[HEAD : HEAD + 1, :]
                attn = (total[0:HEAD, :] * inverse).astype(jnp.bfloat16)
                out[:, span_i] = turn(attn, r["eye"])
                product = gt[span_i, :].astype(jnp.float32) * attn.astype(jnp.float32)
                rowdots.append(jnp.sum(product, axis=0, keepdims=True))
                inverses.append(inverse)
            for i, span_i in enumerate(spans):
                dprob = nn(vw[low:, :], gt[span_i, :])
                ds = (scores[i, low:, :] * (dprob - rowdots[i])).astype(jnp.bfloat16)
                moved = nn(kt[:, low:], ds)
                gquery[span_i, :] = (moved * (inverses[i] * (LIFT * scale))).astype(jnp.bfloat16)

        for reached in range(REACH + 1):

            @pl.when(r["reach"][0] == reached)
            def _():
                @pl.loop(0, group // pair)
                def _(i):
                    run(reached, [i * pair + k for k in range(pair)])

        r["part"][...] = nt(r["bottle_t"][...], gquery[...]).astype(jnp.bfloat16)
        keep[...] = r["part"][pl.ds(pl.multiple_of(sub * half, half), half), :]
        send[...] = r["part"][pl.ds(pl.multiple_of((1 - sub) * half, half), half), :]
        r["total"][...] += nn(up[...], gquery[...])

        @pl.when(step == count - 1)
        def _():
            folded = fold(r["total"][...], owner_of(info, rank), tenants, rank)
            projected[...] = folded if before is None else folded + refs[18][...]

    return pl.pallas_call(
        kernel,
        grid=(count,),
        out_shape=[
            jax.ShapeDtypeStruct((rows, width), jnp.bfloat16),
            *halves_of(tall, count * span),
            jax.ShapeDtypeStruct((rank, rows), jnp.float32),
        ],
        in_specs=specs,
        out_specs=[wide(rows), narrow, narrow, pl.BlockSpec((rank, rows), lambda i: (0, 0))],
        scratch_shapes=list(held.values()),
        input_output_aliases={19: 0} if before is not None else {},
        compiler_params=params(VMEM_HEADS),
        cost_estimate=pl.CostEstimate(
            flops=8 * rows * window * span * count,
            bytes_accessed=6 * rows * span * count,
            transcendentals=rows * window * group * count,
        ),
        name="attention",
    )(*operands)


def small_call(kernel, name, shapes, *operands, after=(), through=(), scratch=()):
    size = sum(2 * a.size for a in operands)
    count, results = len(operands), jax.tree.leaves(shapes)
    given = (*operands, *after, *through)
    outs = len(given) + len(results)
    calls = pl.pallas_call(
        lambda *refs: kernel(
            *refs[:count], *refs[len(given) : outs], *refs[outs + len(through) :]
        ),
        out_shape=results + [jax.ShapeDtypeStruct(a.shape, a.dtype) for a in through],
        in_specs=[VM] * count + [ANY] * (len(after) + len(through)),
        out_specs=[VM] * len(results) + [ANY] * len(through),
        scratch_shapes=list(scratch),
        input_output_aliases={
            count + len(after) + i: len(results) + i for i in range(len(through))
        },
        compiler_params=params(),
        cost_estimate=pl.CostEstimate(flops=size, bytes_accessed=2 * size, transcendentals=0),
        name=name,
    )(*given)
    return calls if isinstance(shapes, list) or through else calls[0]


def grad_a_of(tenants, rank, one, other, info, x):
    g = unfold((one[...] + other[...]), owner_of(info[...], rank), tenants, rank)
    return nn(g.astype(jnp.bfloat16), x[...]).astype(jnp.bfloat16)


def grad_a_kernel(tenants, rank, one, other, info, x, out):
    out[...] = grad_a_of(tenants, rank, one, other, info, x)


def split_kernel(tenants, rank, one, other, info, x, keep, send):
    part = grad_a_of(tenants, rank, one, other, info, x)
    half = keep.shape[0]
    sub = lax.axis_index("sub")

    @pl.when(sub == 0)
    def _():
        keep[...] = part[0:half, :]
        send[...] = part[half:, :]

    @pl.when(sub != 0)
    def _():
        keep[...] = part[half:, :]
        send[...] = part[0:half, :]


def scatter_kernel(size, count, *refs):
    mine, *sends, total = refs[2 * count :]
    col = 0
    for keep, got in zip(refs[0 : 2 * count : 2], refs[1 : 2 * count : 2]):
        both = keep[...].astype(jnp.float32) + got[...].astype(jnp.float32)
        total[:, col : col + keep.shape[1]] = both.astype(jnp.bfloat16)
        col += keep.shape[1]
    me = lax.axis_index("seq")
    rows = mine.shape[0]
    for d, out in enumerate((mine, *sends)):
        at = pl.multiple_of(lax.rem(me + d, size) * rows, rows)
        out[...] = total[pl.ds(at, rows), :]


def sum_kernel(*refs):
    total = refs[0][...].astype(jnp.float32)
    for ref in refs[1:-1]:
        total = total + ref[...].astype(jnp.float32)
    refs[-1][...] = total.astype(jnp.bfloat16)


def gather_kernel(size, *refs):
    pieces, out = refs[:-1], refs[-1]
    me = lax.axis_index("seq")
    rows = pieces[0].shape[0]
    for d, piece in enumerate(pieces):
        at = pl.multiple_of(lax.rem(me + size - d, size) * rows, rows)
        out[pl.ds(at, rows), :] = piece[...]


def gather(pieces, after=()):
    size, (rows, width) = len(pieces), pieces[0].shape
    return small_call(
        functools.partial(gather_kernel, size), "gather_grads",
        jax.ShapeDtypeStruct((rows * size, width), jnp.bfloat16), *pieces, after=after,
    )


def finish_kernel(count, *refs):
    grad_b, grad_a = refs[2 * count :]
    sub = lax.axis_index("sub")
    half, wide = refs[0].shape[0], grad_b.shape[1]
    here = pl.ds(pl.multiple_of(sub * half, half), half)
    there = pl.ds(pl.multiple_of((1 - sub) * half, half), half)
    for at, group in ((here, refs[0 : 2 * count : 2]), (there, refs[1 : 2 * count : 2])):
        col = 0
        for ref in group:
            width = ref.shape[1]
            first = min(width, wide - col)
            grad_b[at, col : col + first] = ref[:, 0:first].astype(jnp.float32)
            if first < width:
                grad_a[at, :] = ref[:, first:].astype(jnp.float32)
            col += width


def finish(pairs, wide):
    rows, width = pairs[0][0].shape[0] * 2, sum(half.shape[1] for half, _ in pairs)
    return small_call(
        functools.partial(finish_kernel, len(pairs)), "finish_grads",
        [
            jax.ShapeDtypeStruct((rows, wide), jnp.float32),
            jax.ShapeDtypeStruct((rows, width - wide), jnp.float32),
        ],
        *[block for pair in pairs for block in pair],
    )


def halves_of(rows, width):
    return [jax.ShapeDtypeStruct((rows // 2, width), jnp.bfloat16)] * 2


def scatter(*pairs, after=()):
    size = lax.axis_size("seq")
    rows, width = pairs[0][0].shape[0], sum(keep.shape[1] for keep, _ in pairs)
    shard = jax.ShapeDtypeStruct((rows // size, width), jnp.bfloat16)
    return small_call(
        functools.partial(scatter_kernel, size, len(pairs)), "scatter_grads", [shard] * size,
        *[block for pair in pairs for block in pair],
        after=after, scratch=[pltpu.VMEM((rows, width), jnp.bfloat16)],
    )


def exchange(shards):
    return [shards[0]] + [rotate_over(block, "seq", d + 1) for d, block in enumerate(shards[1:])]


def add_up(pieces, after=(), through=()):
    shape = jax.ShapeDtypeStruct(pieces[0].shape, pieces[0].dtype)
    return small_call(sum_kernel, "sum_grads", shape, *pieces, after=after, through=through)


def spread(shard):
    return [shard] + [rotate_over(shard, "seq", d) for d in range(1, lax.axis_size("seq"))]


def swap_over(block, axis):
    return lax.ppermute(block, axis, [(0, 1), (1, 0)])


def rotate_over(block, axis, d):
    size = lax.axis_size(axis)
    return lax.ppermute(block, axis, [(i, (i + d) % size) for i in range(size)])


def terms_over(block, axis):
    if lax.axis_size(axis) == 2:
        return block, swap_over(block, axis)
    return lax.psum(block, axis), jnp.zeros_like(block)


def shift_over(block, axis):
    size = lax.axis_size(axis)
    return lax.ppermute(block, axis, [(i, i + 1) for i in range(size - 1)])


def body(
    normed_inputs, base_queries, base_keys, base_values, adapter_down, adapter_up,
    position_document, document_tenant, output_gradient,
):
    rows, width = normed_inputs.shape
    tenants, _, rank = adapter_down.shape
    tall, up_width = tenants * rank, adapter_up.shape[2]
    doc = position_document.reshape(1, rows)
    adapter = jnp.transpose(adapter_down, (0, 2, 1)).reshape(tall, width)
    up = adapter_up.reshape(tall, up_width)
    key_heads = base_keys.shape[1] // HEAD
    chunks = 2 if key_heads % 4 == 0 else 1
    size = lax.axis_size("seq")
    by_hand = chunks == 2 and tall % (2 * TAIL * size) == 0

    own = pack(base_keys, base_values, doc, chunks)
    info = down_project(normed_inputs, adapter, doc, document_tenant, tenants, rank)
    terms = terms_over(info, "mp")
    group = base_queries.shape[1] // HEAD // key_heads
    per = key_heads // chunks
    counts = [1, per - 1, per] if chunks == 2 else [1] * per
    state, pairs, held, with_ids, head = None, [], [], None, 0
    for i, count in enumerate(counts):
        chunk = head // per
        if len(held) < chunks and i < 2:
            two = shift_over(own[i], "seq")
            passing, two = relay(own[i], two, terms[1] if i == 0 else state[1])
            held.append((own[i], two, swap_over(two, "sub"), shift_over(passing, ("seq", "sub"))))
        with_ids = held[0]
        out, keep, send, gdown = attention(
            head, head % per, count, group, base_queries, output_gradient, up, held[chunk],
            with_ids, info, terms, state, tenants, rank,
        )
        state = (out, gdown)
        pairs.append((keep, send))
        head += count
    if by_hand:
        keep_late, send_late = pairs[-1]
        one, other = terms_over(gdown, "mp")
        swapped = [(keep, swap_over(send, "sub")) for keep, send in pairs[:-1]]
        pieces = exchange(scatter(*swapped, after=[keep_late]))
        early = add_up(pieces)
        keep_a, send_a = small_call(
            functools.partial(split_kernel, tenants, rank), "split_grads", halves_of(tall, width),
            one, other, info, normed_inputs, after=pieces[1:2],
        )
        shards = scatter(
            (keep_late, swap_over(send_late, "sub")), (keep_a, swap_over(send_a, "sub")), after=[early]
        )
        late = add_up(exchange(shards))
        half_early = gather(spread(early), after=[late])
        other_early = swap_over(half_early, "sub")
        half_late = gather(spread(late), after=[other_early])
        grad_b, grad_a = finish(
            [(half_early, other_early), (half_late, swap_over(half_late, "sub"))], up_width
        )
    else:
        one, other = terms_over(gdown, "mp")
        part_a = small_call(
            functools.partial(grad_a_kernel, tenants, rank), "grad_a_part",
            jax.ShapeDtypeStruct((tall, width), jnp.bfloat16), one, other, info, normed_inputs,
        )
        grad_a = lax.psum(part_a, ("seq", "sub")).astype(jnp.float32)
        keeps = jnp.concatenate([keep for keep, _ in pairs], axis=1)
        sends = jnp.concatenate([send for _, send in pairs], axis=1)
        low = lax.axis_index("sub") == 0
        part_b = jnp.concatenate([jnp.where(low, keeps, sends), jnp.where(low, sends, keeps)])
        grad_b = lax.psum(part_b, ("seq", "sub")).astype(jnp.float32)
    grad_a = jnp.transpose(grad_a.reshape(tenants, rank, width), (0, 2, 1))
    return out, grad_a, grad_b.reshape(tenants, rank, up_width)


def solution(mesh):
    split = P(("rep", "seq", "sub"), "mp")
    in_specs = (
        split, split, split, split, P(None, "mp", None), P(None, None, "mp"),
        P(("rep", "seq", "sub")), P("rep"), split,
    )
    out_specs = (split, P("rep", "mp", None), P("rep", None, "mp"))
    return jax.shard_map(body, mesh=mesh, in_specs=in_specs, out_specs=out_specs, check_vma=False)
```

```python
import functools

import jax
import jax.numpy as jnp
from jax import lax
from jax.experimental import pallas as pl
from jax.experimental.pallas import tpu as pltpu
from jax.sharding import PartitionSpec as P

HEAD = 128
REACH = 3
NEG = -1e30
LIFT = 2.0
LOG2E = 1.4426950408889634
TAIL = 16
VMEM_BYTES = 48 * 1024 * 1024
VMEM_MOST = 60 * 1024 * 1024
VMEM_HEADS = 57 * 1024 * 1024

VM = pl.BlockSpec(memory_space=pltpu.VMEM)
SM = pl.BlockSpec(memory_space=pltpu.SMEM)
ANY = pl.BlockSpec(memory_space=pl.ANY)


def nt(a, b):
    return lax.dot_general(a, b, (((1,), (1,)), ((), ())), preferred_element_type=jnp.float32)


def nn(a, b):
    return jnp.dot(a, b, preferred_element_type=jnp.float32)


def params(limit=VMEM_BYTES):
    return pltpu.CompilerParams(vmem_limit_bytes=limit)


def fetch(pairs, sems):
    copies = [pltpu.make_async_copy(src, dst, sems.at[i]) for i, (src, dst) in enumerate(pairs)]
    for copy in copies:
        copy.start()
    return copies


def pack_kernel(keys, values, doc, *rest):
    outs, (ids, blocks, sems) = rest[:-3], rest[-3:]
    rows, width = keys.shape
    part = width // len(outs)
    pairs = [(doc, ids)]
    for c in range(len(outs)):
        cols = pl.ds(c * part, part)
        pairs.append((keys.at[:, cols], blocks.at[c, pl.ds(0, rows), pl.ds(0, part)]))
        pairs.append((values.at[:, cols], blocks.at[c, pl.ds(0, rows), pl.ds(part, part)]))
    loads = fetch(pairs, sems.at[pl.ds(0, len(pairs))])
    loads[0].wait()
    tail = jnp.broadcast_to((ids[...] + 1).astype(jnp.float32), (TAIL, rows)).astype(jnp.bfloat16)
    stores = []
    for c, out in enumerate(outs):
        blocks[c, rows:, :] = jnp.zeros((TAIL, 2 * part), jnp.bfloat16)
        blocks[c, rows:, 0:rows] = tail
        loads[1 + 2 * c].wait()
        loads[2 + 2 * c].wait()
        stores += fetch([(blocks.at[c], out)], sems.at[pl.ds(len(pairs) + c, 1)])
    for store in stores:
        store.wait()


def pack(keys, values, doc, chunks):
    rows, width = keys.shape
    shape = (rows + TAIL, 2 * width // chunks)
    return pl.pallas_call(
        pack_kernel,
        out_shape=[jax.ShapeDtypeStruct(shape, jnp.bfloat16)] * chunks,
        in_specs=[ANY] * 3,
        out_specs=[ANY] * chunks,
        scratch_shapes=[
            pltpu.VMEM((1, rows), jnp.int32),
            pltpu.VMEM((chunks, *shape), jnp.bfloat16),
            pltpu.SemaphoreType.DMA((1 + 3 * chunks,)),
        ],
        compiler_params=params(VMEM_MOST),
        cost_estimate=pl.CostEstimate(flops=0, bytes_accessed=8 * rows * width, transcendentals=0),
        name="pack_keys_values",
    )(keys, values, doc)


def relay_kernel(own, got, after, out, got_out, held, sems):
    sub = lax.axis_index("sub")

    def move(source):
        load = pltpu.make_async_copy(source, held, sems.at[0])
        load.start()
        load.wait()

    @pl.when(sub == 0)
    def _():
        move(own)

    @pl.when(sub != 0)
    def _():
        move(got)

    store = pltpu.make_async_copy(held, out, sems.at[1])
    store.start()
    store.wait()


def relay(own, got, after):
    shape = jax.ShapeDtypeStruct(own.shape, own.dtype)
    return pl.pallas_call(
        relay_kernel,
        out_shape=[shape, shape],
        in_specs=[ANY, ANY, ANY],
        out_specs=[ANY, ANY],
        input_output_aliases={1: 1},
        scratch_shapes=[pltpu.VMEM(own.shape, own.dtype), pltpu.SemaphoreType.DMA((2,))],
        compiler_params=params(),
        cost_estimate=pl.CostEstimate(flops=0, bytes_accessed=4 * own.size, transcendentals=0),
        name="relay_block",
    )(own, got, after)


def selector_of(owner, tenants, rank):
    rows = owner.shape[1]
    tenant = lax.broadcasted_iota(jnp.int32, (tenants * rank, rows), 0) // rank
    return tenant == owner


def fold(full, owner, tenants, rank):
    kept = jnp.where(selector_of(owner, tenants, rank), full, 0.0)
    total = kept[0:rank]
    for t in range(1, tenants):
        total = total + kept[t * rank : (t + 1) * rank]
    return total


def unfold(compact, owner, tenants, rank):
    spread = jnp.concatenate([compact] * tenants, axis=0)
    return jnp.where(selector_of(owner, tenants, rank), spread, 0.0)


def down_kernel(tenants, rank, x_hbm, adapter_hbm, doc_hbm, tenant_of, info, x, adapter, doc, sems):
    copies = fetch([(doc_hbm, doc), (x_hbm, x), (adapter_hbm, adapter)], sems)
    copies[0].wait()
    ids = doc[...]
    found = jnp.zeros(ids.shape, jnp.int32)
    for s in range(tenant_of.shape[0]):
        found = jnp.where(ids == s, tenant_of[s], found)
    info[rank:, :] = jnp.broadcast_to(found.astype(jnp.float32), (info.shape[0] - rank, ids.shape[1]))
    copies[1].wait()
    copies[2].wait()
    info[0:rank, :] = fold(nt(x[...], adapter[...]).T, found, tenants, rank)


def down_project(x, adapter, doc, tenant_of, tenants, rank):
    rows, width = x.shape
    return pl.pallas_call(
        functools.partial(down_kernel, tenants, rank),
        out_shape=jax.ShapeDtypeStruct((rank + 8, rows), jnp.float32),
        in_specs=[ANY, ANY, ANY, SM],
        out_specs=VM,
        scratch_shapes=[
            pltpu.VMEM(x.shape, x.dtype),
            pltpu.VMEM(adapter.shape, adapter.dtype),
            pltpu.VMEM(doc.shape, doc.dtype),
            pltpu.SemaphoreType.DMA((3,)),
        ],
        compiler_params=params(VMEM_MOST),
        cost_estimate=pl.CostEstimate(
            flops=2 * rows * width * tenants * rank,
            bytes_accessed=2 * width * (rows + tenants * rank),
            transcendentals=0,
        ),
        name="down_project",
    )(x, adapter, doc, tenant_of)


def owner_of(info, rank):
    return info[rank : rank + 1, :].astype(jnp.int32)


def turn(x):
    return x.astype(jnp.float32).T.astype(jnp.bfloat16)


def attention(
    head, at, count, group, base, grad, up, blocks, with_ids, info, terms, before, tenants, rank
):
    rows, width = base.shape
    window = (REACH + 1) * rows
    tall = tenants * rank
    half = tall // 2
    span = group * HEAD
    pair = min(4, group)
    scale = HEAD**-0.5
    wide = lambda r: pl.BlockSpec((r, span), lambda i: (0, i + head))
    narrow = pl.BlockSpec((half, span), lambda i: (0, i))
    keys = pl.BlockSpec((rows, HEAD), lambda i: (0, i + at))
    skip = blocks[0].shape[1] // (2 * HEAD)
    values = pl.BlockSpec((rows, HEAD), lambda i: (0, i + at + skip))
    ids = pl.BlockSpec((TAIL, rows), lambda i: (rows // TAIL, 0))
    same = lambda a: pl.BlockSpec(a.shape, lambda i: (0, 0))
    operands, specs = [base, grad, up], [wide(rows), wide(rows), wide(tall)]
    for block in blocks:
        operands += [block, block]
        specs += [keys, values]
    operands += [*with_ids, info, *terms]
    specs += [ids] * 4 + [same(info)] * 3
    if before is not None:
        operands += [before[1], before[0]]
        specs += [same(before[1]), ANY]
    held = dict(
        kw=pltpu.VMEM((window, HEAD), jnp.bfloat16),
        vw=pltpu.VMEM((window, HEAD), jnp.bfloat16),
        kt=pltpu.VMEM((HEAD, window), jnp.bfloat16),
        vt=pltpu.VMEM((HEAD + TAIL, window), jnp.bfloat16),
        bottle=pltpu.VMEM((rows, tall), jnp.bfloat16),
        bottle_t=pltpu.VMEM((tall, rows), jnp.bfloat16),
        bias=pltpu.VMEM((window, rows), jnp.float32),
        query=pltpu.VMEM((span, rows), jnp.bfloat16),
        gt=pltpu.VMEM((span, rows), jnp.bfloat16),
        gquery=pltpu.VMEM((span, rows), jnp.bfloat16),
        scores=pltpu.VMEM((pair, window, rows), jnp.float32),
        part=pltpu.VMEM((tall, span), jnp.bfloat16),
        total=pltpu.VMEM((tall, rows), jnp.float32),
        reach=pltpu.SMEM((1,), jnp.int32),
    )

    def kernel(*refs):
        base, grad, up = refs[0:3]
        kv, tails, info, terms = refs[3:11], refs[11:15], refs[15], refs[16:18]
        out, keep, send, projected = refs[len(operands) : len(operands) + 4]
        r = dict(zip(held, refs[len(operands) + 4 :]))
        kw, vw, kt, vt = (r[n] for n in ("kw", "vw", "kt", "vt"))
        bias, query, gt, gquery, scores = (
            r[n] for n in ("bias", "query", "gt", "gquery", "scores")
        )
        sub = lax.axis_index("sub")
        step = pl.program_id(0)

        @pl.when(step == 0)
        def _():
            owner = owner_of(info, rank)
            lifted = unfold((terms[0][...] + terms[1][...])[0:rank], owner, tenants, rank)
            r["bottle_t"][...] = lifted.astype(jnp.bfloat16)
            r["bottle"][...] = lifted.T.astype(jnp.bfloat16)
            r["total"][...] = jnp.zeros((tall, rows), jnp.float32)
            vt[HEAD:, :] = jnp.ones((TAIL, window), jnp.bfloat16)
            own, two, swap, passed = (ref[...].astype(jnp.float32) for ref in tails)
            near = jnp.where(sub == 0, swap, passed)
            far = jnp.where(sub == 0, passed, swap)
            mine = own[0:1, :]
            lowest = jnp.min(mine)
            reach = 0
            for slot, block in ((REACH, own), (2, near), (1, two), (0, far)):
                same = block.T[:, 0:1] == mine
                if slot == REACH:
                    same = same & (
                        lax.broadcasted_iota(jnp.int32, (rows, rows), 0)
                        <= lax.broadcasted_iota(jnp.int32, (rows, rows), 1)
                    )
                else:
                    reach = jnp.where(jnp.max(block[0:1, :]) == lowest, REACH - slot, reach)
                bias[slot * rows : (slot + 1) * rows, :] = jnp.where(same, 0.0, NEG)
            r["reach"][0] = reach

        def place(slot, k_ref, v_ref):
            at = slice(slot * rows, (slot + 1) * rows)
            k, v = k_ref[...], v_ref[...]
            kw[at, :] = k
            vw[at, :] = v
            kt[:, at] = turn(k)
            vt[0:HEAD, at] = turn(v)

        place(REACH, *kv[0:2])
        place(1, *kv[2:4])

        @pl.when(sub == 0)
        def _():
            place(2, *kv[4:6])
            place(0, *kv[6:8])

        @pl.when(sub != 0)
        def _():
            place(2, *kv[6:8])
            place(0, *kv[4:6])

        lift = LIFT * nn(r["bottle"][...], up[...])
        query[...] = (base[...].astype(jnp.float32) + lift).T.astype(jnp.bfloat16)
        gt[...] = turn(grad[...])

        def run(reached, numbers):
            chunks = [slice(c * rows, (c + 1) * rows) for c in range(REACH - reached, REACH + 1)]
            spans = [pl.ds(pl.multiple_of(h * HEAD, HEAD), HEAD) for h in numbers]
            peaks = []
            for i, span_i in enumerate(spans):
                q, peak = query[span_i, :], None
                for c in chunks:
                    s = nn(kw[c, :], q) + bias[c, :]
                    scores[i, c, :] = s
                    top = jnp.max(s, axis=0, keepdims=True)
                    peak = top if peak is None else jnp.maximum(peak, top)
                peaks.append(peak)
            inverses, rowdots = [], []
            for i, span_i in enumerate(spans):
                total = None
                for c in chunks:
                    w = jnp.exp2((scores[i, c, :] - peaks[i]) * (scale * LOG2E))
                    scores[i, c, :] = w
                    o = nn(vt[:, c], w.astype(jnp.bfloat16))
                    total = o if total is None else total + o
                inverse = 1.0 / total[HEAD : HEAD + 1, :]
                attn = total[0:HEAD, :] * inverse
                out[:, span_i] = attn.T.astype(jnp.bfloat16)
                attn = attn.astype(jnp.bfloat16)
                product = gt[span_i, :].astype(jnp.float32) * attn.astype(jnp.float32)
                rowdots.append(jnp.sum(product, axis=0, keepdims=True))
                inverses.append(inverse)
            for i, span_i in enumerate(spans):
                g, moved = gt[span_i, :], None
                for c in chunks:
                    dprob = nn(vw[c, :], g)
                    ds = (scores[i, c, :] * (dprob - rowdots[i])).astype(jnp.bfloat16)
                    dq = nn(kt[:, c], ds)
                    moved = dq if moved is None else moved + dq
                gquery[span_i, :] = (moved * (inverses[i] * (LIFT * scale))).astype(jnp.bfloat16)

        for reached in range(REACH + 1):

            @pl.when(r["reach"][0] == reached)
            def _():
                @pl.loop(0, group // pair)
                def _(i):
                    run(reached, [i * pair + k for k in range(pair)])

        r["part"][...] = nt(r["bottle_t"][...], gquery[...]).astype(jnp.bfloat16)
        keep[...] = r["part"][pl.ds(pl.multiple_of(sub * half, half), half), :]
        send[...] = r["part"][pl.ds(pl.multiple_of((1 - sub) * half, half), half), :]
        r["total"][...] += nn(up[...], gquery[...])

        @pl.when(step == count - 1)
        def _():
            folded = fold(r["total"][...], owner_of(info, rank), tenants, rank)
            projected[...] = folded if before is None else folded + refs[18][...]

    return pl.pallas_call(
        kernel,
        grid=(count,),
        out_shape=[
            jax.ShapeDtypeStruct((rows, width), jnp.bfloat16),
            *halves_of(tall, count * span),
            jax.ShapeDtypeStruct((rank, rows), jnp.float32),
        ],
        in_specs=specs,
        out_specs=[wide(rows), narrow, narrow, pl.BlockSpec((rank, rows), lambda i: (0, 0))],
        scratch_shapes=list(held.values()),
        input_output_aliases={19: 0} if before is not None else {},
        compiler_params=params(VMEM_HEADS),
        cost_estimate=pl.CostEstimate(
            flops=8 * rows * window * span * count,
            bytes_accessed=6 * rows * span * count,
            transcendentals=rows * window * group * count,
        ),
        name="attention",
    )(*operands)


def small_call(kernel, name, shapes, *operands, after=(), through=(), scratch=()):
    size = sum(2 * a.size for a in operands)
    count, results = len(operands), jax.tree.leaves(shapes)
    given = (*operands, *after, *through)
    outs = len(given) + len(results)
    calls = pl.pallas_call(
        lambda *refs: kernel(
            *refs[:count], *refs[len(given) : outs], *refs[outs + len(through) :]
        ),
        out_shape=results + [jax.ShapeDtypeStruct(a.shape, a.dtype) for a in through],
        in_specs=[VM] * count + [ANY] * (len(after) + len(through)),
        out_specs=[VM] * len(results) + [ANY] * len(through),
        scratch_shapes=list(scratch),
        input_output_aliases={
            count + len(after) + i: len(results) + i for i in range(len(through))
        },
        compiler_params=params(),
        cost_estimate=pl.CostEstimate(flops=size, bytes_accessed=2 * size, transcendentals=0),
        name=name,
    )(*given)
    return calls if isinstance(shapes, list) or through else calls[0]


def grad_a_of(tenants, rank, one, other, info, x):
    g = unfold((one[...] + other[...]), owner_of(info[...], rank), tenants, rank)
    return nn(g.astype(jnp.bfloat16), x[...]).astype(jnp.bfloat16)


def grad_a_kernel(tenants, rank, one, other, info, x, out):
    out[...] = grad_a_of(tenants, rank, one, other, info, x)


def split_kernel(tenants, rank, one, other, info, x, keep, send):
    part = grad_a_of(tenants, rank, one, other, info, x)
    half = keep.shape[0]
    sub = lax.axis_index("sub")

    @pl.when(sub == 0)
    def _():
        keep[...] = part[0:half, :]
        send[...] = part[half:, :]

    @pl.when(sub != 0)
    def _():
        keep[...] = part[half:, :]
        send[...] = part[0:half, :]


def scatter_kernel(size, count, *refs):
    mine, *sends, total = refs[2 * count :]
    col = 0
    for keep, got in zip(refs[0 : 2 * count : 2], refs[1 : 2 * count : 2]):
        both = keep[...].astype(jnp.float32) + got[...].astype(jnp.float32)
        total[:, col : col + keep.shape[1]] = both.astype(jnp.bfloat16)
        col += keep.shape[1]
    me = lax.axis_index("seq")
    rows = mine.shape[0]
    for d, out in enumerate((mine, *sends)):
        at = pl.multiple_of(lax.rem(me + d, size) * rows, rows)
        out[...] = total[pl.ds(at, rows), :]


def sum_kernel(*refs):
    total = refs[0][...].astype(jnp.float32)
    for ref in refs[1:-1]:
        total = total + ref[...].astype(jnp.float32)
    refs[-1][...] = total.astype(jnp.bfloat16)


def gather_kernel(size, *refs):
    pieces, out = refs[:-1], refs[-1]
    me = lax.axis_index("seq")
    rows = pieces[0].shape[0]
    for d, piece in enumerate(pieces):
        at = pl.multiple_of(lax.rem(me + size - d, size) * rows, rows)
        out[pl.ds(at, rows), :] = piece[...]


def gather(pieces, after=()):
    size, (rows, width) = len(pieces), pieces[0].shape
    return small_call(
        functools.partial(gather_kernel, size), "gather_grads",
        jax.ShapeDtypeStruct((rows * size, width), jnp.bfloat16), *pieces, after=after,
    )


def finish_kernel(count, *refs):
    grad_b, grad_a = refs[2 * count :]
    sub = lax.axis_index("sub")
    half, wide = refs[0].shape[0], grad_b.shape[1]
    here = pl.ds(pl.multiple_of(sub * half, half), half)
    there = pl.ds(pl.multiple_of((1 - sub) * half, half), half)
    for at, group in ((here, refs[0 : 2 * count : 2]), (there, refs[1 : 2 * count : 2])):
        col = 0
        for ref in group:
            width = ref.shape[1]
            first = min(width, wide - col)
            grad_b[at, col : col + first] = ref[:, 0:first].astype(jnp.float32)
            if first < width:
                grad_a[at, :] = ref[:, first:].astype(jnp.float32)
            col += width


def finish(pairs, wide):
    rows, width = pairs[0][0].shape[0] * 2, sum(half.shape[1] for half, _ in pairs)
    return small_call(
        functools.partial(finish_kernel, len(pairs)), "finish_grads",
        [
            jax.ShapeDtypeStruct((rows, wide), jnp.float32),
            jax.ShapeDtypeStruct((rows, width - wide), jnp.float32),
        ],
        *[block for pair in pairs for block in pair],
    )


def halves_of(rows, width):
    return [jax.ShapeDtypeStruct((rows // 2, width), jnp.bfloat16)] * 2


def scatter(*pairs, after=()):
    size = lax.axis_size("seq")
    rows, width = pairs[0][0].shape[0], sum(keep.shape[1] for keep, _ in pairs)
    shard = jax.ShapeDtypeStruct((rows // size, width), jnp.bfloat16)
    return small_call(
        functools.partial(scatter_kernel, size, len(pairs)), "scatter_grads", [shard] * size,
        *[block for pair in pairs for block in pair],
        after=after, scratch=[pltpu.VMEM((rows, width), jnp.bfloat16)],
    )


def exchange(shards):
    return [shards[0]] + [rotate_over(block, "seq", d + 1) for d, block in enumerate(shards[1:])]


def add_up(pieces, after=(), through=()):
    shape = jax.ShapeDtypeStruct(pieces[0].shape, pieces[0].dtype)
    return small_call(sum_kernel, "sum_grads", shape, *pieces, after=after, through=through)


def spread(shard):
    return [shard] + [rotate_over(shard, "seq", d) for d in range(1, lax.axis_size("seq"))]


def swap_over(block, axis):
    return lax.ppermute(block, axis, [(0, 1), (1, 0)])


def rotate_over(block, axis, d):
    size = lax.axis_size(axis)
    return lax.ppermute(block, axis, [(i, (i + d) % size) for i in range(size)])


def terms_over(block, axis):
    if lax.axis_size(axis) == 2:
        return block, swap_over(block, axis)
    return lax.psum(block, axis), jnp.zeros_like(block)


def shift_over(block, axis):
    size = lax.axis_size(axis)
    return lax.ppermute(block, axis, [(i, i + 1) for i in range(size - 1)])


def body(
    normed_inputs, base_queries, base_keys, base_values, adapter_down, adapter_up,
    position_document, document_tenant, output_gradient,
):
    rows, width = normed_inputs.shape
    tenants, _, rank = adapter_down.shape
    tall, up_width = tenants * rank, adapter_up.shape[2]
    doc = position_document.reshape(1, rows)
    adapter = jnp.transpose(adapter_down, (0, 2, 1)).reshape(tall, width)
    up = adapter_up.reshape(tall, up_width)
    key_heads = base_keys.shape[1] // HEAD
    chunks = 2 if key_heads % 4 == 0 else 1
    size = lax.axis_size("seq")
    by_hand = chunks == 2 and tall % (2 * TAIL * size) == 0

    own = pack(base_keys, base_values, doc, chunks)
    info = down_project(normed_inputs, adapter, doc, document_tenant, tenants, rank)
    terms = terms_over(info, "mp")
    group = base_queries.shape[1] // HEAD // key_heads
    per = key_heads // chunks
    counts = [1, per - 1, per] if chunks == 2 else [1] * per
    state, pairs, held, with_ids, head = None, [], [], None, 0
    for i, count in enumerate(counts):
        chunk = head // per
        if len(held) < chunks and i < 2:
            two = shift_over(own[i], "seq")
            passing, two = relay(own[i], two, terms[1] if i == 0 else state[1])
            held.append((own[i], two, swap_over(two, "sub"), shift_over(passing, ("seq", "sub"))))
        with_ids = held[0]
        out, keep, send, gdown = attention(
            head, head % per, count, group, base_queries, output_gradient, up, held[chunk],
            with_ids, info, terms, state, tenants, rank,
        )
        state = (out, gdown)
        pairs.append((keep, send))
        head += count
    if by_hand:
        keep_late, send_late = pairs[-1]
        one, other = terms_over(gdown, "mp")
        swapped = [(keep, swap_over(send, "sub")) for keep, send in pairs[:-1]]
        pieces = exchange(scatter(*swapped, after=[keep_late]))
        early = add_up(pieces)
        keep_a, send_a = small_call(
            functools.partial(split_kernel, tenants, rank), "split_grads", halves_of(tall, width),
            one, other, info, normed_inputs, after=pieces[1:2],
        )
        shards = scatter(
            (keep_late, swap_over(send_late, "sub")), (keep_a, swap_over(send_a, "sub")), after=[early]
        )
        late = add_up(exchange(shards))
        half_early = gather(spread(early), after=[late])
        other_early = swap_over(half_early, "sub")
        half_late = gather(spread(late), after=[other_early])
        grad_b, grad_a = finish(
            [(half_early, other_early), (half_late, swap_over(half_late, "sub"))], up_width
        )
    else:
        one, other = terms_over(gdown, "mp")
        part_a = small_call(
            functools.partial(grad_a_kernel, tenants, rank), "grad_a_part",
            jax.ShapeDtypeStruct((tall, width), jnp.bfloat16), one, other, info, normed_inputs,
        )
        grad_a = lax.psum(part_a, ("seq", "sub")).astype(jnp.float32)
        keeps = jnp.concatenate([keep for keep, _ in pairs], axis=1)
        sends = jnp.concatenate([send for _, send in pairs], axis=1)
        low = lax.axis_index("sub") == 0
        part_b = jnp.concatenate([jnp.where(low, keeps, sends), jnp.where(low, sends, keeps)])
        grad_b = lax.psum(part_b, ("seq", "sub")).astype(jnp.float32)
    grad_a = jnp.transpose(grad_a.reshape(tenants, rank, width), (0, 2, 1))
    return out, grad_a, grad_b.reshape(tenants, rank, up_width)


def solution(mesh):
    split = P(("rep", "seq", "sub"), "mp")
    in_specs = (
        split, split, split, split, P(None, "mp", None), P(None, None, "mp"),
        P(("rep", "seq", "sub")), P("rep"), split,
    )
    out_specs = (split, P("rep", "mp", None), P("rep", None, "mp"))
    return jax.shard_map(body, mesh=mesh, in_specs=in_specs, out_specs=out_specs, check_vma=False)
```

```python
import functools

import jax
import jax.numpy as jnp
from jax import lax
from jax.experimental import pallas as pl
from jax.experimental.pallas import tpu as pltpu
from jax.sharding import PartitionSpec as P

HEAD = 128
REACH = 3
NEG = -1e30
LIFT = 2.0
LOG2E = 1.4426950408889634
TAIL = 16
VMEM_BYTES = 48 * 1024 * 1024
VMEM_MOST = 60 * 1024 * 1024
VMEM_HEADS = 57 * 1024 * 1024

VM = pl.BlockSpec(memory_space=pltpu.VMEM)
SM = pl.BlockSpec(memory_space=pltpu.SMEM)
ANY = pl.BlockSpec(memory_space=pl.ANY)


def nt(a, b):
    return lax.dot_general(a, b, (((1,), (1,)), ((), ())), preferred_element_type=jnp.float32)


def nn(a, b):
    return jnp.dot(a, b, preferred_element_type=jnp.float32)


def params(limit=VMEM_BYTES):
    return pltpu.CompilerParams(vmem_limit_bytes=limit)


def fetch(pairs, sems):
    copies = [pltpu.make_async_copy(src, dst, sems.at[i]) for i, (src, dst) in enumerate(pairs)]
    for copy in copies:
        copy.start()
    return copies


def pack_kernel(keys, values, doc, *rest):
    outs, (ids, blocks, sems) = rest[:-3], rest[-3:]
    rows, width = keys.shape
    part = width // len(outs)
    pairs = [(doc, ids)]
    for c in range(len(outs)):
        cols = pl.ds(c * part, part)
        pairs.append((keys.at[:, cols], blocks.at[c, pl.ds(0, rows), pl.ds(0, part)]))
        pairs.append((values.at[:, cols], blocks.at[c, pl.ds(0, rows), pl.ds(part, part)]))
    loads = fetch(pairs, sems.at[pl.ds(0, len(pairs))])
    loads[0].wait()
    tail = jnp.broadcast_to((ids[...] + 1).astype(jnp.float32), (TAIL, rows)).astype(jnp.bfloat16)
    stores = []
    for c, out in enumerate(outs):
        blocks[c, rows:, :] = jnp.zeros((TAIL, 2 * part), jnp.bfloat16)
        blocks[c, rows:, 0:rows] = tail
        loads[1 + 2 * c].wait()
        loads[2 + 2 * c].wait()
        stores += fetch([(blocks.at[c], out)], sems.at[pl.ds(len(pairs) + c, 1)])
    for store in stores:
        store.wait()


def pack(keys, values, doc, chunks):
    rows, width = keys.shape
    shape = (rows + TAIL, 2 * width // chunks)
    return pl.pallas_call(
        pack_kernel,
        out_shape=[jax.ShapeDtypeStruct(shape, jnp.bfloat16)] * chunks,
        in_specs=[ANY] * 3,
        out_specs=[ANY] * chunks,
        scratch_shapes=[
            pltpu.VMEM((1, rows), jnp.int32),
            pltpu.VMEM((chunks, *shape), jnp.bfloat16),
            pltpu.SemaphoreType.DMA((1 + 3 * chunks,)),
        ],
        compiler_params=params(VMEM_MOST),
        cost_estimate=pl.CostEstimate(flops=0, bytes_accessed=8 * rows * width, transcendentals=0),
        name="pack_keys_values",
    )(keys, values, doc)


def relay_kernel(own, got, after, out, got_out, held, sems):
    sub = lax.axis_index("sub")

    def move(source):
        load = pltpu.make_async_copy(source, held, sems.at[0])
        load.start()
        load.wait()

    @pl.when(sub == 0)
    def _():
        move(own)

    @pl.when(sub != 0)
    def _():
        move(got)

    store = pltpu.make_async_copy(held, out, sems.at[1])
    store.start()
    store.wait()


def relay(own, got, after):
    shape = jax.ShapeDtypeStruct(own.shape, own.dtype)
    return pl.pallas_call(
        relay_kernel,
        out_shape=[shape, shape],
        in_specs=[ANY, ANY, ANY],
        out_specs=[ANY, ANY],
        input_output_aliases={1: 1},
        scratch_shapes=[pltpu.VMEM(own.shape, own.dtype), pltpu.SemaphoreType.DMA((2,))],
        compiler_params=params(),
        cost_estimate=pl.CostEstimate(flops=0, bytes_accessed=4 * own.size, transcendentals=0),
        name="relay_block",
    )(own, got, after)


def selector_of(owner, tenants, rank):
    rows = owner.shape[1]
    tenant = lax.broadcasted_iota(jnp.int32, (tenants * rank, rows), 0) // rank
    return tenant == owner


def fold(full, owner, tenants, rank):
    kept = jnp.where(selector_of(owner, tenants, rank), full, 0.0)
    total = kept[0:rank]
    for t in range(1, tenants):
        total = total + kept[t * rank : (t + 1) * rank]
    return total


def unfold(compact, owner, tenants, rank):
    spread = jnp.concatenate([compact] * tenants, axis=0)
    return jnp.where(selector_of(owner, tenants, rank), spread, 0.0)


def down_kernel(tenants, rank, x_hbm, adapter_hbm, doc_hbm, tenant_of, info, x, adapter, doc, sems):
    copies = fetch([(doc_hbm, doc), (x_hbm, x), (adapter_hbm, adapter)], sems)
    copies[0].wait()
    ids = doc[...]
    found = jnp.zeros(ids.shape, jnp.int32)
    for s in range(tenant_of.shape[0]):
        found = jnp.where(ids == s, tenant_of[s], found)
    info[rank:, :] = jnp.broadcast_to(found.astype(jnp.float32), (info.shape[0] - rank, ids.shape[1]))
    copies[1].wait()
    copies[2].wait()
    info[0:rank, :] = fold(nt(x[...], adapter[...]).T, found, tenants, rank)


def down_project(x, adapter, doc, tenant_of, tenants, rank):
    rows, width = x.shape
    return pl.pallas_call(
        functools.partial(down_kernel, tenants, rank),
        out_shape=jax.ShapeDtypeStruct((rank + 8, rows), jnp.float32),
        in_specs=[ANY, ANY, ANY, SM],
        out_specs=VM,
        scratch_shapes=[
            pltpu.VMEM(x.shape, x.dtype),
            pltpu.VMEM(adapter.shape, adapter.dtype),
            pltpu.VMEM(doc.shape, doc.dtype),
            pltpu.SemaphoreType.DMA((3,)),
        ],
        compiler_params=params(VMEM_MOST),
        cost_estimate=pl.CostEstimate(
            flops=2 * rows * width * tenants * rank,
            bytes_accessed=2 * width * (rows + tenants * rank),
            transcendentals=0,
        ),
        name="down_project",
    )(x, adapter, doc, tenant_of)


def owner_of(info, rank):
    return info[rank : rank + 1, :].astype(jnp.int32)


def turn(x):
    return x.astype(jnp.float32).T.astype(jnp.bfloat16)


def attention(
    head, at, count, group, base, grad, up, blocks, with_ids, info, terms, before, tenants, rank
):
    rows, width = base.shape
    window = (REACH + 1) * rows
    tall = tenants * rank
    half = tall // 2
    span = group * HEAD
    pair = min(8, group)
    scale = HEAD**-0.5
    wide = lambda r: pl.BlockSpec((r, span), lambda i: (0, i + head))
    narrow = pl.BlockSpec((half, span), lambda i: (0, i))
    keys = pl.BlockSpec((rows, HEAD), lambda i: (0, i + at))
    skip = blocks[0].shape[1] // (2 * HEAD)
    values = pl.BlockSpec((rows, HEAD), lambda i: (0, i + at + skip))
    ids = pl.BlockSpec((TAIL, rows), lambda i: (rows // TAIL, 0))
    same = lambda a: pl.BlockSpec(a.shape, lambda i: (0, 0))
    operands, specs = [base, grad, up], [wide(rows), wide(rows), wide(tall)]
    for block in blocks:
        operands += [block, block]
        specs += [keys, values]
    operands += [*with_ids, info, *terms]
    specs += [ids] * 4 + [same(info)] * 3
    if before is not None:
        operands += [before[1], before[0]]
        specs += [same(before[1]), ANY]
    held = dict(
        kw=pltpu.VMEM((window, HEAD), jnp.bfloat16),
        vw=pltpu.VMEM((window, HEAD), jnp.bfloat16),
        kt=pltpu.VMEM((HEAD, window), jnp.bfloat16),
        vt=pltpu.VMEM((HEAD + TAIL, window), jnp.bfloat16),
        bottle=pltpu.VMEM((rows, tall), jnp.bfloat16),
        bottle_t=pltpu.VMEM((tall, rows), jnp.bfloat16),
        bias=pltpu.VMEM((window, rows), jnp.float32),
        query=pltpu.VMEM((span, rows), jnp.bfloat16),
        gt=pltpu.VMEM((span, rows), jnp.bfloat16),
        gquery=pltpu.VMEM((span, rows), jnp.bfloat16),
        scores=pltpu.VMEM((pair, window, rows), jnp.float32),
        part=pltpu.VMEM((tall, span), jnp.bfloat16),
        total=pltpu.VMEM((tall, rows), jnp.float32),
        reach=pltpu.SMEM((1,), jnp.int32),
    )

    def kernel(*refs):
        base, grad, up = refs[0:3]
        kv, tails, info, terms = refs[3:11], refs[11:15], refs[15], refs[16:18]
        out, keep, send, projected = refs[len(operands) : len(operands) + 4]
        r = dict(zip(held, refs[len(operands) + 4 :]))
        kw, vw, kt, vt = (r[n] for n in ("kw", "vw", "kt", "vt"))
        bias, query, gt, gquery, scores = (
            r[n] for n in ("bias", "query", "gt", "gquery", "scores")
        )
        sub = lax.axis_index("sub")
        step = pl.program_id(0)

        @pl.when(step == 0)
        def _():
            owner = owner_of(info, rank)
            lifted = unfold((terms[0][...] + terms[1][...])[0:rank], owner, tenants, rank)
            r["bottle_t"][...] = lifted.astype(jnp.bfloat16)
            r["bottle"][...] = lifted.T.astype(jnp.bfloat16)
            r["total"][...] = jnp.zeros((tall, rows), jnp.float32)
            vt[HEAD:, :] = jnp.ones((TAIL, window), jnp.bfloat16)
            own, two, swap, passed = (ref[...].astype(jnp.float32) for ref in tails)
            near = jnp.where(sub == 0, swap, passed)
            far = jnp.where(sub == 0, passed, swap)
            mine = own[0:1, :]
            lowest = jnp.min(mine)
            reach = 0
            for slot, block in ((REACH, own), (2, near), (1, two), (0, far)):
                same = block.T[:, 0:1] == mine
                if slot == REACH:
                    same = same & (
                        lax.broadcasted_iota(jnp.int32, (rows, rows), 0)
                        <= lax.broadcasted_iota(jnp.int32, (rows, rows), 1)
                    )
                else:
                    reach = jnp.where(jnp.max(block[0:1, :]) == lowest, REACH - slot, reach)
                bias[slot * rows : (slot + 1) * rows, :] = jnp.where(same, 0.0, NEG)
            r["reach"][0] = reach

        def place(slot, k_ref, v_ref):
            at = slice(slot * rows, (slot + 1) * rows)
            k, v = k_ref[...], v_ref[...]
            kw[at, :] = k
            vw[at, :] = v
            kt[:, at] = turn(k)
            vt[0:HEAD, at] = turn(v)

        place(REACH, *kv[0:2])
        place(1, *kv[2:4])

        @pl.when(sub == 0)
        def _():
            place(2, *kv[4:6])
            place(0, *kv[6:8])

        @pl.when(sub != 0)
        def _():
            place(2, *kv[6:8])
            place(0, *kv[4:6])

        lift = LIFT * nn(r["bottle"][...], up[...])
        query[...] = (base[...].astype(jnp.float32) + lift).T.astype(jnp.bfloat16)
        gt[...] = turn(grad[...])

        def run(reached, numbers):
            chunks = [slice(c * rows, (c + 1) * rows) for c in range(REACH - reached, REACH + 1)]
            spans = [pl.ds(pl.multiple_of(h * HEAD, HEAD), HEAD) for h in numbers]
            peaks = []
            for i, span_i in enumerate(spans):
                q, peak = query[span_i, :], None
                for c in chunks:
                    s = nn(kw[c, :], q) + bias[c, :]
                    scores[i, c, :] = s
                    top = jnp.max(s, axis=0, keepdims=True)
                    peak = top if peak is None else jnp.maximum(peak, top)
                peaks.append(peak)
            inverses, rowdots = [], []
            for i, span_i in enumerate(spans):
                total = None
                for c in chunks:
                    w = jnp.exp2((scores[i, c, :] - peaks[i]) * (scale * LOG2E))
                    scores[i, c, :] = w
                    o = nn(vt[:, c], w.astype(jnp.bfloat16))
                    total = o if total is None else total + o
                inverse = 1.0 / total[HEAD : HEAD + 1, :]
                attn = total[0:HEAD, :] * inverse
                out[:, span_i] = attn.T.astype(jnp.bfloat16)
                attn = attn.astype(jnp.bfloat16)
                product = gt[span_i, :].astype(jnp.float32) * attn.astype(jnp.float32)
                rowdots.append(jnp.sum(product, axis=0, keepdims=True))
                inverses.append(inverse)
            for i, span_i in enumerate(spans):
                g, moved = gt[span_i, :], None
                for c in chunks:
                    dprob = nn(vw[c, :], g)
                    ds = (scores[i, c, :] * (dprob - rowdots[i])).astype(jnp.bfloat16)
                    dq = nn(kt[:, c], ds)
                    moved = dq if moved is None else moved + dq
                gquery[span_i, :] = (moved * (inverses[i] * (LIFT * scale))).astype(jnp.bfloat16)

        for reached in (1, REACH):

            @pl.when((r["reach"][0] > 1) == (reached > 1))
            def _():
                @pl.loop(0, group // pair)
                def _(i):
                    run(reached, [i * pair + k for k in range(pair)])

        r["part"][...] = nt(r["bottle_t"][...], gquery[...]).astype(jnp.bfloat16)
        keep[...] = r["part"][pl.ds(pl.multiple_of(sub * half, half), half), :]
        send[...] = r["part"][pl.ds(pl.multiple_of((1 - sub) * half, half), half), :]
        r["total"][...] += nn(up[...], gquery[...])

        @pl.when(step == count - 1)
        def _():
            folded = fold(r["total"][...], owner_of(info, rank), tenants, rank)
            projected[...] = folded if before is None else folded + refs[18][...]

    return pl.pallas_call(
        kernel,
        grid=(count,),
        out_shape=[
            jax.ShapeDtypeStruct((rows, width), jnp.bfloat16),
            *halves_of(tall, count * span),
            jax.ShapeDtypeStruct((rank, rows), jnp.float32),
        ],
        in_specs=specs,
        out_specs=[wide(rows), narrow, narrow, pl.BlockSpec((rank, rows), lambda i: (0, 0))],
        scratch_shapes=list(held.values()),
        input_output_aliases={19: 0} if before is not None else {},
        compiler_params=params(VMEM_HEADS),
        cost_estimate=pl.CostEstimate(
            flops=8 * rows * window * span * count,
            bytes_accessed=6 * rows * span * count,
            transcendentals=rows * window * group * count,
        ),
        name="attention",
    )(*operands)


def small_call(kernel, name, shapes, *operands, after=(), through=(), scratch=()):
    size = sum(2 * a.size for a in operands)
    count, results = len(operands), jax.tree.leaves(shapes)
    given = (*operands, *after, *through)
    outs = len(given) + len(results)
    calls = pl.pallas_call(
        lambda *refs: kernel(
            *refs[:count], *refs[len(given) : outs], *refs[outs + len(through) :]
        ),
        out_shape=results + [jax.ShapeDtypeStruct(a.shape, a.dtype) for a in through],
        in_specs=[VM] * count + [ANY] * (len(after) + len(through)),
        out_specs=[VM] * len(results) + [ANY] * len(through),
        scratch_shapes=list(scratch),
        input_output_aliases={
            count + len(after) + i: len(results) + i for i in range(len(through))
        },
        compiler_params=params(),
        cost_estimate=pl.CostEstimate(flops=size, bytes_accessed=2 * size, transcendentals=0),
        name=name,
    )(*given)
    return calls if isinstance(shapes, list) or through else calls[0]


def grad_a_of(tenants, rank, one, other, info, x):
    g = unfold((one[...] + other[...]), owner_of(info[...], rank), tenants, rank)
    return nn(g.astype(jnp.bfloat16), x[...]).astype(jnp.bfloat16)


def grad_a_kernel(tenants, rank, one, other, info, x, out):
    out[...] = grad_a_of(tenants, rank, one, other, info, x)


def split_kernel(tenants, rank, one, other, info, x, keep, send):
    part = grad_a_of(tenants, rank, one, other, info, x)
    half = keep.shape[0]
    sub = lax.axis_index("sub")

    @pl.when(sub == 0)
    def _():
        keep[...] = part[0:half, :]
        send[...] = part[half:, :]

    @pl.when(sub != 0)
    def _():
        keep[...] = part[half:, :]
        send[...] = part[0:half, :]


def scatter_kernel(size, count, *refs):
    mine, *sends, total = refs[2 * count :]
    col = 0
    for keep, got in zip(refs[0 : 2 * count : 2], refs[1 : 2 * count : 2]):
        both = keep[...].astype(jnp.float32) + got[...].astype(jnp.float32)
        total[:, col : col + keep.shape[1]] = both.astype(jnp.bfloat16)
        col += keep.shape[1]
    me = lax.axis_index("seq")
    rows = mine.shape[0]
    for d, out in enumerate((mine, *sends)):
        at = pl.multiple_of(lax.rem(me + d, size) * rows, rows)
        out[...] = total[pl.ds(at, rows), :]


def sum_kernel(*refs):
    total = refs[0][...].astype(jnp.float32)
    for ref in refs[1:-1]:
        total = total + ref[...].astype(jnp.float32)
    refs[-1][...] = total.astype(jnp.bfloat16)


def gather_kernel(size, *refs):
    pieces, out, col = refs[:-1], refs[-1], 0
    me = lax.axis_index("seq")
    for first in range(0, len(pieces), size):
        rows, width = pieces[first].shape
        for d in range(size):
            at = pl.multiple_of(lax.rem(me + size - d, size) * rows, rows)
            out[pl.ds(at, rows), col : col + width] = pieces[first + d][...]
        col += width


def gather(*sums):
    size, rows = len(sums[0]), sums[0][0].shape[0]
    width = sum(pieces[0].shape[1] for pieces in sums)
    return small_call(
        functools.partial(gather_kernel, size), "gather_grads",
        jax.ShapeDtypeStruct((rows * size, width), jnp.bfloat16),
        *[piece for pieces in sums for piece in pieces],
    )


def finish_kernel(count, *refs):
    grad_b, grad_a = refs[2 * count :]
    sub = lax.axis_index("sub")
    half, wide = refs[0].shape[0], grad_b.shape[1]
    here = pl.ds(pl.multiple_of(sub * half, half), half)
    there = pl.ds(pl.multiple_of((1 - sub) * half, half), half)
    for at, group in ((here, refs[0 : 2 * count : 2]), (there, refs[1 : 2 * count : 2])):
        col = 0
        for ref in group:
            width = ref.shape[1]
            first = min(width, wide - col)
            grad_b[at, col : col + first] = ref[:, 0:first].astype(jnp.float32)
            if first < width:
                grad_a[at, :] = ref[:, first:].astype(jnp.float32)
            col += width


def finish(pairs, wide):
    rows, width = pairs[0][0].shape[0] * 2, sum(half.shape[1] for half, _ in pairs)
    return small_call(
        functools.partial(finish_kernel, len(pairs)), "finish_grads",
        [
            jax.ShapeDtypeStruct((rows, wide), jnp.float32),
            jax.ShapeDtypeStruct((rows, width - wide), jnp.float32),
        ],
        *[block for pair in pairs for block in pair],
    )


def halves_of(rows, width):
    return [jax.ShapeDtypeStruct((rows // 2, width), jnp.bfloat16)] * 2


def scatter(*pairs, after=()):
    size = lax.axis_size("seq")
    rows, width = pairs[0][0].shape[0], sum(keep.shape[1] for keep, _ in pairs)
    shard = jax.ShapeDtypeStruct((rows // size, width), jnp.bfloat16)
    return small_call(
        functools.partial(scatter_kernel, size, len(pairs)), "scatter_grads", [shard] * size,
        *[block for pair in pairs for block in pair],
        after=after, scratch=[pltpu.VMEM((rows, width), jnp.bfloat16)],
    )


def exchange(shards):
    return [shards[0]] + [rotate_over(block, "seq", d + 1) for d, block in enumerate(shards[1:])]


def add_up(pieces, after=(), through=()):
    shape = jax.ShapeDtypeStruct(pieces[0].shape, pieces[0].dtype)
    return small_call(sum_kernel, "sum_grads", shape, *pieces, after=after, through=through)


def spread(shard):
    return [shard] + [rotate_over(shard, "seq", d) for d in range(1, lax.axis_size("seq"))]


def swap_over(block, axis):
    return lax.ppermute(block, axis, [(0, 1), (1, 0)])


def rotate_over(block, axis, d):
    size = lax.axis_size(axis)
    return lax.ppermute(block, axis, [(i, (i + d) % size) for i in range(size)])


def terms_over(block, axis):
    if lax.axis_size(axis) == 2:
        return block, swap_over(block, axis)
    return lax.psum(block, axis), jnp.zeros_like(block)


def shift_over(block, axis):
    size = lax.axis_size(axis)
    return lax.ppermute(block, axis, [(i, i + 1) for i in range(size - 1)])


def body(
    normed_inputs, base_queries, base_keys, base_values, adapter_down, adapter_up,
    position_document, document_tenant, output_gradient,
):
    rows, width = normed_inputs.shape
    tenants, _, rank = adapter_down.shape
    tall, up_width = tenants * rank, adapter_up.shape[2]
    doc = position_document.reshape(1, rows)
    adapter = jnp.transpose(adapter_down, (0, 2, 1)).reshape(tall, width)
    up = adapter_up.reshape(tall, up_width)
    key_heads = base_keys.shape[1] // HEAD
    chunks = 2 if key_heads % 4 == 0 else 1
    size = lax.axis_size("seq")
    by_hand = chunks == 2 and tall % (2 * TAIL * size) == 0

    own = pack(base_keys, base_values, doc, chunks)
    info = down_project(normed_inputs, adapter, doc, document_tenant, tenants, rank)
    terms = terms_over(info, "mp")
    group = base_queries.shape[1] // HEAD // key_heads
    per = key_heads // chunks
    counts = [1, per - 1, per] if chunks == 2 else [1] * per
    state, pairs, held, with_ids, head = None, [], [], None, 0
    for i, count in enumerate(counts):
        chunk = head // per
        if len(held) < chunks and i < 2:
            two = shift_over(own[i], "seq")
            passing, two = relay(own[i], two, terms[1] if i == 0 else state[1])
            held.append((own[i], two, swap_over(two, "sub"), shift_over(passing, ("seq", "sub"))))
        with_ids = held[0]
        out, keep, send, gdown = attention(
            head, head % per, count, group, base_queries, output_gradient, up, held[chunk],
            with_ids, info, terms, state, tenants, rank,
        )
        state = (out, gdown)
        pairs.append((keep, send))
        head += count
    if by_hand:
        keep_late, send_late = pairs[-1]
        one, other = terms_over(gdown, "mp")
        swapped = [(keep, swap_over(send, "sub")) for keep, send in pairs[:-1]]
        pieces = exchange(scatter(*swapped, after=[keep_late]))
        early = add_up(pieces)
        keep_a, send_a = small_call(
            functools.partial(split_kernel, tenants, rank), "split_grads", halves_of(tall, width),
            one, other, info, normed_inputs, after=pieces[1:2],
        )
        shards = scatter(
            (keep_late, swap_over(send_late, "sub")), (keep_a, swap_over(send_a, "sub")), after=[early]
        )
        all_early = spread(early)
        late = add_up(exchange(shards), after=all_early[1:])
        half = gather(all_early, spread(late))
        grad_b, grad_a = finish([(half, swap_over(half, "sub"))], up_width)
    else:
        one, other = terms_over(gdown, "mp")
        part_a = small_call(
            functools.partial(grad_a_kernel, tenants, rank), "grad_a_part",
            jax.ShapeDtypeStruct((tall, width), jnp.bfloat16), one, other, info, normed_inputs,
        )
        grad_a = lax.psum(part_a, ("seq", "sub")).astype(jnp.float32)
        keeps = jnp.concatenate([keep for keep, _ in pairs], axis=1)
        sends = jnp.concatenate([send for _, send in pairs], axis=1)
        low = lax.axis_index("sub") == 0
        part_b = jnp.concatenate([jnp.where(low, keeps, sends), jnp.where(low, sends, keeps)])
        grad_b = lax.psum(part_b, ("seq", "sub")).astype(jnp.float32)
    grad_a = jnp.transpose(grad_a.reshape(tenants, rank, width), (0, 2, 1))
    return out, grad_a, grad_b.reshape(tenants, rank, up_width)


def solution(mesh):
    split = P(("rep", "seq", "sub"), "mp")
    in_specs = (
        split, split, split, split, P(None, "mp", None), P(None, None, "mp"),
        P(("rep", "seq", "sub")), P("rep"), split,
    )
    out_specs = (split, P("rep", "mp", None), P("rep", None, "mp"))
    return jax.shard_map(body, mesh=mesh, in_specs=in_specs, out_specs=out_specs, check_vma=False)
```

```python
import functools

import jax
import jax.numpy as jnp
from jax import lax
from jax.experimental import pallas as pl
from jax.experimental.pallas import tpu as pltpu
from jax.sharding import PartitionSpec as P

HEAD = 128
REACH = 3
NEG = -1e30
LIFT = 2.0
LOG2E = 1.4426950408889634
TAIL = 16
VMEM_BYTES = 48 * 1024 * 1024
VMEM_MOST = 60 * 1024 * 1024
VMEM_HEADS = 57 * 1024 * 1024

VM = pl.BlockSpec(memory_space=pltpu.VMEM)
SM = pl.BlockSpec(memory_space=pltpu.SMEM)
ANY = pl.BlockSpec(memory_space=pl.ANY)


def nt(a, b):
    return lax.dot_general(a, b, (((1,), (1,)), ((), ())), preferred_element_type=jnp.float32)


def nn(a, b):
    return jnp.dot(a, b, preferred_element_type=jnp.float32)


def params(limit=VMEM_BYTES):
    return pltpu.CompilerParams(vmem_limit_bytes=limit)


def fetch(pairs, sems):
    copies = [pltpu.make_async_copy(src, dst, sems.at[i]) for i, (src, dst) in enumerate(pairs)]
    for copy in copies:
        copy.start()
    return copies


def pack_kernel(keys, values, doc, *rest):
    outs, (ids, blocks, sems) = rest[:-3], rest[-3:]
    rows, width = keys.shape
    part = width // len(outs)
    pairs = [(doc, ids)]
    for c in range(len(outs)):
        cols = pl.ds(c * part, part)
        pairs.append((keys.at[:, cols], blocks.at[c, pl.ds(0, rows), pl.ds(0, part)]))
        pairs.append((values.at[:, cols], blocks.at[c, pl.ds(0, rows), pl.ds(part, part)]))
    loads = fetch(pairs, sems.at[pl.ds(0, len(pairs))])
    loads[0].wait()
    tail = jnp.broadcast_to((ids[...] + 1).astype(jnp.float32), (TAIL, rows)).astype(jnp.bfloat16)
    stores = []
    for c, out in enumerate(outs):
        blocks[c, rows:, :] = jnp.zeros((TAIL, 2 * part), jnp.bfloat16)
        blocks[c, rows:, 0:rows] = tail
        loads[1 + 2 * c].wait()
        loads[2 + 2 * c].wait()
        stores += fetch([(blocks.at[c], out)], sems.at[pl.ds(len(pairs) + c, 1)])
    for store in stores:
        store.wait()


def pack(keys, values, doc, chunks):
    rows, width = keys.shape
    shape = (rows + TAIL, 2 * width // chunks)
    return pl.pallas_call(
        pack_kernel,
        out_shape=[jax.ShapeDtypeStruct(shape, jnp.bfloat16)] * chunks,
        in_specs=[ANY] * 3,
        out_specs=[ANY] * chunks,
        scratch_shapes=[
            pltpu.VMEM((1, rows), jnp.int32),
            pltpu.VMEM((chunks, *shape), jnp.bfloat16),
            pltpu.SemaphoreType.DMA((1 + 3 * chunks,)),
        ],
        compiler_params=params(VMEM_MOST),
        cost_estimate=pl.CostEstimate(flops=0, bytes_accessed=8 * rows * width, transcendentals=0),
        name="pack_keys_values",
    )(keys, values, doc)


def relay_kernel(own, got, *rest):
    out, _, held, sems = rest[-4:]
    sub = lax.axis_index("sub")

    def move(source):
        load = pltpu.make_async_copy(source, held, sems.at[0])
        load.start()
        load.wait()

    @pl.when(sub == 0)
    def _():
        move(own)

    @pl.when(sub != 0)
    def _():
        move(got)

    store = pltpu.make_async_copy(held, out, sems.at[1])
    store.start()
    store.wait()


def relay(own, got, after):
    shape = jax.ShapeDtypeStruct(own.shape, own.dtype)
    return pl.pallas_call(
        relay_kernel,
        out_shape=[shape, shape],
        in_specs=[ANY] * (2 + len(after)),
        out_specs=[ANY, ANY],
        input_output_aliases={1: 1},
        scratch_shapes=[pltpu.VMEM(own.shape, own.dtype), pltpu.SemaphoreType.DMA((2,))],
        compiler_params=params(),
        cost_estimate=pl.CostEstimate(flops=0, bytes_accessed=4 * own.size, transcendentals=0),
        name="relay_block",
    )(own, got, *after)


def selector_of(owner, tenants, rank):
    rows = owner.shape[1]
    tenant = lax.broadcasted_iota(jnp.int32, (tenants * rank, rows), 0) // rank
    return tenant == owner


def fold(full, owner, tenants, rank):
    kept = jnp.where(selector_of(owner, tenants, rank), full, 0.0)
    total = kept[0:rank]
    for t in range(1, tenants):
        total = total + kept[t * rank : (t + 1) * rank]
    return total


def unfold(compact, owner, tenants, rank):
    spread = jnp.concatenate([compact] * tenants, axis=0)
    return jnp.where(selector_of(owner, tenants, rank), spread, 0.0)


def down_kernel(tenants, rank, x_hbm, adapter_hbm, doc_hbm, tenant_of, info, x, adapter, doc, sems):
    copies = fetch([(doc_hbm, doc), (x_hbm, x), (adapter_hbm, adapter)], sems)
    copies[0].wait()
    ids = doc[...]
    found = jnp.zeros(ids.shape, jnp.int32)
    for s in range(tenant_of.shape[0]):
        found = jnp.where(ids == s, tenant_of[s], found)
    info[rank:, :] = jnp.broadcast_to(found.astype(jnp.float32), (info.shape[0] - rank, ids.shape[1]))
    copies[1].wait()
    copies[2].wait()
    info[0:rank, :] = fold(nt(x[...], adapter[...]).T, found, tenants, rank)


def down_project(x, adapter, doc, tenant_of, tenants, rank):
    rows, width = x.shape
    return pl.pallas_call(
        functools.partial(down_kernel, tenants, rank),
        out_shape=jax.ShapeDtypeStruct((rank + 8, rows), jnp.float32),
        in_specs=[ANY, ANY, ANY, SM],
        out_specs=VM,
        scratch_shapes=[
            pltpu.VMEM(x.shape, x.dtype),
            pltpu.VMEM(adapter.shape, adapter.dtype),
            pltpu.VMEM(doc.shape, doc.dtype),
            pltpu.SemaphoreType.DMA((3,)),
        ],
        compiler_params=params(VMEM_MOST),
        cost_estimate=pl.CostEstimate(
            flops=2 * rows * width * tenants * rank,
            bytes_accessed=2 * width * (rows + tenants * rank),
            transcendentals=0,
        ),
        name="down_project",
    )(x, adapter, doc, tenant_of)


def owner_of(info, rank):
    return info[rank : rank + 1, :].astype(jnp.int32)


def turn_kernel(base, grad, up, base_t, grad_t, up_t, token):
    base_t[...] = base[...].T
    grad_t[...] = grad[...].T
    up_t[...] = up[...].T
    token[...] = jnp.zeros_like(token)


def turn_operands(base, grad, up, group):
    (rows, width), tall, span = base.shape, up.shape[0], group * HEAD
    flat = lambda r: pl.BlockSpec((r, span), lambda i: (0, i))
    high = lambda r: pl.BlockSpec((span, r), lambda i: (i, 0))
    shape = lambda r: jax.ShapeDtypeStruct((width, r), jnp.bfloat16)
    return pl.pallas_call(
        turn_kernel,
        grid=(width // span,),
        out_shape=[shape(rows), shape(rows), shape(tall), jax.ShapeDtypeStruct((8, HEAD), jnp.float32)],
        in_specs=[flat(rows), flat(rows), flat(tall)],
        out_specs=[high(rows), high(rows), high(tall), pl.BlockSpec((8, HEAD), lambda i: (0, 0))],
        compiler_params=params(VMEM_MOST),
        cost_estimate=pl.CostEstimate(
            flops=0, bytes_accessed=4 * width * (2 * rows + tall), transcendentals=0
        ),
        name="turn_operands",
    )(base, grad, up)


def turn(x):
    return x.astype(jnp.float32).T.astype(jnp.bfloat16)


def attention(
    head, at, count, group, turned, up, blocks, with_ids, info, terms, before, tenants, rank
):
    width, rows = turned[0].shape
    window = (REACH + 1) * rows
    tall = tenants * rank
    half = tall // 2
    span = group * HEAD
    pair = min(8, group)
    scale = HEAD**-0.5
    wide = lambda r: pl.BlockSpec((r, span), lambda i: (0, i + head))
    narrow = pl.BlockSpec((half, span), lambda i: (0, i))
    keys = pl.BlockSpec((rows, HEAD), lambda i: (0, i + at))
    skip = blocks[0].shape[1] // (2 * HEAD)
    values = pl.BlockSpec((rows, HEAD), lambda i: (0, i + at + skip))
    ids = pl.BlockSpec((TAIL, rows), lambda i: (rows // TAIL, 0))
    same = lambda a: pl.BlockSpec(a.shape, lambda i: (0, 0))
    high = lambda r: pl.BlockSpec((span, r), lambda i: (i + head, 0))
    operands, specs = [*turned, up], [high(rows), high(rows), high(tall), wide(tall)]
    for block in blocks:
        operands += [block, block]
        specs += [keys, values]
    operands += [*with_ids, info, *terms]
    specs += [ids] * 4 + [same(info)] * 3
    if before is not None:
        operands += [before[1], before[0]]
        specs += [same(before[1]), ANY]
    held = dict(
        kw=pltpu.VMEM((window, HEAD), jnp.bfloat16),
        vw=pltpu.VMEM((window, HEAD), jnp.bfloat16),
        kt=pltpu.VMEM((HEAD, window), jnp.bfloat16),
        vt=pltpu.VMEM((HEAD + TAIL, window), jnp.bfloat16),
        bottle_t=pltpu.VMEM((tall, rows), jnp.bfloat16),
        bias=pltpu.VMEM((window, rows), jnp.float32),
        query=pltpu.VMEM((span, rows), jnp.bfloat16),
        gquery=pltpu.VMEM((span, rows), jnp.bfloat16),
        scores=pltpu.VMEM((pair, window, rows), jnp.float32),
        part=pltpu.VMEM((tall, span), jnp.bfloat16),
        total=pltpu.VMEM((tall, rows), jnp.float32),
        reach=pltpu.SMEM((1,), jnp.int32),
    )

    def kernel(*refs):
        base, gt, up_t, up = refs[0:4]
        kv, tails, info, terms = refs[4:12], refs[12:16], refs[16], refs[17:19]
        out, keep, send, projected = refs[len(operands) : len(operands) + 4]
        r = dict(zip(held, refs[len(operands) + 4 :]))
        kw, vw, kt, vt = (r[n] for n in ("kw", "vw", "kt", "vt"))
        bias, query, gquery, scores = (r[n] for n in ("bias", "query", "gquery", "scores"))
        sub = lax.axis_index("sub")
        step = pl.program_id(0)

        @pl.when(step == 0)
        def _():
            owner = owner_of(info, rank)
            lifted = unfold((terms[0][...] + terms[1][...])[0:rank], owner, tenants, rank)
            r["bottle_t"][...] = lifted.astype(jnp.bfloat16)
            r["total"][...] = jnp.zeros((tall, rows), jnp.float32)
            vt[HEAD:, :] = jnp.ones((TAIL, window), jnp.bfloat16)
            own, two, swap, passed = (ref[...].astype(jnp.float32) for ref in tails)
            near = jnp.where(sub == 0, swap, passed)
            far = jnp.where(sub == 0, passed, swap)
            mine = own[0:1, :]
            lowest = jnp.min(mine)
            reach = 0
            for slot, block in ((REACH, own), (2, near), (1, two), (0, far)):
                same = block.T[:, 0:1] == mine
                if slot == REACH:
                    same = same & (
                        lax.broadcasted_iota(jnp.int32, (rows, rows), 0)
                        <= lax.broadcasted_iota(jnp.int32, (rows, rows), 1)
                    )
                else:
                    reach = jnp.where(jnp.max(block[0:1, :]) == lowest, REACH - slot, reach)
                bias[slot * rows : (slot + 1) * rows, :] = jnp.where(same, 0.0, NEG)
            r["reach"][0] = reach

        def place(slot, k_ref, v_ref):
            at = slice(slot * rows, (slot + 1) * rows)
            k, v = k_ref[...], v_ref[...]
            kw[at, :] = k
            vw[at, :] = v
            kt[:, at] = turn(k)
            vt[0:HEAD, at] = turn(v)

        place(REACH, *kv[0:2])
        place(1, *kv[2:4])

        @pl.when(sub == 0)
        def _():
            place(2, *kv[4:6])
            place(0, *kv[6:8])

        @pl.when(sub != 0)
        def _():
            place(2, *kv[6:8])
            place(0, *kv[4:6])

        lift = LIFT * nn(up_t[...], r["bottle_t"][...])
        query[...] = (base[...].astype(jnp.float32) + lift).astype(jnp.bfloat16)

        def run(reached, numbers):
            chunks = [slice(c * rows, (c + 1) * rows) for c in range(REACH - reached, REACH + 1)]
            spans = [pl.ds(pl.multiple_of(h * HEAD, HEAD), HEAD) for h in numbers]
            peaks = []
            for i, span_i in enumerate(spans):
                q, peak = query[span_i, :], None
                for c in chunks:
                    s = nn(kw[c, :], q) + bias[c, :]
                    scores[i, c, :] = s
                    top = jnp.max(s, axis=0, keepdims=True)
                    peak = top if peak is None else jnp.maximum(peak, top)
                peaks.append(peak)
            inverses, rowdots = [], []
            for i, span_i in enumerate(spans):
                total = None
                for c in chunks:
                    w = jnp.exp2((scores[i, c, :] - peaks[i]) * (scale * LOG2E))
                    scores[i, c, :] = w
                    o = nn(vt[:, c], w.astype(jnp.bfloat16))
                    total = o if total is None else total + o
                inverse = 1.0 / total[HEAD : HEAD + 1, :]
                attn = total[0:HEAD, :] * inverse
                out[:, span_i] = attn.T.astype(jnp.bfloat16)
                attn = attn.astype(jnp.bfloat16)
                product = gt[span_i, :].astype(jnp.float32) * attn.astype(jnp.float32)
                rowdots.append(jnp.sum(product, axis=0, keepdims=True))
                inverses.append(inverse)
            for i, span_i in enumerate(spans):
                g, moved = gt[span_i, :], None
                for c in chunks:
                    dprob = nn(vw[c, :], g)
                    ds = (scores[i, c, :] * (dprob - rowdots[i])).astype(jnp.bfloat16)
                    dq = nn(kt[:, c], ds)
                    moved = dq if moved is None else moved + dq
                gquery[span_i, :] = (moved * (inverses[i] * (LIFT * scale))).astype(jnp.bfloat16)

        for reached in (1, REACH):

            @pl.when((r["reach"][0] > 1) == (reached > 1))
            def _():
                @pl.loop(0, group // pair)
                def _(i):
                    run(reached, [i * pair + k for k in range(pair)])

        r["part"][...] = nt(r["bottle_t"][...], gquery[...]).astype(jnp.bfloat16)
        keep[...] = r["part"][pl.ds(pl.multiple_of(sub * half, half), half), :]
        send[...] = r["part"][pl.ds(pl.multiple_of((1 - sub) * half, half), half), :]
        r["total"][...] += nn(up[...], gquery[...])

        @pl.when(step == count - 1)
        def _():
            folded = fold(r["total"][...], owner_of(info, rank), tenants, rank)
            projected[...] = folded if before is None else folded + refs[19][...]

    return pl.pallas_call(
        kernel,
        grid=(count,),
        out_shape=[
            jax.ShapeDtypeStruct((rows, width), jnp.bfloat16),
            *halves_of(tall, count * span),
            jax.ShapeDtypeStruct((rank, rows), jnp.float32),
        ],
        in_specs=specs,
        out_specs=[wide(rows), narrow, narrow, pl.BlockSpec((rank, rows), lambda i: (0, 0))],
        scratch_shapes=list(held.values()),
        input_output_aliases={20: 0} if before is not None else {},
        compiler_params=params(VMEM_HEADS),
        cost_estimate=pl.CostEstimate(
            flops=8 * rows * window * span * count,
            bytes_accessed=6 * rows * span * count,
            transcendentals=rows * window * group * count,
        ),
        name="attention",
    )(*operands)


def small_call(kernel, name, shapes, *operands, after=(), through=(), scratch=()):
    size = sum(2 * a.size for a in operands)
    count, results = len(operands), jax.tree.leaves(shapes)
    given = (*operands, *after, *through)
    outs = len(given) + len(results)
    calls = pl.pallas_call(
        lambda *refs: kernel(
            *refs[:count], *refs[len(given) : outs], *refs[outs + len(through) :]
        ),
        out_shape=results + [jax.ShapeDtypeStruct(a.shape, a.dtype) for a in through],
        in_specs=[VM] * count + [ANY] * (len(after) + len(through)),
        out_specs=[VM] * len(results) + [ANY] * len(through),
        scratch_shapes=list(scratch),
        input_output_aliases={
            count + len(after) + i: len(results) + i for i in range(len(through))
        },
        compiler_params=params(),
        cost_estimate=pl.CostEstimate(flops=size, bytes_accessed=2 * size, transcendentals=0),
        name=name,
    )(*given)
    return calls if isinstance(shapes, list) or through else calls[0]


def grad_a_of(tenants, rank, one, other, info, x):
    g = unfold((one[...] + other[...]), owner_of(info[...], rank), tenants, rank)
    return nn(g.astype(jnp.bfloat16), x[...]).astype(jnp.bfloat16)


def grad_a_kernel(tenants, rank, one, other, info, x, out):
    out[...] = grad_a_of(tenants, rank, one, other, info, x)


def split_kernel(tenants, rank, one, other, info, x, keep, send):
    part = grad_a_of(tenants, rank, one, other, info, x)
    half = keep.shape[0]
    sub = lax.axis_index("sub")

    @pl.when(sub == 0)
    def _():
        keep[...] = part[0:half, :]
        send[...] = part[half:, :]

    @pl.when(sub != 0)
    def _():
        keep[...] = part[half:, :]
        send[...] = part[0:half, :]


def scatter_kernel(size, count, *refs):
    mine, *sends, total = refs[2 * count :]
    col = 0
    for keep, got in zip(refs[0 : 2 * count : 2], refs[1 : 2 * count : 2]):
        both = keep[...].astype(jnp.float32) + got[...].astype(jnp.float32)
        total[:, col : col + keep.shape[1]] = both.astype(jnp.bfloat16)
        col += keep.shape[1]
    me = lax.axis_index("seq")
    rows = mine.shape[0]
    for d, out in enumerate((mine, *sends)):
        at = pl.multiple_of(lax.rem(me + d, size) * rows, rows)
        out[...] = total[pl.ds(at, rows), :]


def sum_kernel(*refs):
    total = refs[0][...].astype(jnp.float32)
    for ref in refs[1:-1]:
        total = total + ref[...].astype(jnp.float32)
    refs[-1][...] = total.astype(jnp.bfloat16)


def gather_kernel(size, *refs):
    pieces, out, col = refs[:-1], refs[-1], 0
    me = lax.axis_index("seq")
    for first in range(0, len(pieces), size):
        rows, width = pieces[first].shape
        for d in range(size):
            at = pl.multiple_of(lax.rem(me + size - d, size) * rows, rows)
            out[pl.ds(at, rows), col : col + width] = pieces[first + d][...]
        col += width


def gather(*sums):
    size, rows = len(sums[0]), sums[0][0].shape[0]
    width = sum(pieces[0].shape[1] for pieces in sums)
    return small_call(
        functools.partial(gather_kernel, size), "gather_grads",
        jax.ShapeDtypeStruct((rows * size, width), jnp.bfloat16),
        *[piece for pieces in sums for piece in pieces],
    )


def finish_kernel(count, *refs):
    grad_b, grad_a = refs[2 * count :]
    sub = lax.axis_index("sub")
    half, wide = refs[0].shape[0], grad_b.shape[1]
    here = pl.ds(pl.multiple_of(sub * half, half), half)
    there = pl.ds(pl.multiple_of((1 - sub) * half, half), half)
    for at, group in ((here, refs[0 : 2 * count : 2]), (there, refs[1 : 2 * count : 2])):
        col = 0
        for ref in group:
            width = ref.shape[1]
            first = min(width, wide - col)
            grad_b[at, col : col + first] = ref[:, 0:first].astype(jnp.float32)
            if first < width:
                grad_a[at, :] = ref[:, first:].astype(jnp.float32)
            col += width


def finish(pairs, wide):
    rows, width = pairs[0][0].shape[0] * 2, sum(half.shape[1] for half, _ in pairs)
    return small_call(
        functools.partial(finish_kernel, len(pairs)), "finish_grads",
        [
            jax.ShapeDtypeStruct((rows, wide), jnp.float32),
            jax.ShapeDtypeStruct((rows, width - wide), jnp.float32),
        ],
        *[block for pair in pairs for block in pair],
    )


def halves_of(rows, width):
    return [jax.ShapeDtypeStruct((rows // 2, width), jnp.bfloat16)] * 2


def scatter(*pairs, after=()):
    size = lax.axis_size("seq")
    rows, width = pairs[0][0].shape[0], sum(keep.shape[1] for keep, _ in pairs)
    shard = jax.ShapeDtypeStruct((rows // size, width), jnp.bfloat16)
    return small_call(
        functools.partial(scatter_kernel, size, len(pairs)), "scatter_grads", [shard] * size,
        *[block for pair in pairs for block in pair],
        after=after, scratch=[pltpu.VMEM((rows, width), jnp.bfloat16)],
    )


def exchange(shards):
    return [shards[0]] + [rotate_over(block, "seq", d + 1) for d, block in enumerate(shards[1:])]


def add_up(pieces, after=(), through=()):
    shape = jax.ShapeDtypeStruct(pieces[0].shape, pieces[0].dtype)
    return small_call(sum_kernel, "sum_grads", shape, *pieces, after=after, through=through)


def spread(shard):
    return [shard] + [rotate_over(shard, "seq", d) for d in range(1, lax.axis_size("seq"))]


def swap_over(block, axis):
    return lax.ppermute(block, axis, [(0, 1), (1, 0)])


def rotate_over(block, axis, d):
    size = lax.axis_size(axis)
    return lax.ppermute(block, axis, [(i, (i + d) % size) for i in range(size)])


def terms_over(block, axis):
    if lax.axis_size(axis) == 2:
        return block, swap_over(block, axis)
    return lax.psum(block, axis), jnp.zeros_like(block)


def shift_over(block, axis):
    size = lax.axis_size(axis)
    return lax.ppermute(block, axis, [(i, i + 1) for i in range(size - 1)])


def body(
    normed_inputs, base_queries, base_keys, base_values, adapter_down, adapter_up,
    position_document, document_tenant, output_gradient,
):
    rows, width = normed_inputs.shape
    tenants, _, rank = adapter_down.shape
    tall, up_width = tenants * rank, adapter_up.shape[2]
    doc = position_document.reshape(1, rows)
    adapter = jnp.transpose(adapter_down, (0, 2, 1)).reshape(tall, width)
    up = adapter_up.reshape(tall, up_width)
    key_heads = base_keys.shape[1] // HEAD
    chunks = 2 if key_heads % 4 == 0 else 1
    size = lax.axis_size("seq")
    by_hand = chunks == 2 and tall % (2 * TAIL * size) == 0

    own = pack(base_keys, base_values, doc, chunks)
    info = down_project(normed_inputs, adapter, doc, document_tenant, tenants, rank)
    terms = terms_over(info, "mp")
    group = base_queries.shape[1] // HEAD // key_heads
    *turned, token = turn_operands(base_queries, output_gradient, up, group)
    per = key_heads // chunks
    counts = [1, per - 1, per] if chunks == 2 else [1] * per
    state, pairs, held, with_ids, head = None, [], [], None, 0
    for i, count in enumerate(counts):
        chunk = head // per
        if len(held) < chunks and i < 2:
            two = shift_over(own[i], "seq")
            passing, two = relay(own[i], two, [terms[1], token] if i == 0 else [pairs[0][0]])
            held.append((own[i], two, swap_over(two, "sub"), shift_over(passing, ("seq", "sub"))))
        with_ids = held[0]
        out, keep, send, gdown = attention(
            head, head % per, count, group, turned, up, held[chunk], with_ids,
            info, terms, state, tenants, rank,
        )
        state = (out, gdown)
        pairs.append((keep, send))
        head += count
    if by_hand:
        keep_late, send_late = pairs[-1]
        one, other = terms_over(gdown, "mp")
        swapped = [(keep, swap_over(send, "sub")) for keep, send in pairs[:-1]]
        pieces = exchange(scatter(*swapped, after=[keep_late]))
        early = add_up(pieces)
        keep_a, send_a = small_call(
            functools.partial(split_kernel, tenants, rank), "split_grads", halves_of(tall, width),
            one, other, info, normed_inputs, after=pieces[1:],
        )
        shards = scatter(
            (keep_late, swap_over(send_late, "sub")), (keep_a, swap_over(send_a, "sub"))
        )
        all_early = spread(early)
        late = add_up(exchange(shards), after=all_early[1:])
        half = gather(all_early, spread(late))
        grad_b, grad_a = finish([(half, swap_over(half, "sub"))], up_width)
    else:
        one, other = terms_over(gdown, "mp")
        part_a = small_call(
            functools.partial(grad_a_kernel, tenants, rank), "grad_a_part",
            jax.ShapeDtypeStruct((tall, width), jnp.bfloat16), one, other, info, normed_inputs,
        )
        grad_a = lax.psum(part_a, ("seq", "sub")).astype(jnp.float32)
        keeps = jnp.concatenate([keep for keep, _ in pairs], axis=1)
        sends = jnp.concatenate([send for _, send in pairs], axis=1)
        low = lax.axis_index("sub") == 0
        part_b = jnp.concatenate([jnp.where(low, keeps, sends), jnp.where(low, sends, keeps)])
        grad_b = lax.psum(part_b, ("seq", "sub")).astype(jnp.float32)
    grad_a = jnp.transpose(grad_a.reshape(tenants, rank, width), (0, 2, 1))
    return out, grad_a, grad_b.reshape(tenants, rank, up_width)


def solution(mesh):
    split = P(("rep", "seq", "sub"), "mp")
    in_specs = (
        split, split, split, split, P(None, "mp", None), P(None, None, "mp"),
        P(("rep", "seq", "sub")), P("rep"), split,
    )
    out_specs = (split, P("rep", "mp", None), P("rep", None, "mp"))
    return jax.shard_map(body, mesh=mesh, in_specs=in_specs, out_specs=out_specs, check_vma=False)
```

```python
import functools

import jax
import jax.numpy as jnp
from jax import lax
from jax.experimental import pallas as pl
from jax.experimental.pallas import tpu as pltpu
from jax.sharding import PartitionSpec as P

HEAD = 128
REACH = 3
NEG = -1e30
LIFT = 2.0
LOG2E = 1.4426950408889634
TAIL = 16
VMEM_BYTES = 48 * 1024 * 1024
VMEM_MOST = 60 * 1024 * 1024
VMEM_HEADS = 57 * 1024 * 1024
VMEM_RELAY = 59 * 1024 * 1024

VM = pl.BlockSpec(memory_space=pltpu.VMEM)
SM = pl.BlockSpec(memory_space=pltpu.SMEM)
ANY = pl.BlockSpec(memory_space=pl.ANY)


def nt(a, b):
    return lax.dot_general(a, b, (((1,), (1,)), ((), ())), preferred_element_type=jnp.float32)


def nn(a, b):
    return jnp.dot(a, b, preferred_element_type=jnp.float32)


def params(limit=VMEM_BYTES):
    return pltpu.CompilerParams(vmem_limit_bytes=limit)


def fetch(pairs, sems):
    copies = [pltpu.make_async_copy(src, dst, sems.at[i]) for i, (src, dst) in enumerate(pairs)]
    for copy in copies:
        copy.start()
    return copies


def pack_kernel(keys, values, doc, *rest):
    outs, (ids, blocks, sems) = rest[:-3], rest[-3:]
    rows, width = keys.shape
    part = width // len(outs)
    pairs = [(doc, ids)]
    for c in range(len(outs)):
        cols = pl.ds(c * part, part)
        pairs.append((keys.at[:, cols], blocks.at[c, pl.ds(0, rows), pl.ds(0, part)]))
        pairs.append((values.at[:, cols], blocks.at[c, pl.ds(0, rows), pl.ds(part, part)]))
    loads = fetch(pairs, sems.at[pl.ds(0, len(pairs))])
    loads[0].wait()
    tail = jnp.broadcast_to((ids[...] + 1).astype(jnp.float32), (TAIL, rows)).astype(jnp.bfloat16)
    stores = []
    for c, out in enumerate(outs):
        blocks[c, rows:, :] = jnp.zeros((TAIL, 2 * part), jnp.bfloat16)
        blocks[c, rows:, 0:rows] = tail
        loads[1 + 2 * c].wait()
        loads[2 + 2 * c].wait()
        stores += fetch([(blocks.at[c], out)], sems.at[pl.ds(len(pairs) + c, 1)])
    for store in stores:
        store.wait()


def pack(keys, values, doc, chunks):
    rows, width = keys.shape
    shape = (rows + TAIL, 2 * width // chunks)
    return pl.pallas_call(
        pack_kernel,
        out_shape=[jax.ShapeDtypeStruct(shape, jnp.bfloat16)] * chunks,
        in_specs=[ANY] * 3,
        out_specs=[ANY] * chunks,
        scratch_shapes=[
            pltpu.VMEM((1, rows), jnp.int32),
            pltpu.VMEM((chunks, *shape), jnp.bfloat16),
            pltpu.SemaphoreType.DMA((1 + 3 * chunks,)),
        ],
        compiler_params=params(VMEM_MOST),
        cost_estimate=pl.CostEstimate(flops=0, bytes_accessed=8 * rows * width, transcendentals=0),
        name="pack_keys_values",
    )(keys, values, doc)


def relay_kernel(own, got, after, out, got_out, held, sems):
    sub = lax.axis_index("sub")

    def move(source):
        load = pltpu.make_async_copy(source, held, sems.at[0])
        load.start()
        load.wait()

    @pl.when(sub == 0)
    def _():
        move(own)

    @pl.when(sub != 0)
    def _():
        move(got)

    store = pltpu.make_async_copy(held, out, sems.at[1])
    store.start()
    store.wait()


def relay(own, got, after):
    shape = jax.ShapeDtypeStruct(own.shape, own.dtype)
    return pl.pallas_call(
        relay_kernel,
        out_shape=[shape, shape],
        in_specs=[ANY, ANY, ANY],
        out_specs=[ANY, ANY],
        input_output_aliases={1: 1},
        scratch_shapes=[pltpu.VMEM(own.shape, own.dtype), pltpu.SemaphoreType.DMA((2,))],
        compiler_params=params(VMEM_RELAY),
        cost_estimate=pl.CostEstimate(flops=0, bytes_accessed=4 * own.size, transcendentals=0),
        name="relay_block",
    )(own, got, after)


def selector_of(owner, tenants, rank):
    rows = owner.shape[1]
    tenant = lax.broadcasted_iota(jnp.int32, (tenants * rank, rows), 0) // rank
    return tenant == owner


def fold(full, owner, tenants, rank):
    kept = jnp.where(selector_of(owner, tenants, rank), full, 0.0)
    total = kept[0:rank]
    for t in range(1, tenants):
        total = total + kept[t * rank : (t + 1) * rank]
    return total


def unfold(compact, owner, tenants, rank):
    spread = jnp.concatenate([compact] * tenants, axis=0)
    return jnp.where(selector_of(owner, tenants, rank), spread, 0.0)


def down_kernel(tenants, rank, x_hbm, adapter_hbm, doc_hbm, tenant_of, info, x, adapter, doc, sems):
    copies = fetch([(doc_hbm, doc), (x_hbm, x), (adapter_hbm, adapter)], sems)
    copies[0].wait()
    ids = doc[...]
    found = jnp.zeros(ids.shape, jnp.int32)
    for s in range(tenant_of.shape[0]):
        found = jnp.where(ids == s, tenant_of[s], found)
    info[rank:, :] = jnp.broadcast_to(found.astype(jnp.float32), (info.shape[0] - rank, ids.shape[1]))
    copies[1].wait()
    copies[2].wait()
    info[0:rank, :] = fold(nt(x[...], adapter[...]).T, found, tenants, rank)


def down_project(x, adapter, doc, tenant_of, tenants, rank):
    rows, width = x.shape
    return pl.pallas_call(
        functools.partial(down_kernel, tenants, rank),
        out_shape=jax.ShapeDtypeStruct((rank + 8, rows), jnp.float32),
        in_specs=[ANY, ANY, ANY, SM],
        out_specs=VM,
        scratch_shapes=[
            pltpu.VMEM(x.shape, x.dtype),
            pltpu.VMEM(adapter.shape, adapter.dtype),
            pltpu.VMEM(doc.shape, doc.dtype),
            pltpu.SemaphoreType.DMA((3,)),
        ],
        compiler_params=params(VMEM_MOST),
        cost_estimate=pl.CostEstimate(
            flops=2 * rows * width * tenants * rank,
            bytes_accessed=2 * width * (rows + tenants * rank),
            transcendentals=0,
        ),
        name="down_project",
    )(x, adapter, doc, tenant_of)


def owner_of(info, rank):
    return info[rank : rank + 1, :].astype(jnp.int32)


def turn(x):
    return x.astype(jnp.float32).T.astype(jnp.bfloat16)


def attention(
    head, at, count, group, base, grad, up, blocks, with_ids, info, terms, before, after, tenants, rank
):
    rows, width = base.shape
    window = (REACH + 1) * rows
    tall = tenants * rank
    half = tall // 2
    span = group * HEAD
    pair = min(8, group)
    scale = HEAD**-0.5
    wide = lambda r: pl.BlockSpec((r, span), lambda i: (0, i + head))
    narrow = pl.BlockSpec((half, span), lambda i: (0, i))
    keys = pl.BlockSpec((rows, HEAD), lambda i: (0, i + at))
    skip = blocks[0].shape[1] // (2 * HEAD)
    values = pl.BlockSpec((rows, HEAD), lambda i: (0, i + at + skip))
    ids = pl.BlockSpec((TAIL, rows), lambda i: (rows // TAIL, 0))
    same = lambda a: pl.BlockSpec(a.shape, lambda i: (0, 0))
    operands, specs = [base, grad, up], [wide(rows), wide(rows), wide(tall)]
    for block in blocks:
        operands += [block, block]
        specs += [keys, values]
    operands += [*with_ids, info, *terms]
    specs += [ids] * 4 + [same(info)] * 3
    if before is not None:
        operands += [before[1], before[0]]
        specs += [same(before[1]), ANY]
    operands += after
    specs += [ANY] * len(after)
    held = dict(
        kw=pltpu.VMEM((window, HEAD), jnp.bfloat16),
        vw=pltpu.VMEM((window, HEAD), jnp.bfloat16),
        kt=pltpu.VMEM((HEAD, window), jnp.bfloat16),
        vt=pltpu.VMEM((HEAD + TAIL, window), jnp.bfloat16),
        bottle=pltpu.VMEM((rows, tall), jnp.bfloat16),
        bottle_t=pltpu.VMEM((tall, rows), jnp.bfloat16),
        bias=pltpu.VMEM((window, rows), jnp.float32),
        query=pltpu.VMEM((span, rows), jnp.bfloat16),
        gt=pltpu.VMEM((span, rows), jnp.bfloat16),
        gquery=pltpu.VMEM((span, rows), jnp.bfloat16),
        scores=pltpu.VMEM((pair, window, rows), jnp.float32),
        part=pltpu.VMEM((tall, span), jnp.bfloat16),
        total=pltpu.VMEM((tall, rows), jnp.float32),
        reach=pltpu.SMEM((1,), jnp.int32),
    )

    def kernel(*refs):
        base, grad, up = refs[0:3]
        kv, tails, info, terms = refs[3:11], refs[11:15], refs[15], refs[16:18]
        out, keep, send, projected = refs[len(operands) : len(operands) + 4]
        r = dict(zip(held, refs[len(operands) + 4 :]))
        kw, vw, kt, vt = (r[n] for n in ("kw", "vw", "kt", "vt"))
        bias, query, gt, gquery, scores = (
            r[n] for n in ("bias", "query", "gt", "gquery", "scores")
        )
        sub = lax.axis_index("sub")
        step = pl.program_id(0)

        @pl.when(step == 0)
        def _():
            owner = owner_of(info, rank)
            lifted = unfold((terms[0][...] + terms[1][...])[0:rank], owner, tenants, rank)
            r["bottle_t"][...] = lifted.astype(jnp.bfloat16)
            r["bottle"][...] = lifted.T.astype(jnp.bfloat16)
            r["total"][...] = jnp.zeros((tall, rows), jnp.float32)
            vt[HEAD:, :] = jnp.ones((TAIL, window), jnp.bfloat16)
            own, two, swap, passed = (ref[...].astype(jnp.float32) for ref in tails)
            near = jnp.where(sub == 0, swap, passed)
            far = jnp.where(sub == 0, passed, swap)
            mine = own[0:1, :]
            lowest = jnp.min(mine)
            reach = 0
            for slot, block in ((REACH, own), (2, near), (1, two), (0, far)):
                same = block.T[:, 0:1] == mine
                if slot == REACH:
                    same = same & (
                        lax.broadcasted_iota(jnp.int32, (rows, rows), 0)
                        <= lax.broadcasted_iota(jnp.int32, (rows, rows), 1)
                    )
                else:
                    reach = jnp.where(jnp.max(block[0:1, :]) == lowest, REACH - slot, reach)
                bias[slot * rows : (slot + 1) * rows, :] = jnp.where(same, 0.0, NEG)
            r["reach"][0] = reach

        def place(slot, k_ref, v_ref):
            at = slice(slot * rows, (slot + 1) * rows)
            k, v = k_ref[...], v_ref[...]
            kw[at, :] = k
            vw[at, :] = v
            kt[:, at] = turn(k)
            vt[0:HEAD, at] = turn(v)

        place(REACH, *kv[0:2])
        place(1, *kv[2:4])

        @pl.when(sub == 0)
        def _():
            place(2, *kv[4:6])
            place(0, *kv[6:8])

        @pl.when(sub != 0)
        def _():
            place(2, *kv[6:8])
            place(0, *kv[4:6])

        lift = LIFT * nn(r["bottle"][...], up[...])
        query[...] = (base[...].astype(jnp.float32) + lift).T.astype(jnp.bfloat16)
        gt[...] = turn(grad[...])

        def run(reached, numbers):
            chunks = [slice(c * rows, (c + 1) * rows) for c in range(REACH - reached, REACH + 1)]
            spans = [pl.ds(pl.multiple_of(h * HEAD, HEAD), HEAD) for h in numbers]
            peaks = []
            for i, span_i in enumerate(spans):
                q, peak = query[span_i, :], None
                for c in chunks:
                    s = nn(kw[c, :], q) + bias[c, :]
                    scores[i, c, :] = s
                    top = jnp.max(s, axis=0, keepdims=True)
                    peak = top if peak is None else jnp.maximum(peak, top)
                peaks.append(peak)
            inverses, rowdots = [], []
            for i, span_i in enumerate(spans):
                total = None
                for c in chunks:
                    w = jnp.exp2((scores[i, c, :] - peaks[i]) * (scale * LOG2E))
                    scores[i, c, :] = w
                    o = nn(vt[:, c], w.astype(jnp.bfloat16))
                    total = o if total is None else total + o
                inverse = 1.0 / total[HEAD : HEAD + 1, :]
                attn = total[0:HEAD, :] * inverse
                out[:, span_i] = attn.T.astype(jnp.bfloat16)
                attn = attn.astype(jnp.bfloat16)
                product = gt[span_i, :].astype(jnp.float32) * attn.astype(jnp.float32)
                rowdots.append(jnp.sum(product, axis=0, keepdims=True))
                inverses.append(inverse)
            for i, span_i in enumerate(spans):
                g, moved = gt[span_i, :], None
                for c in chunks:
                    dprob = nn(vw[c, :], g)
                    ds = (scores[i, c, :] * (dprob - rowdots[i])).astype(jnp.bfloat16)
                    dq = nn(kt[:, c], ds)
                    moved = dq if moved is None else moved + dq
                gquery[span_i, :] = (moved * (inverses[i] * (LIFT * scale))).astype(jnp.bfloat16)

        for reached in (1, REACH):

            @pl.when((r["reach"][0] > 1) == (reached > 1))
            def _():
                @pl.loop(0, group // pair)
                def _(i):
                    run(reached, [i * pair + k for k in range(pair)])

        r["part"][...] = nt(r["bottle_t"][...], gquery[...]).astype(jnp.bfloat16)
        keep[...] = r["part"][pl.ds(pl.multiple_of(sub * half, half), half), :]
        send[...] = r["part"][pl.ds(pl.multiple_of((1 - sub) * half, half), half), :]
        r["total"][...] += nn(up[...], gquery[...])

        @pl.when(step == count - 1)
        def _():
            folded = fold(r["total"][...], owner_of(info, rank), tenants, rank)
            projected[...] = folded if before is None else folded + refs[18][...]

    return pl.pallas_call(
        kernel,
        grid=(count,),
        out_shape=[
            jax.ShapeDtypeStruct((rows, width), jnp.bfloat16),
            *halves_of(tall, count * span),
            jax.ShapeDtypeStruct((rank, rows), jnp.float32),
        ],
        in_specs=specs,
        out_specs=[wide(rows), narrow, narrow, pl.BlockSpec((rank, rows), lambda i: (0, 0))],
        scratch_shapes=list(held.values()),
        input_output_aliases={19: 0} if before is not None else {},
        compiler_params=params(VMEM_HEADS),
        cost_estimate=pl.CostEstimate(
            flops=8 * rows * window * span * count,
            bytes_accessed=6 * rows * span * count,
            transcendentals=rows * window * group * count,
        ),
        name="attention",
    )(*operands)


def small_call(kernel, name, shapes, *operands, after=(), through=(), scratch=()):
    size = sum(2 * a.size for a in operands)
    count, results = len(operands), jax.tree.leaves(shapes)
    given = (*operands, *after, *through)
    outs = len(given) + len(results)
    calls = pl.pallas_call(
        lambda *refs: kernel(
            *refs[:count], *refs[len(given) : outs], *refs[outs + len(through) :]
        ),
        out_shape=results + [jax.ShapeDtypeStruct(a.shape, a.dtype) for a in through],
        in_specs=[VM] * count + [ANY] * (len(after) + len(through)),
        out_specs=[VM] * len(results) + [ANY] * len(through),
        scratch_shapes=list(scratch),
        input_output_aliases={
            count + len(after) + i: len(results) + i for i in range(len(through))
        },
        compiler_params=params(),
        cost_estimate=pl.CostEstimate(flops=size, bytes_accessed=2 * size, transcendentals=0),
        name=name,
    )(*given)
    return calls if isinstance(shapes, list) or through else calls[0]


def grad_a_of(tenants, rank, one, other, info, x):
    g = unfold((one[...] + other[...]), owner_of(info[...], rank), tenants, rank)
    return nn(g.astype(jnp.bfloat16), x[...]).astype(jnp.bfloat16)


def grad_a_kernel(tenants, rank, one, other, info, x, out):
    out[...] = grad_a_of(tenants, rank, one, other, info, x)


def split_kernel(tenants, rank, one, other, info, x, keep, send):
    part = grad_a_of(tenants, rank, one, other, info, x)
    half = keep.shape[0]
    sub = lax.axis_index("sub")

    @pl.when(sub == 0)
    def _():
        keep[...] = part[0:half, :]
        send[...] = part[half:, :]

    @pl.when(sub != 0)
    def _():
        keep[...] = part[half:, :]
        send[...] = part[0:half, :]


def scatter_kernel(size, count, *refs):
    mine, *sends, total = refs[2 * count :]
    col = 0
    for keep, got in zip(refs[0 : 2 * count : 2], refs[1 : 2 * count : 2]):
        both = keep[...].astype(jnp.float32) + got[...].astype(jnp.float32)
        total[:, col : col + keep.shape[1]] = both.astype(jnp.bfloat16)
        col += keep.shape[1]
    me = lax.axis_index("seq")
    rows = mine.shape[0]
    for d, out in enumerate((mine, *sends)):
        at = pl.multiple_of(lax.rem(me + d, size) * rows, rows)
        out[...] = total[pl.ds(at, rows), :]


def sum_kernel(*refs):
    total = refs[0][...].astype(jnp.float32)
    for ref in refs[1:-1]:
        total = total + ref[...].astype(jnp.float32)
    refs[-1][...] = total.astype(jnp.bfloat16)


def gather_kernel(size, *refs):
    pieces, out, col = refs[:-1], refs[-1], 0
    me = lax.axis_index("seq")
    for first in range(0, len(pieces), size):
        rows, width = pieces[first].shape
        for d in range(size):
            at = pl.multiple_of(lax.rem(me + size - d, size) * rows, rows)
            out[pl.ds(at, rows), col : col + width] = pieces[first + d][...]
        col += width


def gather(*sums):
    size, rows = len(sums[0]), sums[0][0].shape[0]
    width = sum(pieces[0].shape[1] for pieces in sums)
    return small_call(
        functools.partial(gather_kernel, size), "gather_grads",
        jax.ShapeDtypeStruct((rows * size, width), jnp.bfloat16),
        *[piece for pieces in sums for piece in pieces],
    )


def finish_kernel(count, *refs):
    grad_b, grad_a = refs[2 * count :]
    sub = lax.axis_index("sub")
    half, wide = refs[0].shape[0], grad_b.shape[1]
    here = pl.ds(pl.multiple_of(sub * half, half), half)
    there = pl.ds(pl.multiple_of((1 - sub) * half, half), half)
    for at, group in ((here, refs[0 : 2 * count : 2]), (there, refs[1 : 2 * count : 2])):
        col = 0
        for ref in group:
            width = ref.shape[1]
            first = min(width, wide - col)
            grad_b[at, col : col + first] = ref[:, 0:first].astype(jnp.float32)
            if first < width:
                grad_a[at, :] = ref[:, first:].astype(jnp.float32)
            col += width


def finish(pairs, wide):
    rows, width = pairs[0][0].shape[0] * 2, sum(half.shape[1] for half, _ in pairs)
    return small_call(
        functools.partial(finish_kernel, len(pairs)), "finish_grads",
        [
            jax.ShapeDtypeStruct((rows, wide), jnp.float32),
            jax.ShapeDtypeStruct((rows, width - wide), jnp.float32),
        ],
        *[block for pair in pairs for block in pair],
    )


def halves_of(rows, width):
    return [jax.ShapeDtypeStruct((rows // 2, width), jnp.bfloat16)] * 2


def scatter(*pairs, after=()):
    size = lax.axis_size("seq")
    rows, width = pairs[0][0].shape[0], sum(keep.shape[1] for keep, _ in pairs)
    shard = jax.ShapeDtypeStruct((rows // size, width), jnp.bfloat16)
    return small_call(
        functools.partial(scatter_kernel, size, len(pairs)), "scatter_grads", [shard] * size,
        *[block for pair in pairs for block in pair],
        after=after, scratch=[pltpu.VMEM((rows, width), jnp.bfloat16)],
    )


def exchange(shards):
    return [shards[0]] + [rotate_over(block, "seq", d + 1) for d, block in enumerate(shards[1:])]


def add_up(pieces, after=(), through=()):
    shape = jax.ShapeDtypeStruct(pieces[0].shape, pieces[0].dtype)
    return small_call(sum_kernel, "sum_grads", shape, *pieces, after=after, through=through)


def spread(shard):
    return [shard] + [rotate_over(shard, "seq", d) for d in range(1, lax.axis_size("seq"))]


def swap_over(block, axis):
    return lax.ppermute(block, axis, [(0, 1), (1, 0)])


def rotate_over(block, axis, d):
    size = lax.axis_size(axis)
    return lax.ppermute(block, axis, [(i, (i + d) % size) for i in range(size)])


def terms_over(block, axis):
    if lax.axis_size(axis) == 2:
        return block, swap_over(block, axis)
    return lax.psum(block, axis), jnp.zeros_like(block)


def shift_over(block, axis):
    size = lax.axis_size(axis)
    return lax.ppermute(block, axis, [(i, i + 1) for i in range(size - 1)])


def body(
    normed_inputs, base_queries, base_keys, base_values, adapter_down, adapter_up,
    position_document, document_tenant, output_gradient,
):
    rows, width = normed_inputs.shape
    tenants, _, rank = adapter_down.shape
    tall, up_width = tenants * rank, adapter_up.shape[2]
    doc = position_document.reshape(1, rows)
    adapter = jnp.transpose(adapter_down, (0, 2, 1)).reshape(tall, width)
    up = adapter_up.reshape(tall, up_width)
    key_heads = base_keys.shape[1] // HEAD
    chunks = 2 if key_heads % 4 == 0 else 1
    size = lax.axis_size("seq")
    by_hand = chunks == 2 and tall % (2 * TAIL * size) == 0

    own = pack(base_keys, base_values, doc, chunks)
    info = down_project(normed_inputs, adapter, doc, document_tenant, tenants, rank)
    terms = terms_over(info, "mp")
    group = base_queries.shape[1] // HEAD // key_heads
    per = key_heads // chunks
    counts = [1, per - 1, per] if chunks == 2 else [1] * per
    state, pairs, held, with_ids, head, after = None, [], [], None, 0, []
    for i, count in enumerate(counts):
        chunk = head // per
        if len(held) < chunks and i < 2:
            two = shift_over(own[i], "seq")
            passing, two = relay(own[i], two, terms[1] if i == 0 else state[0])
            held.append((own[i], two, swap_over(two, "sub"), shift_over(passing, ("seq", "sub"))))
        with_ids = held[0]
        if by_hand and i == 2:
            shards = scatter(*[(keep, swap_over(send, "sub")) for keep, send in pairs])
            pieces, after = exchange(shards), shards[:1]
        out, keep, send, gdown = attention(
            head, head % per, count, group, base_queries, output_gradient, up, held[chunk],
            with_ids, info, terms, state, after, tenants, rank,
        )
        state = (out, gdown)
        pairs.append((keep, send))
        head += count
    if by_hand:
        early, gdown = add_up(pieces, through=[gdown])
        one, other = terms_over(gdown, "mp")
        all_early = spread(early)
        keep_a, send_a = small_call(
            functools.partial(split_kernel, tenants, rank), "split_grads", halves_of(tall, width),
            one, other, info, normed_inputs, after=all_early[1:2],
        )
        shards = scatter((keep, swap_over(send, "sub")), (keep_a, swap_over(send_a, "sub")))
        late = add_up(exchange(shards), after=all_early[2:])
        half = gather(all_early, spread(late))
        grad_b, grad_a = finish([(half, swap_over(half, "sub"))], up_width)
    else:
        one, other = terms_over(gdown, "mp")
        part_a = small_call(
            functools.partial(grad_a_kernel, tenants, rank), "grad_a_part",
            jax.ShapeDtypeStruct((tall, width), jnp.bfloat16), one, other, info, normed_inputs,
        )
        grad_a = lax.psum(part_a, ("seq", "sub")).astype(jnp.float32)
        keeps = jnp.concatenate([keep for keep, _ in pairs], axis=1)
        sends = jnp.concatenate([send for _, send in pairs], axis=1)
        low = lax.axis_index("sub") == 0
        part_b = jnp.concatenate([jnp.where(low, keeps, sends), jnp.where(low, sends, keeps)])
        grad_b = lax.psum(part_b, ("seq", "sub")).astype(jnp.float32)
    grad_a = jnp.transpose(grad_a.reshape(tenants, rank, width), (0, 2, 1))
    return out, grad_a, grad_b.reshape(tenants, rank, up_width)


def solution(mesh):
    split = P(("rep", "seq", "sub"), "mp")
    in_specs = (
        split, split, split, split, P(None, "mp", None), P(None, None, "mp"),
        P(("rep", "seq", "sub")), P("rep"), split,
    )
    out_specs = (split, P("rep", "mp", None), P("rep", None, "mp"))
    return jax.shard_map(body, mesh=mesh, in_specs=in_specs, out_specs=out_specs, check_vma=False)
```

```python
import functools

import jax
import jax.numpy as jnp
from jax import lax
from jax.experimental import pallas as pl
from jax.experimental.pallas import tpu as pltpu
from jax.sharding import PartitionSpec as P

HEAD = 128
REACH = 3
NEG = -1e30
LIFT = 2.0
LOG2E = 1.4426950408889634
TAIL = 16
VMEM_BYTES = 48 * 1024 * 1024
VMEM_MOST = 60 * 1024 * 1024
VMEM_HEADS = 48 * 1024 * 1024

VM = pl.BlockSpec(memory_space=pltpu.VMEM)
SM = pl.BlockSpec(memory_space=pltpu.SMEM)
ANY = pl.BlockSpec(memory_space=pl.ANY)


def nt(a, b):
    return lax.dot_general(a, b, (((1,), (1,)), ((), ())), preferred_element_type=jnp.float32)


def nn(a, b):
    return jnp.dot(a, b, preferred_element_type=jnp.float32)


def params(limit=VMEM_BYTES):
    return pltpu.CompilerParams(vmem_limit_bytes=limit)


def fetch(pairs, sems):
    copies = [pltpu.make_async_copy(src, dst, sems.at[i]) for i, (src, dst) in enumerate(pairs)]
    for copy in copies:
        copy.start()
    return copies


def pack_kernel(keys, values, doc, *rest):
    outs, (ids, blocks, sems) = rest[:-3], rest[-3:]
    rows, width = keys.shape
    part = width // len(outs)
    pairs = [(doc, ids)]
    for c in range(len(outs)):
        cols = pl.ds(c * part, part)
        pairs.append((keys.at[:, cols], blocks.at[c, pl.ds(0, rows), pl.ds(0, part)]))
        pairs.append((values.at[:, cols], blocks.at[c, pl.ds(0, rows), pl.ds(part, part)]))
    loads = fetch(pairs, sems.at[pl.ds(0, len(pairs))])
    loads[0].wait()
    tail = jnp.broadcast_to((ids[...] + 1).astype(jnp.float32), (TAIL, rows)).astype(jnp.bfloat16)
    stores = []
    for c, out in enumerate(outs):
        blocks[c, rows:, :] = jnp.zeros((TAIL, 2 * part), jnp.bfloat16)
        blocks[c, rows:, 0:rows] = tail
        loads[1 + 2 * c].wait()
        loads[2 + 2 * c].wait()
        stores += fetch([(blocks.at[c], out)], sems.at[pl.ds(len(pairs) + c, 1)])
    for store in stores:
        store.wait()


def pack(keys, values, doc, chunks):
    rows, width = keys.shape
    shape = (rows + TAIL, 2 * width // chunks)
    return pl.pallas_call(
        pack_kernel,
        out_shape=[jax.ShapeDtypeStruct(shape, jnp.bfloat16)] * chunks,
        in_specs=[ANY] * 3,
        out_specs=[ANY] * chunks,
        scratch_shapes=[
            pltpu.VMEM((1, rows), jnp.int32),
            pltpu.VMEM((chunks, *shape), jnp.bfloat16),
            pltpu.SemaphoreType.DMA((1 + 3 * chunks,)),
        ],
        compiler_params=params(VMEM_MOST),
        cost_estimate=pl.CostEstimate(flops=0, bytes_accessed=8 * rows * width, transcendentals=0),
        name="pack_keys_values",
    )(keys, values, doc)


def relay_kernel(own, got, after, out, got_out, held, sems):
    sub = lax.axis_index("sub")

    def move(source):
        load = pltpu.make_async_copy(source, held, sems.at[0])
        load.start()
        load.wait()

    @pl.when(sub == 0)
    def _():
        move(own)

    @pl.when(sub != 0)
    def _():
        move(got)

    store = pltpu.make_async_copy(held, out, sems.at[1])
    store.start()
    store.wait()


def relay(own, got, after):
    shape = jax.ShapeDtypeStruct(own.shape, own.dtype)
    return pl.pallas_call(
        relay_kernel,
        out_shape=[shape, shape],
        in_specs=[ANY, ANY, ANY],
        out_specs=[ANY, ANY],
        input_output_aliases={1: 1},
        scratch_shapes=[pltpu.VMEM(own.shape, own.dtype), pltpu.SemaphoreType.DMA((2,))],
        compiler_params=params(),
        cost_estimate=pl.CostEstimate(flops=0, bytes_accessed=4 * own.size, transcendentals=0),
        name="relay_block",
    )(own, got, after)


def selector_of(owner, tenants, rank):
    rows = owner.shape[1]
    tenant = lax.broadcasted_iota(jnp.int32, (tenants * rank, rows), 0) // rank
    return tenant == owner


def fold(full, owner, tenants, rank):
    kept = jnp.where(selector_of(owner, tenants, rank), full, 0.0)
    total = kept[0:rank]
    for t in range(1, tenants):
        total = total + kept[t * rank : (t + 1) * rank]
    return total


def unfold(compact, owner, tenants, rank):
    spread = jnp.concatenate([compact] * tenants, axis=0)
    return jnp.where(selector_of(owner, tenants, rank), spread, 0.0)


def down_kernel(tenants, rank, x_hbm, adapter_hbm, doc_hbm, tenant_of, info, x, adapter, doc, sems):
    copies = fetch([(doc_hbm, doc), (x_hbm, x), (adapter_hbm, adapter)], sems)
    copies[0].wait()
    ids = doc[...]
    found = jnp.zeros(ids.shape, jnp.int32)
    for s in range(tenant_of.shape[0]):
        found = jnp.where(ids == s, tenant_of[s], found)
    info[rank:, :] = jnp.broadcast_to(found.astype(jnp.float32), (info.shape[0] - rank, ids.shape[1]))
    copies[1].wait()
    copies[2].wait()
    info[0:rank, :] = fold(nt(x[...], adapter[...]).T, found, tenants, rank)


def down_project(x, adapter, doc, tenant_of, tenants, rank):
    rows, width = x.shape
    return pl.pallas_call(
        functools.partial(down_kernel, tenants, rank),
        out_shape=jax.ShapeDtypeStruct((rank + 8, rows), jnp.float32),
        in_specs=[ANY, ANY, ANY, SM],
        out_specs=VM,
        scratch_shapes=[
            pltpu.VMEM(x.shape, x.dtype),
            pltpu.VMEM(adapter.shape, adapter.dtype),
            pltpu.VMEM(doc.shape, doc.dtype),
            pltpu.SemaphoreType.DMA((3,)),
        ],
        compiler_params=params(VMEM_MOST),
        cost_estimate=pl.CostEstimate(
            flops=2 * rows * width * tenants * rank,
            bytes_accessed=2 * width * (rows + tenants * rank),
            transcendentals=0,
        ),
        name="down_project",
    )(x, adapter, doc, tenant_of)


def owner_of(info, rank):
    return info[rank : rank + 1, :].astype(jnp.int32)


def turn(x):
    return x.astype(jnp.float32).T.astype(jnp.bfloat16)


def attention(
    head, at, count, group, base, grad, up, blocks, with_ids, info, terms, before, tenants, rank
):
    rows, width = base.shape
    window = (REACH + 1) * rows
    tall = tenants * rank
    half = tall // 2
    span = group * HEAD
    pair = min(8, group)
    scale = HEAD**-0.5
    wide = lambda r: pl.BlockSpec((r, span), lambda i: (0, i + head))
    narrow = pl.BlockSpec((half, span), lambda i: (0, i))
    keys = pl.BlockSpec((rows, HEAD), lambda i: (0, i + at))
    skip = blocks[0].shape[1] // (2 * HEAD)
    values = pl.BlockSpec((rows, HEAD), lambda i: (0, i + at + skip))
    ids = pl.BlockSpec((TAIL, rows), lambda i: (rows // TAIL, 0))
    same = lambda a: pl.BlockSpec(a.shape, lambda i: (0, 0))
    operands, specs = [base, grad, up], [wide(rows), wide(rows), wide(tall)]
    for block in blocks:
        operands += [block, block]
        specs += [keys, values]
    operands += [*with_ids, info, *terms]
    specs += [ids] * 4 + [same(info)] * 3
    if before is not None:
        operands += [before[1], before[0]]
        specs += [same(before[1]), ANY]
    held = dict(
        kw=pltpu.VMEM((window, HEAD), jnp.bfloat16),
        vw=pltpu.VMEM((window, HEAD), jnp.bfloat16),
        kt=pltpu.VMEM((HEAD, window), jnp.bfloat16),
        vt=pltpu.VMEM((HEAD + TAIL, window), jnp.bfloat16),
        bottle=pltpu.VMEM((rows, tall), jnp.bfloat16),
        bottle_t=pltpu.VMEM((tall, rows), jnp.bfloat16),
        bias=pltpu.VMEM((window, rows), jnp.float32),
        query=pltpu.VMEM((span, rows), jnp.bfloat16),
        gt=pltpu.VMEM((span, rows), jnp.bfloat16),
        gquery=pltpu.VMEM((span, rows), jnp.bfloat16),
        scores=pltpu.VMEM((pair, window, rows), jnp.float32),
        part=pltpu.VMEM((tall, span), jnp.bfloat16),
        total=pltpu.VMEM((tall, rows), jnp.float32),
        reach=pltpu.SMEM((1,), jnp.int32),
    )

    def kernel(*refs):
        base, grad, up = refs[0:3]
        kv, tails, info, terms = refs[3:11], refs[11:15], refs[15], refs[16:18]
        out, keep, send, projected = refs[len(operands) : len(operands) + 4]
        r = dict(zip(held, refs[len(operands) + 4 :]))
        kw, vw, kt, vt = (r[n] for n in ("kw", "vw", "kt", "vt"))
        bias, query, gt, gquery, scores = (
            r[n] for n in ("bias", "query", "gt", "gquery", "scores")
        )
        sub = lax.axis_index("sub")
        step = pl.program_id(0)

        @pl.when(step == 0)
        def _():
            owner = owner_of(info, rank)
            lifted = unfold((terms[0][...] + terms[1][...])[0:rank], owner, tenants, rank)
            r["bottle_t"][...] = lifted.astype(jnp.bfloat16)
            r["bottle"][...] = lifted.T.astype(jnp.bfloat16)
            r["total"][...] = jnp.zeros((tall, rows), jnp.float32)
            vt[HEAD:, :] = jnp.ones((TAIL, window), jnp.bfloat16)
            own, two, swap, passed = (ref[...].astype(jnp.float32) for ref in tails)
            near = jnp.where(sub == 0, swap, passed)
            far = jnp.where(sub == 0, passed, swap)
            mine = own[0:1, :]
            lowest = jnp.min(mine)
            reach = 0
            for slot, block in ((REACH, own), (2, near), (1, two), (0, far)):
                same = block.T[:, 0:1] == mine
                if slot == REACH:
                    same = same & (
                        lax.broadcasted_iota(jnp.int32, (rows, rows), 0)
                        <= lax.broadcasted_iota(jnp.int32, (rows, rows), 1)
                    )
                else:
                    reach = jnp.where(jnp.max(block[0:1, :]) == lowest, REACH - slot, reach)
                bias[slot * rows : (slot + 1) * rows, :] = jnp.where(same, 0.0, NEG)
            r["reach"][0] = reach

        def place(slot, k_ref, v_ref):
            at = slice(slot * rows, (slot + 1) * rows)
            k, v = k_ref[...], v_ref[...]
            kw[at, :] = k
            vw[at, :] = v
            kt[:, at] = turn(k)
            vt[0:HEAD, at] = turn(v)

        place(REACH, *kv[0:2])
        place(1, *kv[2:4])

        @pl.when(sub == 0)
        def _():
            place(2, *kv[4:6])
            place(0, *kv[6:8])

        @pl.when(sub != 0)
        def _():
            place(2, *kv[6:8])
            place(0, *kv[4:6])

        lift = LIFT * nn(r["bottle"][...], up[...])
        query[...] = (base[...].astype(jnp.float32) + lift).T.astype(jnp.bfloat16)
        gt[...] = turn(grad[...])

        def run(reached, numbers):
            chunks = [slice(c * rows, (c + 1) * rows) for c in range(REACH - reached, REACH + 1)]
            spans = [pl.ds(pl.multiple_of(h * HEAD, HEAD), HEAD) for h in numbers]
            peaks = []
            for i, span_i in enumerate(spans):
                q, peak = query[span_i, :], None
                for c in chunks:
                    s = nn(kw[c, :], q) + bias[c, :]
                    scores[i, c, :] = s
                    top = jnp.max(s, axis=0, keepdims=True)
                    peak = top if peak is None else jnp.maximum(peak, top)
                peaks.append(peak)
            inverses, rowdots = [], []
            for i, span_i in enumerate(spans):
                total = None
                for c in chunks:
                    w = jnp.exp2((scores[i, c, :] - peaks[i]) * (scale * LOG2E))
                    scores[i, c, :] = w
                    o = nn(vt[:, c], w.astype(jnp.bfloat16))
                    total = o if total is None else total + o
                inverse = 1.0 / total[HEAD : HEAD + 1, :]
                attn = total[0:HEAD, :] * inverse
                out[:, span_i] = attn.T.astype(jnp.bfloat16)
                attn = attn.astype(jnp.bfloat16)
                product = gt[span_i, :].astype(jnp.float32) * attn.astype(jnp.float32)
                rowdots.append(jnp.sum(product, axis=0, keepdims=True))
                inverses.append(inverse)
            for i, span_i in enumerate(spans):
                g, moved = gt[span_i, :], None
                for c in chunks:
                    dprob = nn(vw[c, :], g)
                    ds = (scores[i, c, :] * (dprob - rowdots[i])).astype(jnp.bfloat16)
                    dq = nn(kt[:, c], ds)
                    moved = dq if moved is None else moved + dq
                gquery[span_i, :] = (moved * (inverses[i] * (LIFT * scale))).astype(jnp.bfloat16)

        for reached in (1, REACH):

            @pl.when((r["reach"][0] > 1) == (reached > 1))
            def _():
                @pl.loop(0, group // pair)
                def _(i):
                    run(reached, [i * pair + k for k in range(pair)])

        r["part"][...] = nt(r["bottle_t"][...], gquery[...]).astype(jnp.bfloat16)
        keep[...] = r["part"][pl.ds(pl.multiple_of(sub * half, half), half), :]
        send[...] = r["part"][pl.ds(pl.multiple_of((1 - sub) * half, half), half), :]
        r["total"][...] += nn(up[...], gquery[...])

        @pl.when(step == count - 1)
        def _():
            folded = fold(r["total"][...], owner_of(info, rank), tenants, rank)
            projected[...] = folded if before is None else folded + refs[18][...]

    return pl.pallas_call(
        kernel,
        grid=(count,),
        out_shape=[
            jax.ShapeDtypeStruct((rows, width), jnp.bfloat16),
            *halves_of(tall, count * span),
            jax.ShapeDtypeStruct((rank, rows), jnp.float32),
        ],
        in_specs=specs,
        out_specs=[wide(rows), narrow, narrow, pl.BlockSpec((rank, rows), lambda i: (0, 0))],
        scratch_shapes=list(held.values()),
        input_output_aliases={19: 0} if before is not None else {},
        compiler_params=params(VMEM_HEADS),
        cost_estimate=pl.CostEstimate(
            flops=8 * rows * window * span * count,
            bytes_accessed=6 * rows * span * count,
            transcendentals=rows * window * group * count,
        ),
        name="attention",
    )(*operands)


def small_call(kernel, name, shapes, *operands, after=(), through=(), scratch=()):
    size = sum(2 * a.size for a in operands)
    count, results = len(operands), jax.tree.leaves(shapes)
    given = (*operands, *after, *through)
    outs = len(given) + len(results)
    calls = pl.pallas_call(
        lambda *refs: kernel(
            *refs[:count], *refs[len(given) : outs], *refs[outs + len(through) :]
        ),
        out_shape=results + [jax.ShapeDtypeStruct(a.shape, a.dtype) for a in through],
        in_specs=[VM] * count + [ANY] * (len(after) + len(through)),
        out_specs=[VM] * len(results) + [ANY] * len(through),
        scratch_shapes=list(scratch),
        input_output_aliases={
            count + len(after) + i: len(results) + i for i in range(len(through))
        },
        compiler_params=params(),
        cost_estimate=pl.CostEstimate(flops=size, bytes_accessed=2 * size, transcendentals=0),
        name=name,
    )(*given)
    return calls if isinstance(shapes, list) or through else calls[0]


def grad_a_of(tenants, rank, one, other, info, x):
    g = unfold((one[...] + other[...]), owner_of(info[...], rank), tenants, rank)
    return nn(g.astype(jnp.bfloat16), x[...]).astype(jnp.bfloat16)


def grad_a_kernel(tenants, rank, one, other, info, x, out):
    out[...] = grad_a_of(tenants, rank, one, other, info, x)


def split_kernel(tenants, rank, one, other, info, x, keep, send):
    part = grad_a_of(tenants, rank, one, other, info, x)
    half = keep.shape[0]
    sub = lax.axis_index("sub")

    @pl.when(sub == 0)
    def _():
        keep[...] = part[0:half, :]
        send[...] = part[half:, :]

    @pl.when(sub != 0)
    def _():
        keep[...] = part[half:, :]
        send[...] = part[0:half, :]


def scatter_kernel(size, count, *refs):
    mine, *sends, total = refs[2 * count :]
    col = 0
    for keep, got in zip(refs[0 : 2 * count : 2], refs[1 : 2 * count : 2]):
        both = keep[...].astype(jnp.float32) + got[...].astype(jnp.float32)
        total[:, col : col + keep.shape[1]] = both.astype(jnp.bfloat16)
        col += keep.shape[1]
    me = lax.axis_index("seq")
    rows = mine.shape[0]
    for d, out in enumerate((mine, *sends)):
        at = pl.multiple_of(lax.rem(me + d, size) * rows, rows)
        out[...] = total[pl.ds(at, rows), :]


def sum_kernel(*refs):
    total = refs[0][...].astype(jnp.float32)
    for ref in refs[1:-1]:
        total = total + ref[...].astype(jnp.float32)
    refs[-1][...] = total.astype(jnp.bfloat16)


def gather_kernel(size, *refs):
    pieces, out, col = refs[:-1], refs[-1], 0
    me = lax.axis_index("seq")
    for first in range(0, len(pieces), size):
        rows, width = pieces[first].shape
        for d in range(size):
            at = pl.multiple_of(lax.rem(me + size - d, size) * rows, rows)
            out[pl.ds(at, rows), col : col + width] = pieces[first + d][...]
        col += width


def gather(*sums):
    size, rows = len(sums[0]), sums[0][0].shape[0]
    width = sum(pieces[0].shape[1] for pieces in sums)
    return small_call(
        functools.partial(gather_kernel, size), "gather_grads",
        jax.ShapeDtypeStruct((rows * size, width), jnp.bfloat16),
        *[piece for pieces in sums for piece in pieces],
    )


def finish_kernel(count, *refs):
    grad_b, grad_a = refs[2 * count :]
    sub = lax.axis_index("sub")
    half, wide = refs[0].shape[0], grad_b.shape[1]
    here = pl.ds(pl.multiple_of(sub * half, half), half)
    there = pl.ds(pl.multiple_of((1 - sub) * half, half), half)
    for at, group in ((here, refs[0 : 2 * count : 2]), (there, refs[1 : 2 * count : 2])):
        col = 0
        for ref in group:
            width = ref.shape[1]
            first = min(width, wide - col)
            grad_b[at, col : col + first] = ref[:, 0:first].astype(jnp.float32)
            if first < width:
                grad_a[at, :] = ref[:, first:].astype(jnp.float32)
            col += width


def finish(pairs, wide):
    rows, width = pairs[0][0].shape[0] * 2, sum(half.shape[1] for half, _ in pairs)
    return small_call(
        functools.partial(finish_kernel, len(pairs)), "finish_grads",
        [
            jax.ShapeDtypeStruct((rows, wide), jnp.float32),
            jax.ShapeDtypeStruct((rows, width - wide), jnp.float32),
        ],
        *[block for pair in pairs for block in pair],
    )


def halves_of(rows, width):
    return [jax.ShapeDtypeStruct((rows // 2, width), jnp.bfloat16)] * 2


def scatter(*pairs, after=()):
    size = lax.axis_size("seq")
    rows, width = pairs[0][0].shape[0], sum(keep.shape[1] for keep, _ in pairs)
    shard = jax.ShapeDtypeStruct((rows // size, width), jnp.bfloat16)
    return small_call(
        functools.partial(scatter_kernel, size, len(pairs)), "scatter_grads", [shard] * size,
        *[block for pair in pairs for block in pair],
        after=after, scratch=[pltpu.VMEM((rows, width), jnp.bfloat16)],
    )


def exchange(shards):
    return [shards[0]] + [rotate_over(block, "seq", d + 1) for d, block in enumerate(shards[1:])]


def add_up(pieces, after=(), through=()):
    shape = jax.ShapeDtypeStruct(pieces[0].shape, pieces[0].dtype)
    return small_call(sum_kernel, "sum_grads", shape, *pieces, after=after, through=through)


def spread(shard):
    return [shard] + [rotate_over(shard, "seq", d) for d in range(1, lax.axis_size("seq"))]


def swap_over(block, axis):
    return lax.ppermute(block, axis, [(0, 1), (1, 0)])


def rotate_over(block, axis, d):
    size = lax.axis_size(axis)
    return lax.ppermute(block, axis, [(i, (i + d) % size) for i in range(size)])


def terms_over(block, axis):
    if lax.axis_size(axis) == 2:
        return block, swap_over(block, axis)
    return lax.psum(block, axis), jnp.zeros_like(block)


def shift_over(block, axis):
    size = lax.axis_size(axis)
    return lax.ppermute(block, axis, [(i, i + 1) for i in range(size - 1)])


def body(
    normed_inputs, base_queries, base_keys, base_values, adapter_down, adapter_up,
    position_document, document_tenant, output_gradient,
):
    rows, width = normed_inputs.shape
    tenants, _, rank = adapter_down.shape
    tall, up_width = tenants * rank, adapter_up.shape[2]
    doc = position_document.reshape(1, rows)
    adapter = jnp.transpose(adapter_down, (0, 2, 1)).reshape(tall, width)
    up = adapter_up.reshape(tall, up_width)
    key_heads = base_keys.shape[1] // HEAD
    chunks = 2 if key_heads % 4 == 0 else 1
    size = lax.axis_size("seq")
    by_hand = chunks == 2 and tall % (2 * TAIL * size) == 0

    own = pack(base_keys, base_values, doc, chunks)
    info = down_project(normed_inputs, adapter, doc, document_tenant, tenants, rank)
    terms = terms_over(info, "mp")
    group = base_queries.shape[1] // HEAD // key_heads
    per = key_heads // chunks
    counts = [1, per - 1, per] if chunks == 2 else [1] * per
    state, pairs, held, with_ids, head = None, [], [], None, 0
    for i, count in enumerate(counts):
        chunk = head // per
        if len(held) < chunks and i < 2:
            two = shift_over(own[i], "seq")
            passing, two = relay(own[i], two, terms[1] if i == 0 else state[1])
            held.append((own[i], two, swap_over(two, "sub"), shift_over(passing, ("seq", "sub"))))
        with_ids = held[0]
        out, keep, send, gdown = attention(
            head, head % per, count, group, base_queries, output_gradient, up, held[chunk],
            with_ids, info, terms, state, tenants, rank,
        )
        state = (out, gdown)
        pairs.append((keep, send))
        head += count
    if by_hand:
        one, other = terms_over(gdown, "mp")
        swapped = [(keep, swap_over(send, "sub")) for keep, send in pairs]
        keep, send = small_call(
            functools.partial(split_kernel, tenants, rank), "split_grads", halves_of(tall, width),
            one, other, info, normed_inputs, after=[got for _, got in swapped],
        )
        shards = scatter(*swapped, (keep, swap_over(send, "sub")))
        half = gather(spread(add_up(exchange(shards))))
        grad_b, grad_a = finish([(half, swap_over(half, "sub"))], up_width)
    else:
        one, other = terms_over(gdown, "mp")
        part_a = small_call(
            functools.partial(grad_a_kernel, tenants, rank), "grad_a_part",
            jax.ShapeDtypeStruct((tall, width), jnp.bfloat16), one, other, info, normed_inputs,
        )
        grad_a = lax.psum(part_a, ("seq", "sub")).astype(jnp.float32)
        keeps = jnp.concatenate([keep for keep, _ in pairs], axis=1)
        sends = jnp.concatenate([send for _, send in pairs], axis=1)
        low = lax.axis_index("sub") == 0
        part_b = jnp.concatenate([jnp.where(low, keeps, sends), jnp.where(low, sends, keeps)])
        grad_b = lax.psum(part_b, ("seq", "sub")).astype(jnp.float32)
    grad_a = jnp.transpose(grad_a.reshape(tenants, rank, width), (0, 2, 1))
    return out, grad_a, grad_b.reshape(tenants, rank, up_width)


def solution(mesh):
    split = P(("rep", "seq", "sub"), "mp")
    in_specs = (
        split, split, split, split, P(None, "mp", None), P(None, None, "mp"),
        P(("rep", "seq", "sub")), P("rep"), split,
    )
    out_specs = (split, P("rep", "mp", None), P("rep", None, "mp"))
    return jax.shard_map(body, mesh=mesh, in_specs=in_specs, out_specs=out_specs, check_vma=False)
```

```python
import functools

import jax
import jax.numpy as jnp
from jax import lax
from jax.experimental import pallas as pl
from jax.experimental.pallas import tpu as pltpu
from jax.sharding import PartitionSpec as P

HEAD = 128
REACH = 3
NEG = -1e30
LIFT = 2.0
LOG2E = 1.4426950408889634
TAIL = 16
VMEM_BYTES = 48 * 1024 * 1024
VMEM_MOST = 60 * 1024 * 1024
VMEM_HEADS = 48 * 1024 * 1024

VM = pl.BlockSpec(memory_space=pltpu.VMEM)
SM = pl.BlockSpec(memory_space=pltpu.SMEM)
ANY = pl.BlockSpec(memory_space=pl.ANY)


def nt(a, b):
    return lax.dot_general(a, b, (((1,), (1,)), ((), ())), preferred_element_type=jnp.float32)


def nn(a, b):
    return jnp.dot(a, b, preferred_element_type=jnp.float32)


def params(limit=VMEM_BYTES):
    return pltpu.CompilerParams(vmem_limit_bytes=limit)


def fetch(pairs, sems):
    copies = [pltpu.make_async_copy(src, dst, sems.at[i]) for i, (src, dst) in enumerate(pairs)]
    for copy in copies:
        copy.start()
    return copies


def pack_kernel(keys, values, doc, *rest):
    outs, (ids, blocks, sems) = rest[:-3], rest[-3:]
    rows, width = keys.shape
    part = width // len(outs)
    pairs = [(doc, ids)]
    for c in range(len(outs)):
        cols = pl.ds(c * part, part)
        pairs.append((keys.at[:, cols], blocks.at[c, pl.ds(0, rows), pl.ds(0, part)]))
        pairs.append((values.at[:, cols], blocks.at[c, pl.ds(0, rows), pl.ds(part, part)]))
    loads = fetch(pairs, sems.at[pl.ds(0, len(pairs))])
    loads[0].wait()
    tail = jnp.broadcast_to((ids[...] + 1).astype(jnp.float32), (TAIL, rows)).astype(jnp.bfloat16)
    stores = []
    for c, out in enumerate(outs):
        blocks[c, rows:, :] = jnp.zeros((TAIL, 2 * part), jnp.bfloat16)
        blocks[c, rows:, 0:rows] = tail
        loads[1 + 2 * c].wait()
        loads[2 + 2 * c].wait()
        stores += fetch([(blocks.at[c], out)], sems.at[pl.ds(len(pairs) + c, 1)])
    for store in stores:
        store.wait()


def pack(keys, values, doc, chunks):
    rows, width = keys.shape
    shape = (rows + TAIL, 2 * width // chunks)
    return pl.pallas_call(
        pack_kernel,
        out_shape=[jax.ShapeDtypeStruct(shape, jnp.bfloat16)] * chunks,
        in_specs=[ANY] * 3,
        out_specs=[ANY] * chunks,
        scratch_shapes=[
            pltpu.VMEM((1, rows), jnp.int32),
            pltpu.VMEM((chunks, *shape), jnp.bfloat16),
            pltpu.SemaphoreType.DMA((1 + 3 * chunks,)),
        ],
        compiler_params=params(VMEM_MOST),
        cost_estimate=pl.CostEstimate(flops=0, bytes_accessed=8 * rows * width, transcendentals=0),
        name="pack_keys_values",
    )(keys, values, doc)


def relay_kernel(own, got, after, out, got_out, held, sems):
    sub = lax.axis_index("sub")

    def move(source):
        load = pltpu.make_async_copy(source, held, sems.at[0])
        load.start()
        load.wait()

    @pl.when(sub == 0)
    def _():
        move(own)

    @pl.when(sub != 0)
    def _():
        move(got)

    store = pltpu.make_async_copy(held, out, sems.at[1])
    store.start()
    store.wait()


def relay(own, got, after):
    shape = jax.ShapeDtypeStruct(own.shape, own.dtype)
    return pl.pallas_call(
        relay_kernel,
        out_shape=[shape, shape],
        in_specs=[ANY, ANY, ANY],
        out_specs=[ANY, ANY],
        input_output_aliases={1: 1},
        scratch_shapes=[pltpu.VMEM(own.shape, own.dtype), pltpu.SemaphoreType.DMA((2,))],
        compiler_params=params(),
        cost_estimate=pl.CostEstimate(flops=0, bytes_accessed=4 * own.size, transcendentals=0),
        name="relay_block",
    )(own, got, after)


def selector_of(owner, tenants, rank):
    rows = owner.shape[1]
    tenant = lax.broadcasted_iota(jnp.int32, (tenants * rank, rows), 0) // rank
    return tenant == owner


def fold(full, owner, tenants, rank):
    kept = jnp.where(selector_of(owner, tenants, rank), full, 0.0)
    total = kept[0:rank]
    for t in range(1, tenants):
        total = total + kept[t * rank : (t + 1) * rank]
    return total


def unfold(compact, owner, tenants, rank):
    spread = jnp.concatenate([compact] * tenants, axis=0)
    return jnp.where(selector_of(owner, tenants, rank), spread, 0.0)


def down_kernel(tenants, rank, x_hbm, adapter_hbm, doc_hbm, tenant_of, info, x, adapter, doc, sems):
    copies = fetch([(doc_hbm, doc), (x_hbm, x), (adapter_hbm, adapter)], sems)
    copies[0].wait()
    ids = doc[...]
    found = jnp.zeros(ids.shape, jnp.int32)
    for s in range(tenant_of.shape[0]):
        found = jnp.where(ids == s, tenant_of[s], found)
    info[rank:, :] = jnp.broadcast_to(found.astype(jnp.float32), (info.shape[0] - rank, ids.shape[1]))
    copies[1].wait()
    copies[2].wait()
    info[0:rank, :] = fold(nt(x[...], adapter[...]).T, found, tenants, rank)


def down_project(x, adapter, doc, tenant_of, tenants, rank):
    rows, width = x.shape
    return pl.pallas_call(
        functools.partial(down_kernel, tenants, rank),
        out_shape=jax.ShapeDtypeStruct((rank + 8, rows), jnp.float32),
        in_specs=[ANY, ANY, ANY, SM],
        out_specs=VM,
        scratch_shapes=[
            pltpu.VMEM(x.shape, x.dtype),
            pltpu.VMEM(adapter.shape, adapter.dtype),
            pltpu.VMEM(doc.shape, doc.dtype),
            pltpu.SemaphoreType.DMA((3,)),
        ],
        compiler_params=params(VMEM_MOST),
        cost_estimate=pl.CostEstimate(
            flops=2 * rows * width * tenants * rank,
            bytes_accessed=2 * width * (rows + tenants * rank),
            transcendentals=0,
        ),
        name="down_project",
    )(x, adapter, doc, tenant_of)


def owner_of(info, rank):
    return info[rank : rank + 1, :].astype(jnp.int32)


def turn(x):
    return x.astype(jnp.float32).T.astype(jnp.bfloat16)


def attention(
    head, at, count, group, base, grad, up, blocks, with_ids, info, before, tenants, rank
):
    rows, width = base.shape
    window = (REACH + 1) * rows
    tall = tenants * rank
    half = tall // 2
    span = group * HEAD
    pair = min(8, group)
    scale = HEAD**-0.5
    wide = lambda r: pl.BlockSpec((r, span), lambda i: (0, i + head))
    narrow = pl.BlockSpec((half, span), lambda i: (0, i))
    keys = pl.BlockSpec((rows, HEAD), lambda i: (0, i + at))
    skip = blocks[0].shape[1] // (2 * HEAD)
    values = pl.BlockSpec((rows, HEAD), lambda i: (0, i + at + skip))
    ids = pl.BlockSpec((TAIL, rows), lambda i: (rows // TAIL, 0))
    same = lambda a: pl.BlockSpec(a.shape, lambda i: (0, 0))
    operands, specs = [base, grad, up], [wide(rows), wide(rows), wide(tall)]
    for block in blocks:
        operands += [block, block]
        specs += [keys, values]
    operands += [*with_ids, info]
    specs += [ids] * 4 + [same(info)]
    if before is not None:
        operands += [before[1], before[0]]
        specs += [same(before[1]), ANY]
    held = dict(
        kw=pltpu.VMEM((window, HEAD), jnp.bfloat16),
        vw=pltpu.VMEM((window, HEAD), jnp.bfloat16),
        kt=pltpu.VMEM((HEAD, window), jnp.bfloat16),
        vt=pltpu.VMEM((HEAD + TAIL, window), jnp.bfloat16),
        bottle=pltpu.VMEM((rows, tall), jnp.bfloat16),
        bottle_t=pltpu.VMEM((tall, rows), jnp.bfloat16),
        bias=pltpu.VMEM((window, rows), jnp.float32),
        query=pltpu.VMEM((span, rows), jnp.bfloat16),
        gt=pltpu.VMEM((span, rows), jnp.bfloat16),
        gquery=pltpu.VMEM((span, rows), jnp.bfloat16),
        scores=pltpu.VMEM((pair, window, rows), jnp.float32),
        part=pltpu.VMEM((tall, span), jnp.bfloat16),
        total=pltpu.VMEM((tall, rows), jnp.float32),
        reach=pltpu.SMEM((1,), jnp.int32),
    )

    def kernel(*refs):
        base, grad, up = refs[0:3]
        kv, tails, info = refs[3:11], refs[11:15], refs[15]
        out, keep, send, projected = refs[len(operands) : len(operands) + 4]
        r = dict(zip(held, refs[len(operands) + 4 :]))
        kw, vw, kt, vt = (r[n] for n in ("kw", "vw", "kt", "vt"))
        bias, query, gt, gquery, scores = (
            r[n] for n in ("bias", "query", "gt", "gquery", "scores")
        )
        sub = lax.axis_index("sub")
        step = pl.program_id(0)

        @pl.when(step == 0)
        def _():
            owner = owner_of(info, rank)
            lifted = unfold(info[0:rank, :], owner, tenants, rank)
            r["bottle_t"][...] = lifted.astype(jnp.bfloat16)
            r["bottle"][...] = lifted.T.astype(jnp.bfloat16)
            r["total"][...] = jnp.zeros((tall, rows), jnp.float32)
            vt[HEAD:, :] = jnp.ones((TAIL, window), jnp.bfloat16)
            own, two, swap, passed = (ref[...].astype(jnp.float32) for ref in tails)
            near = jnp.where(sub == 0, swap, passed)
            far = jnp.where(sub == 0, passed, swap)
            mine = own[0:1, :]
            lowest = jnp.min(mine)
            reach = 0
            for slot, block in ((REACH, own), (2, near), (1, two), (0, far)):
                same = block.T[:, 0:1] == mine
                if slot == REACH:
                    same = same & (
                        lax.broadcasted_iota(jnp.int32, (rows, rows), 0)
                        <= lax.broadcasted_iota(jnp.int32, (rows, rows), 1)
                    )
                else:
                    reach = jnp.where(jnp.max(block[0:1, :]) == lowest, REACH - slot, reach)
                bias[slot * rows : (slot + 1) * rows, :] = jnp.where(same, 0.0, NEG)
            r["reach"][0] = reach

        def place(slot, k_ref, v_ref):
            at = slice(slot * rows, (slot + 1) * rows)
            k, v = k_ref[...], v_ref[...]
            kw[at, :] = k
            vw[at, :] = v
            kt[:, at] = turn(k)
            vt[0:HEAD, at] = turn(v)

        place(REACH, *kv[0:2])
        place(1, *kv[2:4])

        @pl.when(sub == 0)
        def _():
            place(2, *kv[4:6])
            place(0, *kv[6:8])

        @pl.when(sub != 0)
        def _():
            place(2, *kv[6:8])
            place(0, *kv[4:6])

        lift = LIFT * nn(r["bottle"][...], up[...])
        query[...] = (base[...].astype(jnp.float32) + lift).T.astype(jnp.bfloat16)
        gt[...] = turn(grad[...])

        def run(reached, numbers):
            chunks = [slice(c * rows, (c + 1) * rows) for c in range(REACH - reached, REACH + 1)]
            spans = [pl.ds(pl.multiple_of(h * HEAD, HEAD), HEAD) for h in numbers]
            peaks = []
            for i, span_i in enumerate(spans):
                q, peak = query[span_i, :], None
                for c in chunks:
                    s = nn(kw[c, :], q) + bias[c, :]
                    scores[i, c, :] = s
                    top = jnp.max(s, axis=0, keepdims=True)
                    peak = top if peak is None else jnp.maximum(peak, top)
                peaks.append(peak)
            inverses, rowdots = [], []
            for i, span_i in enumerate(spans):
                total = None
                for c in chunks:
                    w = jnp.exp2((scores[i, c, :] - peaks[i]) * (scale * LOG2E))
                    scores[i, c, :] = w
                    o = nn(vt[:, c], w.astype(jnp.bfloat16))
                    total = o if total is None else total + o
                inverse = 1.0 / total[HEAD : HEAD + 1, :]
                attn = total[0:HEAD, :] * inverse
                out[:, span_i] = attn.T.astype(jnp.bfloat16)
                attn = attn.astype(jnp.bfloat16)
                product = gt[span_i, :].astype(jnp.float32) * attn.astype(jnp.float32)
                rowdots.append(jnp.sum(product, axis=0, keepdims=True))
                inverses.append(inverse)
            for i, span_i in enumerate(spans):
                g, moved = gt[span_i, :], None
                for c in chunks:
                    dprob = nn(vw[c, :], g)
                    ds = (scores[i, c, :] * (dprob - rowdots[i])).astype(jnp.bfloat16)
                    dq = nn(kt[:, c], ds)
                    moved = dq if moved is None else moved + dq
                gquery[span_i, :] = (moved * (inverses[i] * (LIFT * scale))).astype(jnp.bfloat16)

        for reached in (1, REACH):

            @pl.when((r["reach"][0] > 1) == (reached > 1))
            def _():
                @pl.loop(0, group // pair)
                def _(i):
                    run(reached, [i * pair + k for k in range(pair)])

        r["part"][...] = nt(r["bottle_t"][...], gquery[...]).astype(jnp.bfloat16)
        keep[...] = r["part"][pl.ds(pl.multiple_of(sub * half, half), half), :]
        send[...] = r["part"][pl.ds(pl.multiple_of((1 - sub) * half, half), half), :]
        r["total"][...] += nn(up[...], gquery[...])

        @pl.when(step == count - 1)
        def _():
            folded = fold(r["total"][...], owner_of(info, rank), tenants, rank)
            projected[...] = folded if before is None else folded + refs[16][...]

    return pl.pallas_call(
        kernel,
        grid=(count,),
        out_shape=[
            jax.ShapeDtypeStruct((rows, width), jnp.bfloat16),
            *halves_of(tall, count * span),
            jax.ShapeDtypeStruct((rank, rows), jnp.float32),
        ],
        in_specs=specs,
        out_specs=[wide(rows), narrow, narrow, pl.BlockSpec((rank, rows), lambda i: (0, 0))],
        scratch_shapes=list(held.values()),
        input_output_aliases={17: 0} if before is not None else {},
        compiler_params=params(VMEM_HEADS),
        cost_estimate=pl.CostEstimate(
            flops=8 * rows * window * span * count,
            bytes_accessed=6 * rows * span * count,
            transcendentals=rows * window * group * count,
        ),
        name="attention",
    )(*operands)


def small_call(kernel, name, shapes, *operands, after=(), through=(), scratch=()):
    size = sum(2 * a.size for a in operands)
    count, results = len(operands), jax.tree.leaves(shapes)
    given = (*operands, *after, *through)
    outs = len(given) + len(results)
    calls = pl.pallas_call(
        lambda *refs: kernel(
            *refs[:count], *refs[len(given) : outs], *refs[outs + len(through) :]
        ),
        out_shape=results + [jax.ShapeDtypeStruct(a.shape, a.dtype) for a in through],
        in_specs=[VM] * count + [ANY] * (len(after) + len(through)),
        out_specs=[VM] * len(results) + [ANY] * len(through),
        scratch_shapes=list(scratch),
        input_output_aliases={
            count + len(after) + i: len(results) + i for i in range(len(through))
        },
        compiler_params=params(),
        cost_estimate=pl.CostEstimate(flops=size, bytes_accessed=2 * size, transcendentals=0),
        name=name,
    )(*given)
    return calls if isinstance(shapes, list) or through else calls[0]


def join_kernel(rank, info, one, other, out):
    out[0:rank, :] = one[0:rank, :] + other[0:rank, :]
    out[rank:, :] = info[rank:, :]


def grad_a_of(tenants, rank, one, other, info, x):
    g = unfold((one[...] + other[...]), owner_of(info[...], rank), tenants, rank)
    return nn(g.astype(jnp.bfloat16), x[...]).astype(jnp.bfloat16)


def grad_a_kernel(tenants, rank, one, other, info, x, out):
    out[...] = grad_a_of(tenants, rank, one, other, info, x)


def split_kernel(tenants, rank, one, other, info, x, keep, send):
    part = grad_a_of(tenants, rank, one, other, info, x)
    half = keep.shape[0]
    sub = lax.axis_index("sub")

    @pl.when(sub == 0)
    def _():
        keep[...] = part[0:half, :]
        send[...] = part[half:, :]

    @pl.when(sub != 0)
    def _():
        keep[...] = part[half:, :]
        send[...] = part[0:half, :]


def scatter_kernel(size, count, *refs):
    mine, *sends, total = refs[2 * count :]
    col = 0
    for keep, got in zip(refs[0 : 2 * count : 2], refs[1 : 2 * count : 2]):
        both = keep[...].astype(jnp.float32) + got[...].astype(jnp.float32)
        total[:, col : col + keep.shape[1]] = both.astype(jnp.bfloat16)
        col += keep.shape[1]
    me = lax.axis_index("seq")
    rows = mine.shape[0]
    for d, out in enumerate((mine, *sends)):
        at = pl.multiple_of(lax.rem(me + d, size) * rows, rows)
        out[...] = total[pl.ds(at, rows), :]


def sum_kernel(*refs):
    total = refs[0][...].astype(jnp.float32)
    for ref in refs[1:-1]:
        total = total + ref[...].astype(jnp.float32)
    refs[-1][...] = total.astype(jnp.bfloat16)


def gather_kernel(size, *refs):
    pieces, out, col = refs[:-1], refs[-1], 0
    me = lax.axis_index("seq")
    for first in range(0, len(pieces), size):
        rows, width = pieces[first].shape
        for i, d in enumerate(gather_order(size)):
            at = pl.multiple_of(lax.rem(me + size - d, size) * rows, rows)
            out[pl.ds(at, rows), col : col + width] = pieces[first + i][...]
        col += width


def gather(*sums):
    size, rows = len(sums[0]), sums[0][0].shape[0]
    width = sum(pieces[0].shape[1] for pieces in sums)
    return small_call(
        functools.partial(gather_kernel, size), "gather_grads",
        jax.ShapeDtypeStruct((rows * size, width), jnp.bfloat16),
        *[piece for pieces in sums for piece in pieces],
    )


def finish_kernel(other, block, *refs):
    grad_b, grad_a, held_b, held_a, sems = refs[-5:]
    half, wide = held_b.shape
    sub = lax.axis_index("sub")
    place = (1 - sub if other else sub) * half
    at = pl.ds(pl.multiple_of(place, half), half)
    held_b[...] = block[:, 0:wide].astype(jnp.float32)
    first = fetch([(held_b, grad_b.at[at, :])], sems.at[pl.ds(0, 1)])
    held_a[...] = block[:, wide:].astype(jnp.float32)
    for copy in first + fetch([(held_a, grad_a.at[at, :])], sems.at[pl.ds(1, 1)]):
        copy.wait()


def finish(block, wide, before=None):
    half, width = block.shape
    operands = (block,) if before is None else (block, *before)
    shapes = [(2 * half, wide), (2 * half, width - wide)]
    return pl.pallas_call(
        functools.partial(finish_kernel, before is not None),
        out_shape=[jax.ShapeDtypeStruct(shape, jnp.float32) for shape in shapes],
        in_specs=[VM] + [ANY] * (len(operands) - 1),
        out_specs=[ANY] * 2,
        scratch_shapes=[
            pltpu.VMEM((half, wide), jnp.float32),
            pltpu.VMEM((half, width - wide), jnp.float32),
            pltpu.SemaphoreType.DMA((2,)),
        ],
        input_output_aliases={} if before is None else {1: 0, 2: 1},
        compiler_params=params(),
        cost_estimate=pl.CostEstimate(
            flops=block.size, bytes_accessed=6 * block.size, transcendentals=0
        ),
        name="finish_grads",
    )(*operands)


def halves_of(rows, width):
    return [jax.ShapeDtypeStruct((rows // 2, width), jnp.bfloat16)] * 2


def scatter(*pairs, after=()):
    size = lax.axis_size("seq")
    rows, width = pairs[0][0].shape[0], sum(keep.shape[1] for keep, _ in pairs)
    shard = jax.ShapeDtypeStruct((rows // size, width), jnp.bfloat16)
    return small_call(
        functools.partial(scatter_kernel, size, len(pairs)), "scatter_grads", [shard] * size,
        *[block for pair in pairs for block in pair],
        after=after, scratch=[pltpu.VMEM((rows, width), jnp.bfloat16)],
    )


def longest_first(size):
    return sorted(range(1, size), key=lambda d: -min(d, size - d))


def gather_order(size):
    return [0] + longest_first(size)[::-1]


def exchange(shards):
    return [shards[0]] + [rotate_over(shards[d], "seq", d) for d in longest_first(len(shards))]


def add_up(pieces, after=(), through=()):
    shape = jax.ShapeDtypeStruct(pieces[0].shape, pieces[0].dtype)
    return small_call(sum_kernel, "sum_grads", shape, *pieces, after=after, through=through)


def spread(shard):
    order = gather_order(lax.axis_size("seq"))
    return [rotate_over(shard, "seq", d) if d else shard for d in order]


def swap_over(block, axis):
    return lax.ppermute(block, axis, [(0, 1), (1, 0)])


def rotate_over(block, axis, d):
    size = lax.axis_size(axis)
    return lax.ppermute(block, axis, [(i, (i + d) % size) for i in range(size)])


def terms_over(block, axis):
    if lax.axis_size(axis) == 2:
        return block, swap_over(block, axis)
    return lax.psum(block, axis), jnp.zeros_like(block)


def shift_over(block, axis):
    size = lax.axis_size(axis)
    return lax.ppermute(block, axis, [(i, i + 1) for i in range(size - 1)])


def body(
    normed_inputs, base_queries, base_keys, base_values, adapter_down, adapter_up,
    position_document, document_tenant, output_gradient,
):
    rows, width = normed_inputs.shape
    tenants, _, rank = adapter_down.shape
    tall, up_width = tenants * rank, adapter_up.shape[2]
    doc = position_document.reshape(1, rows)
    adapter = jnp.transpose(adapter_down, (0, 2, 1)).reshape(tall, width)
    up = adapter_up.reshape(tall, up_width)
    key_heads = base_keys.shape[1] // HEAD
    chunks = 2 if key_heads % 4 == 0 else 1
    size = lax.axis_size("seq")
    by_hand = chunks == 2 and tall % (2 * TAIL * size) == 0

    own = pack(base_keys, base_values, doc, chunks)
    info = down_project(normed_inputs, adapter, doc, document_tenant, tenants, rank)
    info = small_call(
        functools.partial(join_kernel, rank), "join_terms",
        jax.ShapeDtypeStruct(info.shape, info.dtype), info, *terms_over(info, "mp"),
    )
    group = base_queries.shape[1] // HEAD // key_heads
    per = key_heads // chunks
    counts = [1, per - 1, per] if chunks == 2 else [1] * per
    state, pairs, held, with_ids, head = None, [], [], None, 0
    for i, count in enumerate(counts):
        chunk = head // per
        if len(held) < chunks and i < 2:
            two = shift_over(own[i], "seq")
            passing, two = relay(own[i], two, info if i == 0 else state[1])
            held.append((own[i], two, swap_over(two, "sub"), shift_over(passing, ("seq", "sub"))))
        with_ids = held[0]
        out, keep, send, gdown = attention(
            head, head % per, count, group, base_queries, output_gradient, up, held[chunk],
            with_ids, info, state, tenants, rank,
        )
        state = (out, gdown)
        pairs.append((keep, send))
        head += count
    if by_hand:
        one, other = terms_over(gdown, "mp")
        swapped = [(keep, swap_over(send, "sub")) for keep, send in pairs]
        keep, send = small_call(
            functools.partial(split_kernel, tenants, rank), "split_grads", halves_of(tall, width),
            one, other, info, normed_inputs, after=[got for _, got in swapped],
        )
        shards = scatter(*swapped, (keep, swap_over(send, "sub")))
        half = gather(spread(add_up(exchange(shards))))
        other = swap_over(half, "sub")
        grad_b, grad_a = finish(other, up_width, finish(half, up_width))
    else:
        one, other = terms_over(gdown, "mp")
        part_a = small_call(
            functools.partial(grad_a_kernel, tenants, rank), "grad_a_part",
            jax.ShapeDtypeStruct((tall, width), jnp.bfloat16), one, other, info, normed_inputs,
        )
        grad_a = lax.psum(part_a, ("seq", "sub")).astype(jnp.float32)
        keeps = jnp.concatenate([keep for keep, _ in pairs], axis=1)
        sends = jnp.concatenate([send for _, send in pairs], axis=1)
        low = lax.axis_index("sub") == 0
        part_b = jnp.concatenate([jnp.where(low, keeps, sends), jnp.where(low, sends, keeps)])
        grad_b = lax.psum(part_b, ("seq", "sub")).astype(jnp.float32)
    grad_a = jnp.transpose(grad_a.reshape(tenants, rank, width), (0, 2, 1))
    return out, grad_a, grad_b.reshape(tenants, rank, up_width)


def solution(mesh):
    split = P(("rep", "seq", "sub"), "mp")
    in_specs = (
        split, split, split, split, P(None, "mp", None), P(None, None, "mp"),
        P(("rep", "seq", "sub")), P("rep"), split,
    )
    out_specs = (split, P("rep", "mp", None), P("rep", None, "mp"))
    return jax.shard_map(body, mesh=mesh, in_specs=in_specs, out_specs=out_specs, check_vma=False)
```

```python
import functools

import jax
import jax.numpy as jnp
from jax import lax
from jax.experimental import pallas as pl
from jax.experimental.pallas import tpu as pltpu
from jax.sharding import PartitionSpec as P

HEAD = 128
REACH = 3
NEG = -1e30
LIFT = 2.0
LOG2E = 1.4426950408889634
TAIL = 16
VMEM_BYTES = 48 * 1024 * 1024
VMEM_MOST = 60 * 1024 * 1024
VMEM_HEADS = 52 * 1024 * 1024

VM = pl.BlockSpec(memory_space=pltpu.VMEM)
SM = pl.BlockSpec(memory_space=pltpu.SMEM)
ANY = pl.BlockSpec(memory_space=pl.ANY)


def nt(a, b):
    return lax.dot_general(a, b, (((1,), (1,)), ((), ())), preferred_element_type=jnp.float32)


def nn(a, b):
    return jnp.dot(a, b, preferred_element_type=jnp.float32)


def params(limit=VMEM_BYTES):
    return pltpu.CompilerParams(vmem_limit_bytes=limit)


def fetch(pairs, sems):
    copies = [pltpu.make_async_copy(src, dst, sems.at[i]) for i, (src, dst) in enumerate(pairs)]
    for copy in copies:
        copy.start()
    return copies


def pack_kernel(keys, values, doc, *rest):
    outs, (ids, blocks, sems) = rest[:-3], rest[-3:]
    rows, width = keys.shape
    part = width // len(outs)
    pairs = [(doc, ids)]
    for c in range(len(outs)):
        cols = pl.ds(c * part, part)
        pairs.append((keys.at[:, cols], blocks.at[c, pl.ds(0, rows), pl.ds(0, part)]))
        pairs.append((values.at[:, cols], blocks.at[c, pl.ds(0, rows), pl.ds(part, part)]))
    loads = fetch(pairs, sems.at[pl.ds(0, len(pairs))])
    loads[0].wait()
    tail = jnp.broadcast_to((ids[...] + 1).astype(jnp.float32), (TAIL, rows)).astype(jnp.bfloat16)
    stores = []
    for c, out in enumerate(outs):
        blocks[c, rows:, :] = jnp.zeros((TAIL, 2 * part), jnp.bfloat16)
        blocks[c, rows:, 0:rows] = tail
        loads[1 + 2 * c].wait()
        loads[2 + 2 * c].wait()
        stores += fetch([(blocks.at[c], out)], sems.at[pl.ds(len(pairs) + c, 1)])
    for store in stores:
        store.wait()


def pack(keys, values, doc, chunks):
    rows, width = keys.shape
    shape = (rows + TAIL, 2 * width // chunks)
    return pl.pallas_call(
        pack_kernel,
        out_shape=[jax.ShapeDtypeStruct(shape, jnp.bfloat16)] * chunks,
        in_specs=[ANY] * 3,
        out_specs=[ANY] * chunks,
        scratch_shapes=[
            pltpu.VMEM((1, rows), jnp.int32),
            pltpu.VMEM((chunks, *shape), jnp.bfloat16),
            pltpu.SemaphoreType.DMA((1 + 3 * chunks,)),
        ],
        compiler_params=params(VMEM_MOST),
        cost_estimate=pl.CostEstimate(flops=0, bytes_accessed=8 * rows * width, transcendentals=0),
        name="pack_keys_values",
    )(keys, values, doc)


def relay_kernel(own, got, after, out, got_out, held, sems):
    sub = lax.axis_index("sub")

    def move(source):
        load = pltpu.make_async_copy(source, held, sems.at[0])
        load.start()
        load.wait()

    @pl.when(sub == 0)
    def _():
        move(own)

    @pl.when(sub != 0)
    def _():
        move(got)

    store = pltpu.make_async_copy(held, out, sems.at[1])
    store.start()
    store.wait()


def relay(own, got, after):
    shape = jax.ShapeDtypeStruct(own.shape, own.dtype)
    return pl.pallas_call(
        relay_kernel,
        out_shape=[shape, shape],
        in_specs=[ANY, ANY, ANY],
        out_specs=[ANY, ANY],
        input_output_aliases={1: 1},
        scratch_shapes=[pltpu.VMEM(own.shape, own.dtype), pltpu.SemaphoreType.DMA((2,))],
        compiler_params=params(),
        cost_estimate=pl.CostEstimate(flops=0, bytes_accessed=4 * own.size, transcendentals=0),
        name="relay_block",
    )(own, got, after)


def selector_of(owner, tenants, rank):
    rows = owner.shape[1]
    tenant = lax.broadcasted_iota(jnp.int32, (tenants * rank, rows), 0) // rank
    return tenant == owner


def fold(full, owner, tenants, rank):
    kept = jnp.where(selector_of(owner, tenants, rank), full, 0.0)
    total = kept[0:rank]
    for t in range(1, tenants):
        total = total + kept[t * rank : (t + 1) * rank]
    return total


def unfold(compact, owner, tenants, rank):
    spread = jnp.concatenate([compact] * tenants, axis=0)
    return jnp.where(selector_of(owner, tenants, rank), spread, 0.0)


def down_kernel(tenants, rank, x_hbm, adapter_hbm, doc_hbm, tenant_of, info, x, adapter, doc, sems):
    copies = fetch([(doc_hbm, doc), (x_hbm, x), (adapter_hbm, adapter)], sems)
    copies[0].wait()
    ids = doc[...]
    found = jnp.zeros(ids.shape, jnp.int32)
    for s in range(tenant_of.shape[0]):
        found = jnp.where(ids == s, tenant_of[s], found)
    info[rank:, :] = jnp.broadcast_to(found.astype(jnp.float32), (info.shape[0] - rank, ids.shape[1]))
    copies[1].wait()
    copies[2].wait()
    info[0:rank, :] = fold(nt(x[...], adapter[...]).T, found, tenants, rank)


def down_project(x, adapter, doc, tenant_of, tenants, rank):
    rows, width = x.shape
    return pl.pallas_call(
        functools.partial(down_kernel, tenants, rank),
        out_shape=jax.ShapeDtypeStruct((rank + 8, rows), jnp.float32),
        in_specs=[ANY, ANY, ANY, SM],
        out_specs=VM,
        scratch_shapes=[
            pltpu.VMEM(x.shape, x.dtype),
            pltpu.VMEM(adapter.shape, adapter.dtype),
            pltpu.VMEM(doc.shape, doc.dtype),
            pltpu.SemaphoreType.DMA((3,)),
        ],
        compiler_params=params(VMEM_MOST),
        cost_estimate=pl.CostEstimate(
            flops=2 * rows * width * tenants * rank,
            bytes_accessed=2 * width * (rows + tenants * rank),
            transcendentals=0,
        ),
        name="down_project",
    )(x, adapter, doc, tenant_of)


def owner_of(info, rank):
    return info[rank : rank + 1, :].astype(jnp.int32)


def turn(x):
    return x.astype(jnp.float32).T.astype(jnp.bfloat16)


def attention(
    head, at, count, group, base, grad, up, blocks, with_ids, info, before, tenants, rank
):
    rows, width = base.shape
    window = (REACH + 1) * rows
    tall = tenants * rank
    half = tall // 2
    span = group * HEAD
    pair = min(8, group)
    scale = HEAD**-0.5
    wide = lambda r: pl.BlockSpec((r, span), lambda i: (0, i + head))
    narrow = pl.BlockSpec((half, span), lambda i: (0, i))
    keys = pl.BlockSpec((rows, HEAD), lambda i: (0, i + at))
    skip = blocks[0].shape[1] // (2 * HEAD)
    values = pl.BlockSpec((rows, HEAD), lambda i: (0, i + at + skip))
    ids = pl.BlockSpec((TAIL, rows), lambda i: (rows // TAIL, 0))
    same = lambda a: pl.BlockSpec(a.shape, lambda i: (0, 0))
    operands, specs = [base, grad, up], [wide(rows), wide(rows), wide(tall)]
    for block in blocks:
        operands += [block, block]
        specs += [keys, values]
    operands += [*with_ids, info]
    specs += [ids] * 4 + [same(info)]
    if before is not None:
        operands += [before[1], before[0]]
        specs += [same(before[1]), ANY]
    held = dict(
        kw=pltpu.VMEM((window, HEAD), jnp.bfloat16),
        vw=pltpu.VMEM((window, HEAD), jnp.bfloat16),
        kt=pltpu.VMEM((HEAD, window), jnp.bfloat16),
        vt=pltpu.VMEM((HEAD + TAIL, window), jnp.bfloat16),
        bottle=pltpu.VMEM((rows, tall), jnp.bfloat16),
        bottle_t=pltpu.VMEM((tall, rows), jnp.bfloat16),
        bias=pltpu.VMEM((window, rows), jnp.float32),
        query=pltpu.VMEM((span, rows), jnp.bfloat16),
        gt=pltpu.VMEM((span, rows), jnp.bfloat16),
        gquery=pltpu.VMEM((span, rows), jnp.bfloat16),
        scores=pltpu.VMEM((pair, window, rows), jnp.float32),
        part=pltpu.VMEM((tall, span), jnp.bfloat16),
        total=pltpu.VMEM((tall, rows), jnp.float32),
        reach=pltpu.SMEM((1,), jnp.int32),
    )

    def kernel(*refs):
        base, grad, up = refs[0:3]
        kv, tails, info = refs[3:11], refs[11:15], refs[15]
        out, keep, send, projected = refs[len(operands) : len(operands) + 4]
        r = dict(zip(held, refs[len(operands) + 4 :]))
        kw, vw, kt, vt = (r[n] for n in ("kw", "vw", "kt", "vt"))
        bias, query, gt, gquery, scores = (
            r[n] for n in ("bias", "query", "gt", "gquery", "scores")
        )
        sub = lax.axis_index("sub")
        step = pl.program_id(0)

        @pl.when(step == 0)
        def _():
            owner = owner_of(info, rank)
            lifted = unfold(info[0:rank, :], owner, tenants, rank)
            r["bottle_t"][...] = lifted.astype(jnp.bfloat16)
            r["bottle"][...] = lifted.T.astype(jnp.bfloat16)
            r["total"][...] = jnp.zeros((tall, rows), jnp.float32)
            vt[HEAD:, :] = jnp.ones((TAIL, window), jnp.bfloat16)
            own, two, swap, passed = (ref[...].astype(jnp.float32) for ref in tails)
            near = jnp.where(sub == 0, swap, passed)
            far = jnp.where(sub == 0, passed, swap)
            mine = own[0:1, :]
            lowest = jnp.min(mine)
            reach = 0
            for slot, block in ((REACH, own), (2, near), (1, two), (0, far)):
                same = block.T[:, 0:1] == mine
                if slot == REACH:
                    same = same & (
                        lax.broadcasted_iota(jnp.int32, (rows, rows), 0)
                        <= lax.broadcasted_iota(jnp.int32, (rows, rows), 1)
                    )
                else:
                    reach = jnp.where(jnp.max(block[0:1, :]) == lowest, REACH - slot, reach)
                bias[slot * rows : (slot + 1) * rows, :] = jnp.where(same, 0.0, NEG)
            r["reach"][0] = reach

        def place(slot, k_ref, v_ref):
            at = slice(slot * rows, (slot + 1) * rows)
            k, v = k_ref[...], v_ref[...]
            kw[at, :] = k
            vw[at, :] = v
            kt[:, at] = turn(k)
            vt[0:HEAD, at] = turn(v)

        place(REACH, *kv[0:2])
        place(1, *kv[2:4])

        @pl.when(sub == 0)
        def _():
            place(2, *kv[4:6])
            place(0, *kv[6:8])

        @pl.when(sub != 0)
        def _():
            place(2, *kv[6:8])
            place(0, *kv[4:6])

        lift = LIFT * nn(r["bottle"][...], up[...])
        query[...] = (base[...].astype(jnp.float32) + lift).T.astype(jnp.bfloat16)
        gt[...] = turn(grad[...])

        def run(reached, numbers):
            chunks = [slice(c * rows, (c + 1) * rows) for c in range(REACH - reached, REACH + 1)]
            spans = [pl.ds(pl.multiple_of(h * HEAD, HEAD), HEAD) for h in numbers]
            peaks = []
            for i, span_i in enumerate(spans):
                q, peak = query[span_i, :], None
                for c in chunks:
                    s = nn(kw[c, :], q) + bias[c, :]
                    scores[i, c, :] = s
                    top = jnp.max(s, axis=0, keepdims=True)
                    peak = top if peak is None else jnp.maximum(peak, top)
                peaks.append(peak)
            inverses, rowdots = [], []
            for i, span_i in enumerate(spans):
                total = None
                for c in chunks:
                    w = jnp.exp2((scores[i, c, :] - peaks[i]) * (scale * LOG2E))
                    scores[i, c, :] = w
                    o = nn(vt[:, c], w.astype(jnp.bfloat16))
                    total = o if total is None else total + o
                inverse = 1.0 / total[HEAD : HEAD + 1, :]
                attn = total[0:HEAD, :] * inverse
                out[:, span_i] = attn.T.astype(jnp.bfloat16)
                attn = attn.astype(jnp.bfloat16)
                product = gt[span_i, :].astype(jnp.float32) * attn.astype(jnp.float32)
                rowdots.append(jnp.sum(product, axis=0, keepdims=True))
                inverses.append(inverse)
            for i, span_i in enumerate(spans):
                g, moved = gt[span_i, :], None
                for c in chunks:
                    dprob = nn(vw[c, :], g)
                    ds = (scores[i, c, :] * (dprob - rowdots[i])).astype(jnp.bfloat16)
                    dq = nn(kt[:, c], ds)
                    moved = dq if moved is None else moved + dq
                gquery[span_i, :] = (moved * (inverses[i] * (LIFT * scale))).astype(jnp.bfloat16)

        for reached in (1, REACH):

            @pl.when((r["reach"][0] > 1) == (reached > 1))
            def _():
                @pl.loop(0, group // pair)
                def _(i):
                    run(reached, [i * pair + k for k in range(pair)])

        r["part"][...] = nt(r["bottle_t"][...], gquery[...]).astype(jnp.bfloat16)
        keep[...] = r["part"][pl.ds(pl.multiple_of(sub * half, half), half), :]
        send[...] = r["part"][pl.ds(pl.multiple_of((1 - sub) * half, half), half), :]
        r["total"][...] += nn(up[...], gquery[...])

        @pl.when(step == count - 1)
        def _():
            folded = fold(r["total"][...], owner_of(info, rank), tenants, rank)
            projected[...] = folded if before is None else folded + refs[16][...]

    return pl.pallas_call(
        kernel,
        grid=(count,),
        out_shape=[
            jax.ShapeDtypeStruct((rows, width), jnp.bfloat16),
            *halves_of(tall, count * span),
            jax.ShapeDtypeStruct((rank, rows), jnp.float32),
        ],
        in_specs=specs,
        out_specs=[wide(rows), narrow, narrow, pl.BlockSpec((rank, rows), lambda i: (0, 0))],
        scratch_shapes=list(held.values()),
        input_output_aliases={17: 0} if before is not None else {},
        compiler_params=params(VMEM_HEADS),
        cost_estimate=pl.CostEstimate(
            flops=8 * rows * window * span * count,
            bytes_accessed=6 * rows * span * count,
            transcendentals=rows * window * group * count,
        ),
        name="attention",
    )(*operands)


def small_call(kernel, name, shapes, *operands, after=(), through=(), scratch=()):
    size = sum(2 * a.size for a in operands)
    count, results = len(operands), jax.tree.leaves(shapes)
    given = (*operands, *after, *through)
    outs = len(given) + len(results)
    calls = pl.pallas_call(
        lambda *refs: kernel(
            *refs[:count], *refs[len(given) : outs], *refs[outs + len(through) :]
        ),
        out_shape=results + [jax.ShapeDtypeStruct(a.shape, a.dtype) for a in through],
        in_specs=[VM] * count + [ANY] * (len(after) + len(through)),
        out_specs=[VM] * len(results) + [ANY] * len(through),
        scratch_shapes=list(scratch),
        input_output_aliases={
            count + len(after) + i: len(results) + i for i in range(len(through))
        },
        compiler_params=params(),
        cost_estimate=pl.CostEstimate(flops=size, bytes_accessed=2 * size, transcendentals=0),
        name=name,
    )(*given)
    return calls if isinstance(shapes, list) or through else calls[0]


def join_kernel(rank, info, one, other, out):
    out[0:rank, :] = one[0:rank, :] + other[0:rank, :]
    out[rank:, :] = info[rank:, :]


def grad_a_of(tenants, rank, one, other, info, x):
    g = unfold((one[...] + other[...]), owner_of(info[...], rank), tenants, rank)
    return nn(g.astype(jnp.bfloat16), x[...]).astype(jnp.bfloat16)


def grad_a_kernel(tenants, rank, one, other, info, x, out):
    out[...] = grad_a_of(tenants, rank, one, other, info, x)


def split_kernel(tenants, rank, one, other, info, x, keep, send):
    part = grad_a_of(tenants, rank, one, other, info, x)
    half = keep.shape[0]
    sub = lax.axis_index("sub")

    @pl.when(sub == 0)
    def _():
        keep[...] = part[0:half, :]
        send[...] = part[half:, :]

    @pl.when(sub != 0)
    def _():
        keep[...] = part[half:, :]
        send[...] = part[0:half, :]


def scatter_kernel(size, count, *refs):
    mine, *sends, total = refs[2 * count :]
    col = 0
    for keep, got in zip(refs[0 : 2 * count : 2], refs[1 : 2 * count : 2]):
        both = keep[...].astype(jnp.float32) + got[...].astype(jnp.float32)
        total[:, col : col + keep.shape[1]] = both.astype(jnp.bfloat16)
        col += keep.shape[1]
    me = lax.axis_index("seq")
    rows = mine.shape[0]
    for d, out in enumerate((mine, *sends)):
        at = pl.multiple_of(lax.rem(me + d, size) * rows, rows)
        out[...] = total[pl.ds(at, rows), :]


def sum_kernel(*refs):
    total = refs[0][...].astype(jnp.float32)
    for ref in refs[1:-1]:
        total = total + ref[...].astype(jnp.float32)
    refs[-1][...] = total.astype(jnp.bfloat16)


def gather_kernel(size, *refs):
    pieces, out, col = refs[:-1], refs[-1], 0
    me = lax.axis_index("seq")
    for first in range(0, len(pieces), size):
        rows, width = pieces[first].shape
        for i, d in enumerate(gather_order(size)):
            at = pl.multiple_of(lax.rem(me + size - d, size) * rows, rows)
            out[pl.ds(at, rows), col : col + width] = pieces[first + i][...]
        col += width


def gather(*sums):
    size, rows = len(sums[0]), sums[0][0].shape[0]
    width = sum(pieces[0].shape[1] for pieces in sums)
    return small_call(
        functools.partial(gather_kernel, size), "gather_grads",
        jax.ShapeDtypeStruct((rows * size, width), jnp.bfloat16),
        *[piece for pieces in sums for piece in pieces],
    )


def finish_kernel(other, block, *refs):
    grad_b, grad_a, held_b, held_a, sems = refs[-5:]
    half, wide = held_b.shape
    sub = lax.axis_index("sub")
    place = (1 - sub if other else sub) * half
    at = pl.ds(pl.multiple_of(place, half), half)
    held_b[...] = block[:, 0:wide].astype(jnp.float32)
    first = fetch([(held_b, grad_b.at[at, :])], sems.at[pl.ds(0, 1)])
    held_a[...] = block[:, wide:].astype(jnp.float32)
    for copy in first + fetch([(held_a, grad_a.at[at, :])], sems.at[pl.ds(1, 1)]):
        copy.wait()


def finish(block, wide, before=None):
    half, width = block.shape
    operands = (block,) if before is None else (block, *before)
    shapes = [(2 * half, wide), (2 * half, width - wide)]
    return pl.pallas_call(
        functools.partial(finish_kernel, before is not None),
        out_shape=[jax.ShapeDtypeStruct(shape, jnp.float32) for shape in shapes],
        in_specs=[VM] + [ANY] * (len(operands) - 1),
        out_specs=[ANY] * 2,
        scratch_shapes=[
            pltpu.VMEM((half, wide), jnp.float32),
            pltpu.VMEM((half, width - wide), jnp.float32),
            pltpu.SemaphoreType.DMA((2,)),
        ],
        input_output_aliases={} if before is None else {1: 0, 2: 1},
        compiler_params=params(),
        cost_estimate=pl.CostEstimate(
            flops=block.size, bytes_accessed=6 * block.size, transcendentals=0
        ),
        name="finish_grads",
    )(*operands)


def halves_of(rows, width):
    return [jax.ShapeDtypeStruct((rows // 2, width), jnp.bfloat16)] * 2


def scatter(*pairs, after=()):
    size = lax.axis_size("seq")
    rows, width = pairs[0][0].shape[0], sum(keep.shape[1] for keep, _ in pairs)
    shard = jax.ShapeDtypeStruct((rows // size, width), jnp.bfloat16)
    return small_call(
        functools.partial(scatter_kernel, size, len(pairs)), "scatter_grads", [shard] * size,
        *[block for pair in pairs for block in pair],
        after=after, scratch=[pltpu.VMEM((rows, width), jnp.bfloat16)],
    )


def longest_first(size):
    return sorted(range(1, size), key=lambda d: -min(d, size - d))


def gather_order(size):
    return [0] + longest_first(size)[::-1]


def exchange(shards):
    return [shards[0]] + [rotate_over(shards[d], "seq", d) for d in longest_first(len(shards))]


def add_up(pieces, after=(), through=()):
    shape = jax.ShapeDtypeStruct(pieces[0].shape, pieces[0].dtype)
    return small_call(sum_kernel, "sum_grads", shape, *pieces, after=after, through=through)


def spread(shard):
    order = gather_order(lax.axis_size("seq"))
    return [rotate_over(shard, "seq", d) if d else shard for d in order]


def swap_over(block, axis):
    return lax.ppermute(block, axis, [(0, 1), (1, 0)])


def rotate_over(block, axis, d):
    size = lax.axis_size(axis)
    return lax.ppermute(block, axis, [(i, (i + d) % size) for i in range(size)])


def terms_over(block, axis):
    if lax.axis_size(axis) == 2:
        return block, swap_over(block, axis)
    return lax.psum(block, axis), jnp.zeros_like(block)


def shift_over(block, axis):
    size = lax.axis_size(axis)
    return lax.ppermute(block, axis, [(i, i + 1) for i in range(size - 1)])


def body(
    normed_inputs, base_queries, base_keys, base_values, adapter_down, adapter_up,
    position_document, document_tenant, output_gradient,
):
    rows, width = normed_inputs.shape
    tenants, _, rank = adapter_down.shape
    tall, up_width = tenants * rank, adapter_up.shape[2]
    doc = position_document.reshape(1, rows)
    adapter = jnp.transpose(adapter_down, (0, 2, 1)).reshape(tall, width)
    up = adapter_up.reshape(tall, up_width)
    key_heads = base_keys.shape[1] // HEAD
    chunks = 2 if key_heads % 4 == 0 else 1
    size = lax.axis_size("seq")
    by_hand = chunks == 2 and tall % (2 * TAIL * size) == 0

    own = pack(base_keys, base_values, doc, chunks)
    info = down_project(normed_inputs, adapter, doc, document_tenant, tenants, rank)
    info = small_call(
        functools.partial(join_kernel, rank), "join_terms",
        jax.ShapeDtypeStruct(info.shape, info.dtype), info, *terms_over(info, "mp"),
    )
    group = base_queries.shape[1] // HEAD // key_heads
    per = key_heads // chunks
    counts = [1, per - 1, per] if chunks == 2 else [1] * per
    state, pairs, held, with_ids, head = None, [], [], None, 0
    for i, count in enumerate(counts):
        chunk = head // per
        if len(held) < chunks and i < 2:
            two = shift_over(own[i], "seq")
            passing, two = relay(own[i], two, info if i == 0 else state[1])
            held.append((own[i], two, swap_over(two, "sub"), shift_over(passing, ("seq", "sub"))))
        with_ids = held[0]
        out, keep, send, gdown = attention(
            head, head % per, count, group, base_queries, output_gradient, up, held[chunk],
            with_ids, info, state, tenants, rank,
        )
        state = (out, gdown)
        pairs.append((keep, send))
        head += count
    if by_hand:
        one, other = terms_over(gdown, "mp")
        swapped = [(keep, swap_over(send, "sub")) for keep, send in pairs]
        keep, send = small_call(
            functools.partial(split_kernel, tenants, rank), "split_grads", halves_of(tall, width),
            one, other, info, normed_inputs, after=[swapped[-1][1]],
        )
        shards = scatter(*swapped, (keep, swap_over(send, "sub")))
        half = gather(spread(add_up(exchange(shards))))
        other = swap_over(half, "sub")
        grad_b, grad_a = finish(other, up_width, finish(half, up_width))
    else:
        one, other = terms_over(gdown, "mp")
        part_a = small_call(
            functools.partial(grad_a_kernel, tenants, rank), "grad_a_part",
            jax.ShapeDtypeStruct((tall, width), jnp.bfloat16), one, other, info, normed_inputs,
        )
        grad_a = lax.psum(part_a, ("seq", "sub")).astype(jnp.float32)
        keeps = jnp.concatenate([keep for keep, _ in pairs], axis=1)
        sends = jnp.concatenate([send for _, send in pairs], axis=1)
        low = lax.axis_index("sub") == 0
        part_b = jnp.concatenate([jnp.where(low, keeps, sends), jnp.where(low, sends, keeps)])
        grad_b = lax.psum(part_b, ("seq", "sub")).astype(jnp.float32)
    grad_a = jnp.transpose(grad_a.reshape(tenants, rank, width), (0, 2, 1))
    return out, grad_a, grad_b.reshape(tenants, rank, up_width)


def solution(mesh):
    split = P(("rep", "seq", "sub"), "mp")
    in_specs = (
        split, split, split, split, P(None, "mp", None), P(None, None, "mp"),
        P(("rep", "seq", "sub")), P("rep"), split,
    )
    out_specs = (split, P("rep", "mp", None), P("rep", None, "mp"))
    return jax.shard_map(body, mesh=mesh, in_specs=in_specs, out_specs=out_specs, check_vma=False)
```
